32 devices in a mesh: dp: 8 (over z, y), mem: 4 (over x, core).
Axes of the slice: x: 2, y: 2, z: 4, core: 2. Of those that a mesh axis runs over, the one named last changes fastest.
Arguments:
- tokens: bfloat16 [16384, 1024], P(('dp', 'mem')), may hold values from -6 to 6
- norm_gains: bfloat16 [2, 1024], P(None, ('dp', 'mem')), may hold values from 0.099609375 to 1.8984375
- norm_shifts: bfloat16 [2, 1024], P(None, ('dp', 'mem')), may hold values from -1.796875 to 1.796875
- w_qkv: bfloat16 [1024, 3072], P(('dp', 'mem')), may hold values from -0.1875 to 0.1875
- w_out: bfloat16 [1024, 1024], P(('dp', 'mem')), may hold values from -1.5 to 1.5
- w_up: bfloat16 [1024, 4096], P(('dp', 'mem')), may hold values from -0.1875 to 0.1875
- w_down: bfloat16 [4096, 1024], P(('dp', 'mem')), may hold values from -0.09375 to 0.09375
- rel_table: float32 [32, 8], replicated, may hold values from -3 to 3
- gate_bias: float32 [8], replicated, may hold values from -2 to 2
- xl_cache: bfloat16 [16384, 2048], P(('dp', 'mem')), may hold values from -6 to 6
- memory: bfloat16 [65536, 8, 256], P(('dp', 'mem')), may hold values from -6 to 6
- slot_index: int32 [16384, 8, 32], P('dp', None, 'mem'), may hold values from 0 to 8191, as said below
- seg_len: int32 [32], P(('dp', 'mem')), may hold values from 64 to 512, as said below
- cotangent: bfloat16 [16384, 1024], P(('dp', 'mem')), may hold values from -6 to 6
Outputs:
- layer_out: bfloat16 [16384, 1024], P(('dp', 'mem'))
- grad_tokens: float32 [16384, 1024], P(('dp', 'mem'))
- grad_gains: float32 [2, 1024], P(None, ('dp', 'mem'))
- grad_shifts: float32 [2, 1024], P(None, ('dp', 'mem'))
- grad_qkv: float32 [1024, 3072], P(('dp', 'mem'))
- grad_wout: float32 [1024, 1024], P(('dp', 'mem'))
- grad_up: float32 [1024, 4096], P(('dp', 'mem'))
- grad_down: float32 [4096, 1024], P(('dp', 'mem'))
- grad_table: float32 [32, 8], replicated
- grad_gate: float32 [8], replicated
The draws below stay inside these ranges and needn't reach their ends.
Inputs may be any that keep to these rules, and one draw needn't show every extreme that they name: `slot_index`: columns m * 8 to (m + 1) * 8 - 1 of a token's row hold slots m * 2048 to (m + 1) * 2048 - 1 of its group, for each m below 4. `seg_len`: some segment has all 512 tokens.
All inputs are finite; a program needn't handle non-finite values.
Results may differ from the reference program's by a relative error of at most 0.01.
Values may be sent and summed in bfloat16 or wider, within the bound.
A program may use at most 448 MiB of HBM per device.

```python
import jax
import jax.numpy as jnp
import numpy as np
from jax import lax

D = 1024
H = 8
HD = 128
FF = 4096
W = 512
BUCKETS = 32
TOPK = 32
SEG_DEV = 1
SLOTS_DEV = 2048
K_LOC = 8
SEGMENTS = 32
TOKENS = 16384
SLOTS_GRP = 8192
SLOTS = 65536
N_MEM = 4


def draw_slot_index(key, part):
    key = jax.random.fold_in(key, 11)
    within = jax.random.randint(key, (TOKENS, H, TOPK), 0, SLOTS_DEV)
    column = lax.broadcasted_iota(jnp.int32, (TOKENS, H, TOPK), 2)
    return (within + column // K_LOC * SLOTS_DEV).astype(jnp.int32)


def draw_seg_len(key, part):
    key = jax.random.fold_in(key, 7)
    length_key, chosen_key = jax.random.split(key)
    lengths = jax.random.randint(length_key, (SEGMENTS,), W // 8, W + 1)
    chosen = jax.random.randint(chosen_key, (), 0, SEGMENTS)
    return jnp.where(jnp.arange(SEGMENTS) == chosen, W, lengths).astype(jnp.int32)


def block_levels(key, dims, shards, low, largest):
    def one(axis_at, shards_of):
        heights = jax.random.uniform(jax.random.fold_in(jax.random.fold_in(key, 6), axis_at), (shards_of,), jnp.float32, low / len(shards), largest / len(shards))
        return jnp.repeat(jnp.exp(heights), dims[axis_at] // shards_of).reshape((-1,) + (1,) * (len(dims) - axis_at - 1))

    gain = one(*shards[0])
    for cut in shards[1:]:
        gain = gain * one(*cut)
    return gain


def gaussian(stream_key, dims, width, most, shards=(), held_as=jnp.bfloat16):
    values = width * jax.random.normal(stream_key, dims, jnp.float32)
    if shards:
        values = values * block_levels(stream_key, dims, shards, -0.22, 0.18)
    return jnp.clip(values, -most, most).astype(held_as)


def setup_inputs(seed: int = 0) -> dict:
    streams_of = jax.random.split(jax.random.key(seed), 15)
    return {
        "tokens": gaussian(streams_of[0], (TOKENS, D), 1.0, 6.0, ((0, 32),)),
        "norm_gains": jnp.clip(1.0 + 0.18 * jax.random.normal(streams_of[1], (2, D), jnp.float32), 0.099609375, 1.8984375).astype(jnp.bfloat16),
        "norm_shifts": gaussian(streams_of[2], (2, D), 0.3, 1.796875, ((1, 32),)),
        "w_qkv": gaussian(streams_of[3], (D, 3 * D), D ** -0.5, 0.1875, ((0, 32),)),
        "w_out": gaussian(streams_of[4], (D, D), (D // 64) ** -0.5, 1.5, ((0, 32),)),
        "w_up": gaussian(streams_of[5], (D, FF), D ** -0.5, 0.1875, ((0, 32),)),
        "w_down": gaussian(streams_of[6], (FF, D), FF ** -0.5, 0.09375, ((0, 32),)),
        "rel_table": gaussian(streams_of[7], (BUCKETS, H), 0.5, 3.0, (), jnp.float32),
        "gate_bias": jnp.clip(jax.random.uniform(streams_of[8], (H,), jnp.float32, -2.0, 2.0), -2.0, 2.0),
        "xl_cache": gaussian(streams_of[9], (TOKENS, 2 * D), 1.0, 6.0, ((0, 32),)),
        "memory": gaussian(streams_of[10], (SLOTS, H, 2 * HD), 1.0, 6.0, ((0, 32),)),
        "slot_index": draw_slot_index(jax.random.fold_in(streams_of[14], 71), 0),
        "seg_len": draw_seg_len(jax.random.fold_in(streams_of[14], 71), 0),
        "cotangent": gaussian(streams_of[13], (TOKENS, D), 1.0, 6.0, ((0, 32),)),
    }


EPSILON = 1e-05
HIGHEST = lax.Precision.HIGHEST

@jax.custom_vjp
def low(v):
    return lax.optimization_barrier(v.astype(jnp.bfloat16)).astype(jnp.float32)

@jax.custom_vjp
def low_back(v):
    return v

def low_keep(v):
    return (low(v), None)

def low_pass(kept, grad):
    return (grad,)

def back_keep(v):
    return (v, None)

def back_low(kept, grad):
    return (low(grad),)
low.defvjp(low_keep, low_pass)
low_back.defvjp(back_keep, back_low)

def bucket_onehot(window, buckets):
    distance = np.arange(2 * window)
    exact_count = buckets // 2
    log_bucket = exact_count + np.floor(np.log(np.maximum(distance, 1) / exact_count) / np.log(128.0 / exact_count) * exact_count)
    bucket = np.where(distance < exact_count, distance, np.minimum(log_bucket, buckets - 1))
    return bucket[:, None] == np.arange(buckets)[None, :]

def layer_norm(values, gain_row, shift_row):
    center = values - lax.optimization_barrier(jnp.mean(values, axis=-1, keepdims=True))
    spread = lax.optimization_barrier(jnp.mean(center * center, axis=-1, keepdims=True))
    return center * lax.rsqrt(spread + EPSILON) * gain_row + shift_row

def relative_bias(rel_table):
    onehot = jnp.asarray(bucket_onehot(W, BUCKETS), jnp.float32)
    bias_rows = jnp.dot(onehot, rel_table, precision=HIGHEST)
    row_ids = lax.broadcasted_iota(jnp.int32, (W, 2 * W), 0)
    col_ids = lax.broadcasted_iota(jnp.int32, (W, 2 * W), 1)
    relative = row_ids - col_ids + W
    return (jnp.take(bias_rows.T, jnp.maximum(relative, 0), axis=1), relative >= 0)

def segment_block(queries, keys_now, values_now, cache_rows, length, picked, bias_full, causal, gate_open):
    key_all = jnp.concatenate([cache_rows[:, :D], keys_now], axis=0).reshape(2 * W, H, HD)
    value_all = jnp.concatenate([cache_rows[:, D:], values_now], axis=0).reshape(2 * W, H, HD)
    query_heads = queries.reshape(W, H, HD)
    raw_scores = jnp.einsum('ihd,chd->hic', query_heads, key_all, precision=HIGHEST)
    col_ids = lax.broadcasted_iota(jnp.int32, (W, 2 * W), 1)
    allowed = causal & ((col_ids < W) | (col_ids - W < length))
    scores = jnp.where(allowed[None], low_back(raw_scores * HD ** (-0.5)) + bias_full, -1e+30)
    lse_local = jax.nn.logsumexp(scores, axis=-1, keepdims=True)
    weights = low(jnp.exp(scores - lse_local))
    local_out = low_back(jnp.einsum('hic,chd->ihd', weights, value_all, precision=HIGHEST))
    mem_keys = picked[..., :HD]
    mem_values = picked[..., HD:]
    mem_scores = jnp.einsum('ihd,ihjd->ihj', query_heads, mem_keys, precision=HIGHEST) * HD ** (-0.5)
    grouped = mem_scores.reshape(W, H, N_MEM, K_LOC)
    part_lse = jax.nn.logsumexp(grouped, axis=-1, keepdims=True)
    part_probs = low(jnp.exp(grouped - part_lse))
    part_out = jnp.einsum('ihmj,ihmjd->ihmd', part_probs, mem_values.reshape(W, H, N_MEM, K_LOC, HD), precision=HIGHEST)
    total_lse = jax.nn.logsumexp(part_lse, axis=2, keepdims=True)
    recalled = lax.optimization_barrier(jnp.sum(jnp.exp(part_lse - total_lse) * part_out, axis=2))
    mixed_out = gate_open[:, None] * recalled + (1.0 - gate_open[:, None]) * local_out
    return mixed_out.reshape(W, D)

def forward(tokens, norm_gains, norm_shifts, w_qkv, w_out, w_up, w_down, rel_table, gate_bias, xl_cache, memory, slot_index, seg_len):
    normed = low(layer_norm(tokens, norm_gains[0], norm_shifts[0]))
    projected = low(low_back(jnp.dot(normed, w_qkv, precision=HIGHEST)))
    bias_full, causal = relative_bias(rel_table)
    gate_open = jax.nn.sigmoid(gate_bias)
    flat_memory = memory.reshape(-1, 2 * HD)
    head_ids = lax.broadcasted_iota(jnp.int32, (W, H, TOPK), 1)

    def one_segment(inputs):
        segment_rows, cache_rows, slot_ids, length, group_id = inputs
        slot_rows = (group_id * SLOTS_GRP + slot_ids) * H + head_ids
        picked = jnp.take(flat_memory, slot_rows, axis=0).astype(jnp.float32)
        return segment_block(segment_rows[:, :D], segment_rows[:, D:2 * D], segment_rows[:, 2 * D:], cache_rows, length, picked, bias_full, causal, gate_open)
    group_ids = jnp.arange(SEGMENTS, dtype=jnp.int32) // (SEG_DEV * N_MEM)
    mixed_out = lax.map(jax.checkpoint(one_segment), (projected.reshape(SEGMENTS, W, 3 * D), xl_cache.reshape(SEGMENTS, W, 2 * D), slot_index.reshape(SEGMENTS, W, H, TOPK), seg_len, group_ids))
    mixed_out = low(mixed_out.reshape(TOKENS, D))
    attended = tokens + low_back(jnp.dot(mixed_out, w_out, precision=HIGHEST))
    normed_two = low(layer_norm(attended, norm_gains[1], norm_shifts[1]))
    hidden = low(jax.nn.gelu(low_back(jnp.dot(normed_two, w_up, precision=HIGHEST))))
    return attended + low_back(jnp.dot(hidden, w_down, precision=HIGHEST))

def reference(tokens, norm_gains, norm_shifts, w_qkv, w_out, w_up, w_down, rel_table, gate_bias, xl_cache, memory, slot_index, seg_len, cotangent):
    primals = (tokens.astype(jnp.float32), norm_gains.astype(jnp.float32), norm_shifts.astype(jnp.float32), w_qkv.astype(jnp.float32), w_out.astype(jnp.float32), w_up.astype(jnp.float32), w_down.astype(jnp.float32), rel_table.astype(jnp.float32), gate_bias.astype(jnp.float32))
    cache_float = xl_cache.astype(jnp.float32)

    def apply_layer(*params):
        return forward(*params, cache_float, memory, slot_index, seg_len)
    result, pullback = jax.vjp(apply_layer, *primals)
    gradients = pullback(cotangent.astype(jnp.float32))
    return (result.astype(jnp.bfloat16), gradients[0], gradients[1], gradients[2], gradients[3], gradients[4], gradients[5], gradients[6], gradients[7], gradients[8])
```

```python
import functools

import jax
import jax.numpy as jnp
import numpy as np
from jax import lax
from jax.experimental import pallas as pl
from jax.experimental.pallas import tpu as pltpu
from jax.sharding import PartitionSpec as P

H = 8
HD = 128
W = 512
BUCKETS = 32
NEAR = 128
EPSILON = 1e-05
NEGATIVE = -1e30
SCALE = HD ** (-0.5)
AXES = ("dp", "mem")
MESH = pl.DeviceIdType.MESH
HIGHEST = lax.Precision.HIGHEST
BF = jnp.bfloat16
F32 = jnp.float32
NT = (((1,), (1,)), ((), ()))
NN = (((1,), (0,)), ((), ()))


def dot(left, right, dims=NN):
    return lax.dot_general(left, right, dims, preferred_element_type=F32)


def gather_kernel(n_hi, orders, *refs):
    n = len(orders)
    ins, outs = refs[:n], refs[n : 2 * n]
    send_sem, recv_sem, local_sem = refs[2 * n :]
    dp, mem = lax.axis_index("dp"), lax.axis_index("mem")
    hi, lo = dp // 2, dp % 2
    x_at, core_at = mem // 2, mem % 2
    sizes = (n_hi, 2, 2, 2)
    own, along_y, along_x, along_core = (0, 0, 0, 0), (0, 1, 0, 0), (0, 0, 1, 0), (0, 0, 0, 1)

    def device(step):
        z = lax.rem(hi + step[0], n_hi)
        return (z * 2 + (lo + step[1]) % 2, (x_at + step[2]) % 2 * 2 + (core_at + step[3]) % 2)

    def plus(left, right):
        return tuple((a + b) % k for a, b, k in zip(left, right, sizes))

    def minus(left, right):
        return tuple((a - b) % k for a, b, k in zip(left, right, sizes))

    def number(step):
        return ((step[0] * 2 + step[1]) * 2 + step[2]) * 2 + step[3]

    partners = [(z, 0, 0, 0) for z in range(1, n_hi)] + [along_y, along_x, along_core]
    barrier = pltpu.get_barrier_semaphore()
    for partner in partners:
        pl.semaphore_signal(barrier, inc=1, device_id=device(partner), device_id_type=MESH)
    pl.semaphore_wait(barrier, len(partners))

    def place(a, source):
        d, m = device(source)
        rows = ins[a].shape[0]
        return outs[a].at[pl.ds(pl.multiple_of((d * 4 + m) * rows, rows), rows)]

    started = []
    counts = [0] * n

    def send(a, source, to):
        copy = pltpu.make_async_remote_copy(
            src_ref=ins[a] if source == own else place(a, source),
            dst_ref=place(a, source),
            send_sem=send_sem.at[a, counts[a]],
            recv_sem=recv_sem.at[a, number(minus(source, to))],
            device_id=device(to),
            device_id_type=MESH,
        )
        counts[a] += 1
        copy.start()
        started.append(copy)

    def arrived(a, source):
        ref = place(a, source)
        pltpu.make_async_remote_copy(
            src_ref=ref,
            dst_ref=ref,
            send_sem=send_sem.at[a, 0],
            recv_sem=recv_sem.at[a, number(source)],
            device_id=device(along_core),
            device_id_type=MESH,
        ).wait_recv()

    first = [along_y if order == "zyx" else along_x for order in orders]
    second = [along_x if order == "zyx" else along_y for order in orders]
    for a in range(n):
        for z in range(1, n_hi):
            send(a, own, (z, 0, 0, 0))
        send(a, own, along_y)
        send(a, own, along_x)
    kept = []
    for a in range(n):
        send(a, own, along_core)
        copy = pltpu.make_async_copy(ins[a], place(a, own), local_sem.at[a])
        copy.start()
        kept.append(copy)
    near_first = [0]
    for z in range(1, n_hi // 2 + 1):
        near_first += [k for k in dict.fromkeys((z, n_hi - z)) if k < n_hi]
    for z in near_first:
        at = (z, 0, 0, 0)
        if z:
            for a in range(n):
                arrived(a, at)
                for to in (first[a], second[a], along_core):
                    send(a, at, to)
        for a in range(n):
            source = plus(at, first[a])
            arrived(a, source)
            for to in (second[a], along_core):
                send(a, source, to)
    for z in near_first:
        for a in range(n):
            for source in (second[a], plus(first[a], second[a])):
                source = plus((z, 0, 0, 0), source)
                arrived(a, source)
                send(a, source, along_core)
    for z in near_first:
        for y in range(2):
            for x in range(2):
                for a in range(n):
                    arrived(a, (z, y, x, 1))
    for copy in started:
        copy.wait_send()
    for copy in kept:
        copy.wait()


def gather_rows(arrays, orders, collective_id):
    n = len(arrays)
    n_hi = lax.axis_size("dp") // 2
    total = n_hi * 8
    sends = (n_hi - 1) + 3 + (n_hi - 1) * 3 + n_hi * 2 + n_hi * 2
    anywhere = pl.BlockSpec(memory_space=pl.ANY)
    return pl.pallas_call(
        functools.partial(gather_kernel, n_hi, orders),
        out_shape=[
            jax.ShapeDtypeStruct((a.shape[0] * total,) + a.shape[1:], a.dtype) for a in arrays
        ],
        in_specs=[anywhere] * n,
        out_specs=[anywhere] * n,
        scratch_shapes=[
            pltpu.SemaphoreType.DMA((n, sends)),
            pltpu.SemaphoreType.DMA((n, total)),
            pltpu.SemaphoreType.DMA((n,)),
        ],
        compiler_params=pltpu.CompilerParams(collective_id=collective_id, has_side_effects=True),
    )(*arrays)


def recall_kernel(qa_ref, qb_ref, mem_ref, slot_ref, outa_ref, outb_ref, lse_ref, p_ref):
    slots, tokens = p_ref.shape[1], p_ref.shape[2]
    half = tokens // 2
    chosen = slot_ref[0]
    low, high = chosen & 7, chosen >> 3
    queries = jnp.concatenate([qa_ref[...], qb_ref[...]], axis=0)
    step = 256
    picked = jnp.zeros((8, tokens), F32)
    for at in range(0, slots, step):
        scores = dot(mem_ref[0, pl.ds(at, step), pl.ds(0, HD)], queries, NT)
        for row in range(0, step, 8):
            got = jnp.take_along_axis(scores[row : row + 8], low, axis=0)
            picked = jnp.where(high == (at + row) // 8, got, picked)
    scores = picked * SCALE
    top = jnp.max(scores, axis=0, keepdims=True)
    weights = jnp.exp(scores - top)
    total = jnp.sum(weights, axis=0, keepdims=True)
    lse_ref[0] = top + jnp.log(total)
    times = jnp.ones_like(weights)
    for turn in range(1, 8):
        times = times + jnp.where(pltpu.roll(chosen, turn, 0) == chosen, 1.0, 0.0)
    probs = (weights / total * times).astype(BF)
    rows = lax.broadcasted_iota(jnp.int32, (step, tokens), 0).astype(F32).astype(BF)
    out = jnp.zeros((HD, tokens), F32)
    values_t = mem_ref[0, :, pl.ds(HD, HD)].T
    for at in range(0, slots, step):
        mine = jnp.where(chosen // step == at // step, chosen % step, -1).astype(F32).astype(BF)
        dense = jnp.zeros((step, tokens), BF)
        for j in range(8):
            dense = jnp.where(rows == mine[j : j + 1], probs[j : j + 1], dense)
        p_ref[0, pl.ds(at, step), :] = dense
        out = out + dot(values_t[:, at : at + step], dense)
    out = out.T.astype(BF)
    outa_ref[...] = out[:half]
    outb_ref[...] = out[half:]


def recall_grad_kernel(ga_ref, gb_ref, mem_ref, p_ref, delta_ref, share_ref, outa_ref, outb_ref):
    slots, tokens = p_ref.shape[1], p_ref.shape[2]
    half = tokens // 2
    grads = jnp.concatenate([ga_ref[...], gb_ref[...]], axis=0)
    delta = delta_ref[0]
    keys_t = mem_ref[0, :, pl.ds(0, HD)].T
    step = 512
    out = jnp.zeros((HD, tokens), F32)
    for at in range(0, slots, step):
        along = dot(mem_ref[0, pl.ds(at, step), pl.ds(HD, HD)], grads, NT)
        scores = (along - delta).astype(BF) * p_ref[0, pl.ds(at, step), :]
        out = out + dot(keys_t[:, at : at + step], scores)
    out = (out * (share_ref[0] * SCALE)).T.astype(BF)
    outa_ref[...] = out[:half]
    outb_ref[...] = out[half:]


def head_columns(rows, first=0):
    return pl.BlockSpec((rows, HD), lambda h: (0, first + h))


def per_head(*shape):
    return pl.BlockSpec((1,) + shape, lambda h: (h,) + (0,) * len(shape))


def recall(query_a, query_b, table, chosen):
    rows, slots = query_a.shape[0], table.shape[1]
    return pl.pallas_call(
        recall_kernel,
        grid=(H,),
        in_specs=[
            head_columns(rows),
            head_columns(rows),
            per_head(slots, 2 * HD),
            per_head(8, 2 * rows),
        ],
        out_specs=[
            head_columns(rows),
            head_columns(rows),
            per_head(1, 2 * rows),
            per_head(slots, 2 * rows),
        ],
        out_shape=[
            jax.ShapeDtypeStruct(query_a.shape, BF),
            jax.ShapeDtypeStruct(query_a.shape, BF),
            jax.ShapeDtypeStruct((H, 1, 2 * rows), F32),
            jax.ShapeDtypeStruct((H, slots, 2 * rows), BF),
        ],
        compiler_params=pltpu.CompilerParams(vmem_limit_bytes=48 << 20),
        cost_estimate=pl.CostEstimate(
            flops=8 * rows * slots * HD * H, bytes_accessed=64 << 20, transcendentals=0
        ),
    )(query_a, query_b, table, chosen)


def recall_grad(grad_a, grad_b, table, probs, delta, share):
    rows, slots = grad_a.shape[0], table.shape[1]
    return pl.pallas_call(
        recall_grad_kernel,
        grid=(H,),
        in_specs=[
            head_columns(rows),
            head_columns(rows),
            per_head(slots, 2 * HD),
            per_head(slots, 2 * rows),
            per_head(1, 2 * rows),
            per_head(1, 2 * rows),
        ],
        out_specs=[head_columns(rows), head_columns(rows)],
        out_shape=[jax.ShapeDtypeStruct(grad_a.shape, BF)] * 2,
        compiler_params=pltpu.CompilerParams(vmem_limit_bytes=48 << 20),
        cost_estimate=pl.CostEstimate(
            flops=8 * rows * slots * HD * H, bytes_accessed=64 << 20, transcendentals=0
        ),
    )(grad_a, grad_b, table, probs, delta, share)


def near_buckets():
    distance = np.arange(NEAR)
    exact = BUCKETS // 2
    far = exact + np.floor(
        np.log(np.maximum(distance, 1) / exact) / np.log(128.0 / exact) * exact
    )
    return np.where(distance < exact, distance, np.minimum(far, BUCKETS - 1)).astype(np.int32)


def near_hot():
    return near_buckets()[:, None] == np.arange(BUCKETS)[None, :]


def near_bias(rel_table):
    above = (rel_table - rel_table[-1:])[None]
    rows = jnp.sum(jnp.where(jnp.asarray(near_hot())[:, :, None], above, 0.0), axis=1)
    return jnp.pad(rows.T, ((0, 0), (0, NEAR)))[:, None, :]


def table_gradient(diagonals, totals):
    near = diagonals[:, 0, NEAR - 1 : 2 * NEAR - 1]
    sums = jnp.dot(near, jnp.asarray(near_hot(), F32), precision=HIGHEST)
    far = jnp.sum(totals, axis=(1, 2)) - jnp.sum(near, axis=1)
    return (sums + far[:, None] * (np.arange(BUCKETS) == BUCKETS - 1)).T


def segment_kernel(len_ref, near_ref, q_ref, kc_ref, kn_ref, vc_ref, vn_ref, out_ref, p_ref):
    length = len_ref[0]
    band = pltpu.roll(
        jnp.broadcast_to(near_ref[0], (NEAR, 2 * NEAR)), 0, 1, stride=1, stride_axis=0
    )
    key_ids = lax.broadcasted_iota(jnp.int32, (NEAR, NEAR), 0)
    query_ids = lax.broadcasted_iota(jnp.int32, (NEAR, NEAR), 1)
    on_diagonal = jnp.where(query_ids >= key_ids, band[:, :NEAR], NEGATIVE)
    beside = band[:, NEAR:]
    masked = jnp.full((NEAR, NEAR), NEGATIVE, F32)
    zero = jnp.zeros((NEAR, NEAR), F32)
    cache_t, values_t = vc_ref[...].T, vn_ref[...].T
    step = 2 * NEAR
    for at in range(W // step):
        count = 2 * (at + 1)
        queries = q_ref[pl.ds(step * at, step), :]
        cached = dot(kc_ref[...], queries, NT) * SCALE
        if at == 0:
            last = cached[W - NEAR :] + jnp.concatenate([beside, zero], axis=1)
            cached = jnp.concatenate([cached[: W - NEAR], last], axis=0)
        fresh = dot(kn_ref[pl.ds(0, NEAR * count), :], queries, NT) * SCALE
        rows = [cached]
        for k in range(count):
            block = fresh[NEAR * k : NEAR * (k + 1)]
            tiles = [
                masked if q < k else on_diagonal if q == k else beside if q == k + 1 else zero
                for q in (2 * at, 2 * at + 1)
            ]
            if any(tile is not zero for tile in tiles):
                block = block + jnp.concatenate(tiles, axis=1)
            ids = lax.broadcasted_iota(jnp.int32, (NEAR, step), 0) + NEAR * k
            rows.append(jnp.where(ids < length, block, NEGATIVE))
        scores = jnp.concatenate(rows, axis=0)
        weights = jnp.exp(scores - jnp.max(scores, axis=0, keepdims=True))
        probs = (weights * (1.0 / jnp.sum(weights, axis=0, keepdims=True))).astype(BF)
        p_ref[0, pl.ds(0, W + NEAR * count), pl.ds(step * at, step)] = probs
        out = dot(cache_t, probs[:W]) + dot(values_t[:, : NEAR * count], probs[W:])
        out_ref[pl.ds(step * at, step), :] = out.T


def segment_grad_kernel(
    open_ref, g_ref, q_ref, kc_ref, kn_ref, vc_ref, vn_ref, p_ref, gq_ref, gk_ref, gv_ref, diag_ref, tot_ref
):
    closed = 1.0 - open_ref[pl.program_id(0)]
    cache_t, keys_t = kc_ref[...].T, kn_ref[...].T
    on_diagonal = jnp.zeros((NEAR, NEAR), F32)
    beside = jnp.zeros((NEAR, NEAR), F32)
    step = 2 * NEAR
    total = jnp.zeros((8, step), F32)
    grad_keys, grad_values = [], []
    for at in range(W // step):
        count = 2 * (at + 1)
        grads = (closed * g_ref[pl.ds(step * at, step), :]).astype(BF)
        queries = q_ref[pl.ds(step * at, step), :]
        grad_probs = jnp.concatenate(
            [dot(vc_ref[...], grads, NT), dot(vn_ref[pl.ds(0, NEAR * count), :], grads, NT)], axis=0
        )
        probs = p_ref[0, pl.ds(0, W + NEAR * count), pl.ds(step * at, step)]
        wide = probs.astype(F32)
        product = wide * grad_probs
        grad_scores = product - wide * jnp.sum(product, axis=0, keepdims=True)
        low = grad_scores.astype(BF)
        grad_q = dot(cache_t, low[:W]) + dot(keys_t[:, : NEAR * count], low[W:])
        gq_ref[pl.ds(step * at, step), :] = (grad_q * SCALE).T
        grad_keys.append(dot(low[W:], queries) * SCALE)
        grad_values.append(dot(probs[W:], grads))
        if at == 0:
            beside = beside + grad_scores[W - NEAR : W, :NEAR]
        for k in range(count):
            for side, q in enumerate((2 * at, 2 * at + 1)):
                tile = grad_scores[W + NEAR * k : W + NEAR * (k + 1), NEAR * side : NEAR * (side + 1)]
                if q == k:
                    on_diagonal = on_diagonal + tile
                elif q == k + 1:
                    beside = beside + tile
        total = total + jnp.sum(grad_scores.reshape(-1, 8, step), axis=0)
    for ref, (early, late) in ((gk_ref, grad_keys), (gv_ref, grad_values)):
        ref[...] = jnp.concatenate([late[:step] + early, late[step:]], axis=0).astype(BF)
    down = lax.broadcasted_iota(jnp.int32, (NEAR, NEAR), 0)
    across = lax.broadcasted_iota(jnp.int32, (NEAR, NEAR), 1)
    turned = lax.dot_general(
        (down + across == NEAR - 1).astype(F32),
        jnp.concatenate([on_diagonal, beside], axis=1),
        NN,
        precision=HIGHEST,
        preferred_element_type=F32,
    )
    diagonals = pltpu.roll(turned, 0, 1, stride=1, stride_axis=0)
    diag_ref[0] = jnp.sum(diagonals, axis=0, keepdims=True)
    tot_ref[0] = total


SCALARS = pl.BlockSpec(memory_space=pltpu.SMEM)


def segment_forward(queries, keys_values, cache, near, length):
    return pl.pallas_call(
        segment_kernel,
        grid=(H,),
        in_specs=[
            SCALARS,
            per_head(1, 2 * NEAR),
            head_columns(W),
            head_columns(W),
            head_columns(W),
            head_columns(W, H),
            head_columns(W, H),
        ],
        out_specs=[head_columns(W), per_head(2 * W, W)],
        out_shape=[
            jax.ShapeDtypeStruct((W, H * HD), F32),
            jax.ShapeDtypeStruct((H, 2 * W, W), BF),
        ],
        compiler_params=pltpu.CompilerParams(vmem_limit_bytes=32 << 20),
        cost_estimate=pl.CostEstimate(
            flops=8 * W * W * HD * H, bytes_accessed=20 << 20, transcendentals=0
        ),
    )(length, near, queries, cache, keys_values, cache, keys_values)


def segment_backward(gate_open, grad_mixed, queries, keys_values, cache, probs):
    return pl.pallas_call(
        segment_grad_kernel,
        grid=(H,),
        in_specs=[
            SCALARS,
            head_columns(W),
            head_columns(W),
            head_columns(W),
            head_columns(W),
            head_columns(W, H),
            head_columns(W, H),
            per_head(2 * W, W),
        ],
        out_specs=[
            head_columns(W),
            head_columns(W),
            head_columns(W),
            per_head(1, 2 * NEAR),
            per_head(8, 2 * NEAR),
        ],
        out_shape=[
            jax.ShapeDtypeStruct((W, H * HD), F32),
            jax.ShapeDtypeStruct((W, H * HD), BF),
            jax.ShapeDtypeStruct((W, H * HD), BF),
            jax.ShapeDtypeStruct((H, 1, 2 * NEAR), F32),
            jax.ShapeDtypeStruct((H, 8, 2 * NEAR), F32),
        ],
        compiler_params=pltpu.CompilerParams(vmem_limit_bytes=32 << 20),
        cost_estimate=pl.CostEstimate(
            flops=16 * W * W * HD * H, bytes_accessed=20 << 20, transcendentals=0
        ),
    )(gate_open, grad_mixed, queries, cache, keys_values, cache, keys_values, probs)


def norm_forward(values, gain_row, shift_row):
    center = values - jnp.mean(values, axis=-1, keepdims=True)
    inverse = lax.rsqrt(jnp.mean(center * center, axis=-1, keepdims=True) + EPSILON)
    scaled = center * inverse
    return (scaled * gain_row + shift_row, scaled, inverse)


def norm_backward(grad_normed, scaled, inverse, gain_row):
    grad_scaled = grad_normed * gain_row
    mean_grad = jnp.mean(grad_scaled, axis=-1, keepdims=True)
    mean_cross = jnp.mean(grad_scaled * scaled, axis=-1, keepdims=True)
    return inverse * (grad_scaled - mean_grad - scaled * mean_cross)


def swap(value, turn):
    return jax.tree.map(
        lambda v: lax.ppermute(v, "mem", [(i, i ^ turn) for i in range(lax.axis_size("mem"))]), value
    )


def combine(outs, lses):
    total = jax.nn.logsumexp(jnp.stack(lses), axis=0)
    rows = outs[0].shape[0]
    result = 0.0
    for out, lse in zip(outs, lses):
        share = jnp.exp(lse - total).T[:, :, None]
        result = result + share * out.reshape(rows, H, HD).astype(F32)
    return result.reshape(rows, H * HD), total


def local(
    tokens,
    norm_gains,
    norm_shifts,
    w_qkv,
    w_out,
    w_up,
    w_down,
    rel_table,
    gate_bias,
    xl_cache,
    memory,
    slot_index,
    seg_len,
    cotangent,
):
    width = tokens.shape[1]
    count = tokens.shape[0]
    slot_count = memory.shape[0]
    groups = lax.axis_size("mem")
    me = lax.axis_index("mem")

    norms = jnp.pad(
        jnp.concatenate([norm_gains, norm_shifts], axis=0),
        ((0, 12), (0, 128 - norm_gains.shape[1])),
    )
    full_q, full_norms = gather_rows([w_qkv[:, :width], norms], ("zyx", "zxy"), 0)
    full_kv, full_out, full_up, full_down = gather_rows(
        [w_qkv[:, width:], w_out, w_up, w_down], ("zxy", "zyx", "zyx", "zxy"), 1
    )
    rows = full_norms.reshape(-1, 16, 128)[:, :4, : norm_gains.shape[1]].astype(F32)
    rows = rows.transpose(1, 0, 2).reshape(4, width)
    gain_rows, shift_rows = rows[:2], rows[2:]

    inputs = tokens.astype(F32)
    normed_one, scaled_one, inverse_one = norm_forward(inputs, gain_rows[0], shift_rows[0])
    normed_one = normed_one.astype(BF)
    queries = dot(normed_one, full_q).astype(BF)
    query_core, query_x = swap(queries, 1), swap(queries, 2)
    query_cross = swap(query_x, 1)

    table = memory.transpose(1, 0, 2)
    slot_rows = (slot_index - me * slot_count).reshape(groups, count, H, -1).transpose(0, 2, 3, 1)
    picks = [
        lax.dynamic_index_in_dim(slot_rows, me ^ turn, 0, keepdims=False) for turn in range(groups)
    ]
    out_own, out_core, lse_chip, probs_chip = recall(
        queries, query_core, table, jnp.concatenate(picks[:2], axis=-1)
    )
    out_x, out_cross, lse_far, probs_far = recall(
        query_x, query_cross, table, jnp.concatenate(picks[2:], axis=-1)
    )
    lse_chip, lse_far = lse_chip[:, 0], lse_far[:, 0]
    keys_values = dot(normed_one, full_kv).astype(BF)
    local_out, probs_local = segment_forward(
        queries, keys_values, xl_cache, near_bias(rel_table), seg_len
    )

    own_lse, own_out = lse_chip[:, :count], out_own
    core_out, core_lse = swap((out_core, lse_chip[:, count:]), 1)
    other_out, other_lse = swap((out_cross, lse_far[:, count:]), 1)
    pair_out, pair_lse = combine((out_x, other_out), (lse_far[:, :count], other_lse))
    far_out, far_lse = swap((pair_out.astype(BF), pair_lse), 2)
    recalled, total_lse = combine((own_out, core_out, far_out), (own_lse, core_lse, far_lse))

    gate_open = jax.nn.sigmoid(gate_bias)
    gate_row = jnp.repeat(gate_open, HD)[None]
    mixed_low = (gate_row * recalled + (1.0 - gate_row) * local_out).astype(BF)
    attended = inputs + dot(mixed_low, full_out)
    normed_two, scaled_two, inverse_two = norm_forward(attended, gain_rows[1], shift_rows[1])
    normed_two = normed_two.astype(BF)
    up_pre = dot(normed_two, full_up)
    hidden = jax.nn.gelu(up_pre).astype(BF)
    output = attended + dot(hidden, full_down)

    grad_output = cotangent.astype(F32)
    grad_down = jnp.einsum("tf,td->fd", hidden, cotangent, preferred_element_type=F32)
    grad_hidden = dot(cotangent, full_down, NT)
    grad_up_pre = jax.vjp(jax.nn.gelu, up_pre)[1](grad_hidden)[0].astype(BF)
    grad_up = jnp.einsum("td,tf->df", normed_two, grad_up_pre, preferred_element_type=F32)
    grad_normed_two = dot(grad_up_pre, full_up, NT)
    grad_attended = grad_output + norm_backward(
        grad_normed_two, scaled_two, inverse_two, gain_rows[1]
    )
    attended_low = grad_attended.astype(BF)
    grad_wout = jnp.einsum("td,te->de", mixed_low, attended_low, preferred_element_type=F32)
    grad_mixed = dot(attended_low, full_out, NT)
    grad_gate = (
        jnp.sum((grad_mixed * (recalled - local_out)).reshape(count, H, HD), axis=(0, 2))
        * gate_open
        * (1.0 - gate_open)
    )
    grad_recalled = (gate_row * grad_mixed).astype(BF)
    delta = jnp.sum(
        (grad_recalled.astype(F32) * recalled).reshape(count, H, HD), axis=-1
    ).T
    sent = (grad_recalled, jnp.concatenate([delta, total_lse], axis=0))
    sent_core, sent_x = swap(sent, 1), swap(sent, 2)
    sent_cross = swap(sent_x, 1)

    grad_query_local, grad_keys, grad_values, diagonals, totals = segment_backward(
        gate_open, grad_mixed, queries, keys_values, xl_cache, probs_local
    )
    grad_table = table_gradient(diagonals, totals)

    def recall_back(left, right, lse, probs):
        delta_rows = jnp.concatenate([left[1][:H], right[1][:H]], axis=1)
        total_rows = jnp.concatenate([left[1][H:], right[1][H:]], axis=1)
        return recall_grad(
            left[0],
            right[0],
            table,
            probs,
            delta_rows[:, None],
            jnp.exp(lse - total_rows)[:, None],
        )

    back_x, back_cross = recall_back(sent_x, sent_cross, lse_far, probs_far)
    back_own, back_core = recall_back(sent, sent_core, lse_chip, probs_chip)
    pair_back = (back_x.astype(F32) + swap(back_cross, 1).astype(F32)).astype(BF)
    grad_query = (
        grad_query_local
        + back_own.astype(F32)
        + swap(back_core, 1).astype(F32)
        + swap(pair_back, 2).astype(F32)
    )
    grad_qkv_low = jnp.concatenate([grad_query.astype(BF), grad_keys, grad_values], axis=1)
    grad_wqkv = jnp.einsum("td,te->de", normed_one, grad_qkv_low, preferred_element_type=F32)
    grad_normed_one = dot(grad_qkv_low[:, :width], full_q, NT) + dot(
        grad_qkv_low[:, width:], full_kv, NT
    )
    grad_tokens = grad_attended + norm_backward(
        grad_normed_one, scaled_one, inverse_one, gain_rows[0]
    )
    grad_norms = jnp.stack(
        [
            jnp.sum(grad_normed_one * scaled_one, axis=0),
            jnp.sum(grad_normed_two * scaled_two, axis=0),
            jnp.sum(grad_normed_one, axis=0),
            jnp.sum(grad_normed_two, axis=0),
        ]
    )
    share_qkv, share_out, share_up, share_down = [
        lax.psum_scatter(g.astype(BF), AXES, scatter_dimension=0, tiled=True).astype(F32)
        for g in (grad_wqkv, grad_wout, grad_up, grad_down)
    ]
    share_norms = lax.psum_scatter(grad_norms, AXES, scatter_dimension=1, tiled=True)
    table_total, gate_total = lax.psum((grad_table, grad_gate), AXES)
    return (
        output.astype(BF),
        grad_tokens,
        share_norms[:2],
        share_norms[2:],
        share_qkv,
        share_out,
        share_up,
        share_down,
        table_total,
        gate_total,
    )


def solution(mesh):
    shard = P(AXES, None)
    placed = (
        shard,
        P(None, AXES),
        P(None, AXES),
        shard,
        shard,
        shard,
        shard,
        P(),
        P(),
        shard,
        P(AXES, None, None),
        P("dp", None, "mem"),
        P(AXES),
        shard,
    )
    return jax.shard_map(
        local,
        mesh=mesh,
        in_specs=placed,
        out_specs=(
            shard,
            shard,
            P(None, AXES),
            P(None, AXES),
            shard,
            shard,
            shard,
            shard,
            P(),
            P(),
        ),
        check_vma=False,
    )
```

```python
import functools

import jax
import jax.numpy as jnp
import numpy as np
from jax import lax
from jax.experimental import pallas as pl
from jax.experimental.pallas import tpu as pltpu
from jax.sharding import PartitionSpec as P

H = 8
HD = 128
W = 512
BUCKETS = 32
NEAR = 128
EPSILON = 1e-05
NEGATIVE = -1e30
SCALE = HD ** (-0.5)
AXES = ("dp", "mem")
MESH = pl.DeviceIdType.MESH
HIGHEST = lax.Precision.HIGHEST
BF = jnp.bfloat16
F32 = jnp.float32
NT = (((1,), (1,)), ((), ()))
NN = (((1,), (0,)), ((), ()))


def dot(left, right, dims=NN):
    return lax.dot_general(left, right, dims, preferred_element_type=F32)


OWN, ALONG_Y, ALONG_X, ALONG_CORE = (0, 0, 0, 0), (0, 1, 0, 0), (0, 0, 1, 0), (0, 0, 0, 1)
ANYWHERE = pl.BlockSpec(memory_space=pl.ANY)
IN_VMEM = pl.BlockSpec(memory_space=pltpu.VMEM)
SCALARS = pl.BlockSpec(memory_space=pltpu.SMEM)


class Place:
    def __init__(self, n_hi):
        self.sizes = (n_hi, 2, 2, 2)
        dp, mem = lax.axis_index("dp"), lax.axis_index("mem")
        self.at = (dp // 2, dp % 2, mem // 2, mem % 2)

    def device(self, step):
        z, y, x, core = [(a + s) % n for a, s, n in zip(self.at, step, self.sizes)]
        return (z * 2 + y, x * 2 + core)

    def number(self, step):
        dp, mem = self.device(step)
        return dp * 4 + mem

    def plus(self, left, right):
        return tuple((a + b) % n for a, b, n in zip(left, right, self.sizes))

    def minus(self, left, right):
        return tuple((a - b) % n for a, b, n in zip(left, right, self.sizes))

    def partners(self):
        return [(z, 0, 0, 0) for z in range(1, self.sizes[0])] + [ALONG_Y, ALONG_X, ALONG_CORE]

    def greet(self):
        barrier = pltpu.get_barrier_semaphore()
        for partner in self.partners():
            pl.semaphore_signal(
                barrier, inc=1, device_id=self.device(partner), device_id_type=MESH
            )
        pl.semaphore_wait(barrier, len(self.partners()))

    def copy(self, src, dst, send, recv, device):
        copy = pltpu.make_async_remote_copy(
            src_ref=src,
            dst_ref=dst,
            send_sem=send,
            recv_sem=recv,
            device_id=device,
            device_id_type=MESH,
        )
        copy.start()
        return copy

    def arrived(self, ref, recv):
        pltpu.make_async_remote_copy(
            src_ref=ref,
            dst_ref=ref,
            send_sem=recv,
            recv_sem=recv,
            device_id=self.device(ALONG_CORE),
            device_id_type=MESH,
        ).wait_recv()


def near_first(n_hi):
    order = [0]
    for z in range(1, n_hi // 2 + 1):
        order += [k for k in dict.fromkeys((z, n_hi - z)) if k < n_hi]
    return order


class Gather:
    def __init__(self, place, orders, ins, outs, sems):
        self.place, self.ins, self.outs = place, ins, outs
        self.send_sem, self.recv_sem, self.own_sem = sems
        self.n = len(orders)
        self.first = [ALONG_Y if order == "zyx" else ALONG_X for order in orders]
        self.second = [ALONG_X if order == "zyx" else ALONG_Y for order in orders]
        self.started = []
        self.counts = [0] * self.n

    def spot(self, a, source):
        return self.outs[a].at[self.place.number(source)]

    def index(self, step):
        return ((step[0] * 2 + step[1]) * 2 + step[2]) * 2 + step[3]

    def send(self, a, source, to):
        place = self.place
        self.started.append(
            place.copy(
                self.ins[a] if source == OWN else self.spot(a, source),
                self.spot(a, source),
                self.send_sem.at[a, self.counts[a]],
                self.recv_sem.at[a, self.index(place.minus(source, to))],
                place.device(to),
            )
        )
        self.counts[a] += 1

    def arrived(self, a, source):
        self.place.arrived(self.spot(a, source), self.recv_sem.at[a, self.index(source)])

    def begin(self):
        for a in range(self.n):
            for to in self.place.partners()[:-1]:
                self.send(a, OWN, to)
        self.kept = []
        for a in range(self.n):
            self.send(a, OWN, ALONG_CORE)
            copy = pltpu.make_async_copy(self.ins[a], self.spot(a, OWN), self.own_sem.at[a])
            copy.start()
            self.kept.append(copy)

    def middle(self, z):
        at = (z, 0, 0, 0)
        if z:
            for a in range(self.n):
                self.arrived(a, at)
                for to in (self.first[a], self.second[a], ALONG_CORE):
                    self.send(a, at, to)
        for a in range(self.n):
            source = self.place.plus(at, self.first[a])
            self.arrived(a, source)
            for to in (self.second[a], ALONG_CORE):
                self.send(a, source, to)

    def late(self, z):
        for a in range(self.n):
            for step in (self.second[a], self.place.plus(self.first[a], self.second[a])):
                source = self.place.plus((z, 0, 0, 0), step)
                self.arrived(a, source)
                self.send(a, source, ALONG_CORE)

    def finish(self):
        for z in near_first(self.place.sizes[0]):
            for y in range(2):
                for x in range(2):
                    for a in range(self.n):
                        self.arrived(a, (z, y, x, 1))
        for copy in self.started:
            copy.wait_send()
        for copy in self.kept:
            copy.wait()


def gather_scratch(n, n_hi):
    sends = (n_hi - 1) + 3 + (n_hi - 1) * 3 + n_hi * 2 + n_hi * 2
    dma = pltpu.SemaphoreType.DMA
    return [dma((n, sends)), dma((n, n_hi * 8)), dma((n,))]


def gather_kernel(n_hi, orders, *refs):
    n = len(orders)
    place = Place(n_hi)
    place.greet()
    gather = Gather(place, orders, refs[:n], refs[n : 2 * n], refs[2 * n :])
    gather.begin()
    for z in near_first(n_hi):
        gather.middle(z)
    for z in near_first(n_hi):
        gather.late(z)
    gather.finish()


def gather_rows(arrays, orders, collective_id):
    n = len(arrays)
    n_hi = lax.axis_size("dp") // 2
    return pl.pallas_call(
        functools.partial(gather_kernel, n_hi, orders),
        out_shape=[jax.ShapeDtypeStruct((n_hi * 8,) + a.shape, a.dtype) for a in arrays],
        in_specs=[ANYWHERE] * n,
        out_specs=[ANYWHERE] * n,
        scratch_shapes=gather_scratch(n, n_hi),
        compiler_params=pltpu.CompilerParams(collective_id=collective_id, has_side_effects=True),
    )(*arrays)


class Scatter:
    def __init__(self, place, orders, ins, outs, buffers, sems, small=None):
        self.place, self.ins, self.outs = place, ins, outs
        self.accs, self.from_core, self.from_first, self.from_second, self.from_z = buffers
        (
            self.load_sem,
            self.core_send,
            self.core_recv,
            self.first_send,
            self.first_recv,
            self.second_send,
            self.second_recv,
            self.z_send,
            self.z_recv,
        ) = sems[:9]
        self.small = small
        self.small_sems = sems[9:]
        self.n = len(orders)
        self.n_hi = place.sizes[0]
        self.first = [ALONG_X if order == "xyz" else ALONG_Y for order in orders]
        self.second = [ALONG_Y if order == "xyz" else ALONG_X for order in orders]
        self.started = []
        self.loads = {}

    def step(self, a, z, two, one):
        y, x = (two, one) if self.second[a] == ALONG_Y else (one, two)
        return (z, y, x, 0)

    def send(self, src, dst, send, recv, to):
        self.started.append(self.place.copy(src, dst, send, recv, self.place.device(to)))

    def begin(self, z, a):
        for two, one in ((1, 1), (0, 1), (1, 0), (0, 0)):
            s = (z * 2 + two) * 2 + one
            step = self.step(a, z, two, one)
            self.send(
                self.ins[a].at[self.place.number(step[:3] + (1,))],
                self.from_core[a].at[s],
                self.core_send.at[a, s],
                self.core_recv.at[a, s],
                ALONG_CORE,
            )
            load = pltpu.make_async_copy(
                self.ins[a].at[self.place.number(step)], self.accs[a].at[s], self.load_sem.at[a, s]
            )
            load.start()
            self.loads[a, s] = load

    def add(self, acc, got):
        width = min(acc.shape[1], 1024)

        def piece(k, carry):
            at = pl.ds(pl.multiple_of(k * width, width), width)
            acc[:, at] = (acc[:, at].astype(F32) + got[:, at].astype(F32)).astype(BF)
            return carry

        lax.fori_loop(0, acc.shape[1] // width, piece, 0)

    def core(self, z, a):
        for two, one in ((1, 1), (0, 1), (1, 0), (0, 0)):
            k = z * 2 + two
            s = k * 2 + one
            self.loads[a, s].wait()
            self.place.arrived(self.from_core[a].at[s], self.core_recv.at[a, s])
            self.add(self.accs[a].at[s], self.from_core[a].at[s])
            if one:
                self.send(
                    self.accs[a].at[s],
                    self.from_first[a].at[k],
                    self.first_send.at[a, k],
                    self.first_recv.at[a, k],
                    self.first[a],
                )

    def one(self, z, a):
        for two in (1, 0):
            k = z * 2 + two
            acc = self.accs[a].at[k * 2]
            self.place.arrived(self.from_first[a].at[k], self.first_recv.at[a, k])
            self.add(acc, self.from_first[a].at[k])
            if two:
                self.send(
                    acc,
                    self.from_second[a].at[z],
                    self.second_send.at[a, z],
                    self.second_recv.at[a, z],
                    self.second[a],
                )

    def two(self, z, a):
        acc = self.accs[a].at[z * 4]
        self.place.arrived(self.from_second[a].at[z], self.second_recv.at[a, z])
        self.add(acc, self.from_second[a].at[z])
        if z:
            self.send(
                acc,
                self.from_z[a].at[z - 1],
                self.z_send.at[a, z - 1],
                self.z_recv.at[a, z - 1],
                (z, 0, 0, 0),
            )

    def last(self, a):
        for z in range(1, self.n_hi):
            self.place.arrived(self.from_z[a].at[z - 1], self.z_recv.at[a, z - 1])
        out, acc, got = self.outs[a], self.accs[a].at[0], self.from_z[a]
        width = min(out.shape[1], 1024)

        def piece(k, carry):
            at = pl.ds(pl.multiple_of(k * width, width), width)
            total = acc[:, at].astype(F32)
            for z in range(1, self.n_hi):
                total = total + got[z - 1, :, at].astype(F32)
            out[:, at] = total
            return carry

        lax.fori_loop(0, out.shape[1] // width, piece, 0)

    def small_steps(self):
        return [ALONG_CORE, ALONG_X, ALONG_Y] + [1 << k for k in range((self.n_hi - 1).bit_length())]

    def small_begin(self):
        source, total, _ = self.small
        total[...] = source[...]
        self.small_send(0)

    def small_send(self, k):
        _, total, buffer = self.small
        step = self.small_steps()[k]
        z, y, x, core = self.place.at
        if isinstance(step, int):
            device = ((z + step - 2 * step * ((z // step) % 2)) * 2 + y, x * 2 + core)
        else:
            device = self.place.device(step)
        buffer[0, k] = total[...]
        send, recv = self.small_sems
        self.started.append(
            self.place.copy(buffer.at[0, k], buffer.at[1, k], send.at[k], recv.at[k], device)
        )

    def small_next(self, k):
        _, total, buffer = self.small
        self.place.arrived(buffer.at[1, k], self.small_sems[1].at[k])
        total[...] = total[...] + buffer[1, k]
        if k + 1 < len(self.small_steps()):
            self.small_send(k + 1)

    def finish(self):
        for copy in self.started:
            copy.wait_send()


def scatter_buffers(shapes, n_hi):
    counts = (n_hi * 4, n_hi * 4, n_hi * 2, n_hi, n_hi - 1)
    return [pltpu.VMEM((count,) + shape, BF) for count in counts for shape in shapes]


def scatter_sems(n, n_hi):
    counts = (n_hi * 4,) * 3 + (n_hi * 2,) * 2 + (n_hi,) * 2 + (n_hi - 1,) * 2
    return [pltpu.SemaphoreType.DMA((n, count)) for count in counts]


def scatter_kernel(n_hi, orders, *refs):
    n = len(orders)
    ins, small_in, outs, small_out = refs[:n], refs[n], refs[n + 1 : 2 * n + 1], refs[2 * n + 1]
    rest = refs[2 * n + 2 :]
    buffers = [rest[k * n : (k + 1) * n] for k in range(5)]
    place = Place(n_hi)
    place.greet()
    scatter = Scatter(
        place, orders, ins, outs, buffers, rest[5 * n + 1 :], (small_in, small_out, rest[5 * n])
    )
    order = near_first(n_hi)[::-1]
    rounds = len(scatter.small_steps())
    for k, z in enumerate(order):
        for a in range(n):
            scatter.begin(z, a)
        if k == 0:
            scatter.small_begin()
    for k in range(max(len(order) + 2, rounds)):
        for a in range(n):
            if k < len(order):
                scatter.core(order[k], a)
        for a in range(n):
            if 0 <= k - 1 < len(order):
                scatter.one(order[k - 1], a)
        for a in range(n):
            if 0 <= k - 2 < len(order):
                scatter.two(order[k - 2], a)
        if k < rounds:
            scatter.small_next(k)
    for a in range(n):
        scatter.last(a)
    scatter.finish()


def scatter_sums(arrays, orders, small, collective_id):
    n = len(arrays)
    n_hi = lax.axis_size("dp") // 2
    shapes = [a.shape[1:] for a in arrays]
    rounds = 3 + (n_hi - 1).bit_length()
    dma = pltpu.SemaphoreType.DMA
    return pl.pallas_call(
        functools.partial(scatter_kernel, n_hi, orders),
        out_shape=[jax.ShapeDtypeStruct(shape, F32) for shape in shapes]
        + [jax.ShapeDtypeStruct(small.shape, F32)],
        in_specs=[ANYWHERE] * n + [IN_VMEM],
        out_specs=[IN_VMEM] * (n + 1),
        scratch_shapes=scatter_buffers(shapes, n_hi)
        + [pltpu.VMEM((2, rounds) + small.shape, F32)]
        + scatter_sems(n, n_hi)
        + [dma((rounds,)), dma((rounds,))],
        compiler_params=pltpu.CompilerParams(
            collective_id=collective_id, has_side_effects=True, vmem_limit_bytes=56 << 20
        ),
    )(*arrays, small)


def recall_kernel(qa_ref, qb_ref, mem_ref, slot_ref, outa_ref, outb_ref, lse_ref, p_ref):
    slots, tokens = p_ref.shape[1], p_ref.shape[2]
    half = tokens // 2
    chosen = slot_ref[0]
    low, high = chosen & 7, chosen >> 3
    queries = jnp.concatenate([qa_ref[...], qb_ref[...]], axis=0)
    step = 256
    picked = jnp.zeros((8, tokens), F32)
    for at in range(0, slots, step):
        scores = dot(mem_ref[0, pl.ds(at, step), pl.ds(0, HD)], queries, NT)
        for row in range(0, step, 8):
            got = jnp.take_along_axis(scores[row : row + 8], low, axis=0)
            picked = jnp.where(high == (at + row) // 8, got, picked)
    scores = picked * SCALE
    top = jnp.max(scores, axis=0, keepdims=True)
    weights = jnp.exp(scores - top)
    total = jnp.sum(weights, axis=0, keepdims=True)
    lse_ref[0] = top + jnp.log(total)
    times = jnp.ones_like(weights)
    for turn in range(1, 8):
        times = times + jnp.where(pltpu.roll(chosen, turn, 0) == chosen, 1.0, 0.0)
    probs = (weights / total * times).astype(BF)
    rows = lax.broadcasted_iota(jnp.int32, (step, tokens), 0).astype(F32).astype(BF)
    out = jnp.zeros((HD, tokens), F32)
    values_t = mem_ref[0, :, pl.ds(HD, HD)].T
    for at in range(0, slots, step):
        mine = jnp.where(chosen // step == at // step, chosen % step, -1).astype(F32).astype(BF)
        dense = jnp.zeros((step, tokens), BF)
        for j in range(8):
            dense = jnp.where(rows == mine[j : j + 1], probs[j : j + 1], dense)
        p_ref[0, pl.ds(at, step), :] = dense
        out = out + dot(values_t[:, at : at + step], dense)
    out = out.T.astype(BF)
    outa_ref[...] = out[:half]
    outb_ref[...] = out[half:]


def recall_grad_kernel(ga_ref, gb_ref, mem_ref, p_ref, delta_ref, share_ref, outa_ref, outb_ref):
    slots, tokens = p_ref.shape[1], p_ref.shape[2]
    half = tokens // 2
    grads = jnp.concatenate([ga_ref[...], gb_ref[...]], axis=0)
    delta = delta_ref[0]
    keys_t = mem_ref[0, :, pl.ds(0, HD)].T
    step = 512
    out = jnp.zeros((HD, tokens), F32)
    for at in range(0, slots, step):
        along = dot(mem_ref[0, pl.ds(at, step), pl.ds(HD, HD)], grads, NT)
        scores = (along - delta).astype(BF) * p_ref[0, pl.ds(at, step), :]
        out = out + dot(keys_t[:, at : at + step], scores)
    out = (out * (share_ref[0] * SCALE)).T.astype(BF)
    outa_ref[...] = out[:half]
    outb_ref[...] = out[half:]


def head_columns(rows, first=0):
    return pl.BlockSpec((rows, HD), lambda h: (0, first + h))


def per_head(*shape):
    return pl.BlockSpec((1,) + shape, lambda h: (h,) + (0,) * len(shape))


def recall(query_a, query_b, table, chosen):
    rows, slots = query_a.shape[0], table.shape[1]
    return pl.pallas_call(
        recall_kernel,
        grid=(H,),
        in_specs=[
            head_columns(rows),
            head_columns(rows),
            per_head(slots, 2 * HD),
            per_head(8, 2 * rows),
        ],
        out_specs=[
            head_columns(rows),
            head_columns(rows),
            per_head(1, 2 * rows),
            per_head(slots, 2 * rows),
        ],
        out_shape=[
            jax.ShapeDtypeStruct(query_a.shape, BF),
            jax.ShapeDtypeStruct(query_a.shape, BF),
            jax.ShapeDtypeStruct((H, 1, 2 * rows), F32),
            jax.ShapeDtypeStruct((H, slots, 2 * rows), BF),
        ],
        compiler_params=pltpu.CompilerParams(vmem_limit_bytes=48 << 20),
        cost_estimate=pl.CostEstimate(
            flops=8 * rows * slots * HD * H, bytes_accessed=64 << 20, transcendentals=0
        ),
    )(query_a, query_b, table, chosen)


def recall_grad(grad_a, grad_b, table, probs, delta, share):
    rows, slots = grad_a.shape[0], table.shape[1]
    return pl.pallas_call(
        recall_grad_kernel,
        grid=(H,),
        in_specs=[
            head_columns(rows),
            head_columns(rows),
            per_head(slots, 2 * HD),
            per_head(slots, 2 * rows),
            per_head(1, 2 * rows),
            per_head(1, 2 * rows),
        ],
        out_specs=[head_columns(rows), head_columns(rows)],
        out_shape=[jax.ShapeDtypeStruct(grad_a.shape, BF)] * 2,
        compiler_params=pltpu.CompilerParams(vmem_limit_bytes=48 << 20),
        cost_estimate=pl.CostEstimate(
            flops=8 * rows * slots * HD * H, bytes_accessed=64 << 20, transcendentals=0
        ),
    )(grad_a, grad_b, table, probs, delta, share)


def near_buckets():
    distance = np.arange(NEAR)
    exact = BUCKETS // 2
    far = exact + np.floor(
        np.log(np.maximum(distance, 1) / exact) / np.log(128.0 / exact) * exact
    )
    return np.where(distance < exact, distance, np.minimum(far, BUCKETS - 1)).astype(np.int32)


def near_hot():
    return near_buckets()[:, None] == np.arange(BUCKETS)[None, :]


def near_bias(rel_table):
    above = (rel_table - rel_table[-1:])[None]
    rows = jnp.sum(jnp.where(jnp.asarray(near_hot())[:, :, None], above, 0.0), axis=1)
    return jnp.pad(rows.T, ((0, 0), (0, NEAR)))[:, None, :]


def table_gradient(diagonals, totals):
    near = diagonals[:, 0, NEAR - 1 : 2 * NEAR - 1]
    sums = jnp.dot(near, jnp.asarray(near_hot(), F32), precision=HIGHEST)
    far = jnp.sum(totals, axis=(1, 2)) - jnp.sum(near, axis=1)
    return (sums + far[:, None] * (np.arange(BUCKETS) == BUCKETS - 1)).T


def segment_kernel(len_ref, near_ref, q_ref, kc_ref, kn_ref, vc_ref, vn_ref, out_ref, p_ref):
    length = len_ref[0]
    band = pltpu.roll(
        jnp.broadcast_to(near_ref[0], (NEAR, 2 * NEAR)), 0, 1, stride=1, stride_axis=0
    )
    key_ids = lax.broadcasted_iota(jnp.int32, (NEAR, NEAR), 0)
    query_ids = lax.broadcasted_iota(jnp.int32, (NEAR, NEAR), 1)
    on_diagonal = jnp.where(query_ids >= key_ids, band[:, :NEAR], NEGATIVE)
    beside = band[:, NEAR:]
    masked = jnp.full((NEAR, NEAR), NEGATIVE, F32)
    zero = jnp.zeros((NEAR, NEAR), F32)
    cache_t, values_t = vc_ref[...].T, vn_ref[...].T
    step = 2 * NEAR
    for at in range(W // step):
        count = 2 * (at + 1)
        queries = q_ref[pl.ds(step * at, step), :]
        cached = dot(kc_ref[...], queries, NT) * SCALE
        if at == 0:
            last = cached[W - NEAR :] + jnp.concatenate([beside, zero], axis=1)
            cached = jnp.concatenate([cached[: W - NEAR], last], axis=0)
        fresh = dot(kn_ref[pl.ds(0, NEAR * count), :], queries, NT) * SCALE
        rows = [cached]
        for k in range(count):
            block = fresh[NEAR * k : NEAR * (k + 1)]
            tiles = [
                masked if q < k else on_diagonal if q == k else beside if q == k + 1 else zero
                for q in (2 * at, 2 * at + 1)
            ]
            if any(tile is not zero for tile in tiles):
                block = block + jnp.concatenate(tiles, axis=1)
            ids = lax.broadcasted_iota(jnp.int32, (NEAR, step), 0) + NEAR * k
            rows.append(jnp.where(ids < length, block, NEGATIVE))
        scores = jnp.concatenate(rows, axis=0)
        weights = jnp.exp(scores - jnp.max(scores, axis=0, keepdims=True))
        probs = (weights * (1.0 / jnp.sum(weights, axis=0, keepdims=True))).astype(BF)
        p_ref[0, pl.ds(0, W + NEAR * count), pl.ds(step * at, step)] = probs
        out = dot(cache_t, probs[:W]) + dot(values_t[:, : NEAR * count], probs[W:])
        out_ref[pl.ds(step * at, step), :] = out.T


def segment_grad_kernel(
    open_ref, g_ref, q_ref, kc_ref, kn_ref, vc_ref, vn_ref, p_ref, gq_ref, gk_ref, gv_ref, diag_ref, tot_ref
):
    closed = 1.0 - open_ref[pl.program_id(0)]
    cache_t, keys_t = kc_ref[...].T, kn_ref[...].T
    on_diagonal = jnp.zeros((NEAR, NEAR), F32)
    beside = jnp.zeros((NEAR, NEAR), F32)
    step = 2 * NEAR
    total = jnp.zeros((8, step), F32)
    grad_keys, grad_values = [], []
    for at in range(W // step):
        count = 2 * (at + 1)
        grads = (closed * g_ref[pl.ds(step * at, step), :]).astype(BF)
        queries = q_ref[pl.ds(step * at, step), :]
        grad_probs = jnp.concatenate(
            [dot(vc_ref[...], grads, NT), dot(vn_ref[pl.ds(0, NEAR * count), :], grads, NT)], axis=0
        )
        probs = p_ref[0, pl.ds(0, W + NEAR * count), pl.ds(step * at, step)]
        wide = probs.astype(F32)
        product = wide * grad_probs
        grad_scores = product - wide * jnp.sum(product, axis=0, keepdims=True)
        low = grad_scores.astype(BF)
        grad_q = dot(cache_t, low[:W]) + dot(keys_t[:, : NEAR * count], low[W:])
        gq_ref[pl.ds(step * at, step), :] = (grad_q * SCALE).T
        grad_keys.append(dot(low[W:], queries) * SCALE)
        grad_values.append(dot(probs[W:], grads))
        if at == 0:
            beside = beside + grad_scores[W - NEAR : W, :NEAR]
        for k in range(count):
            for side, q in enumerate((2 * at, 2 * at + 1)):
                tile = grad_scores[W + NEAR * k : W + NEAR * (k + 1), NEAR * side : NEAR * (side + 1)]
                if q == k:
                    on_diagonal = on_diagonal + tile
                elif q == k + 1:
                    beside = beside + tile
        total = total + jnp.sum(grad_scores.reshape(-1, 8, step), axis=0)
    for ref, (early, late) in ((gk_ref, grad_keys), (gv_ref, grad_values)):
        ref[...] = jnp.concatenate([late[:step] + early, late[step:]], axis=0).astype(BF)
    down = lax.broadcasted_iota(jnp.int32, (NEAR, NEAR), 0)
    across = lax.broadcasted_iota(jnp.int32, (NEAR, NEAR), 1)
    turned = lax.dot_general(
        (down + across == NEAR - 1).astype(F32),
        jnp.concatenate([on_diagonal, beside], axis=1),
        NN,
        precision=HIGHEST,
        preferred_element_type=F32,
    )
    diagonals = pltpu.roll(turned, 0, 1, stride=1, stride_axis=0)
    diag_ref[0] = jnp.sum(diagonals, axis=0, keepdims=True)
    tot_ref[0] = total


def segment_forward(queries, keys_values, cache, near, length):
    return pl.pallas_call(
        segment_kernel,
        grid=(H,),
        in_specs=[
            SCALARS,
            per_head(1, 2 * NEAR),
            head_columns(W),
            head_columns(W),
            head_columns(W),
            head_columns(W, H),
            head_columns(W, H),
        ],
        out_specs=[head_columns(W), per_head(2 * W, W)],
        out_shape=[
            jax.ShapeDtypeStruct((W, H * HD), F32),
            jax.ShapeDtypeStruct((H, 2 * W, W), BF),
        ],
        compiler_params=pltpu.CompilerParams(vmem_limit_bytes=32 << 20),
        cost_estimate=pl.CostEstimate(
            flops=8 * W * W * HD * H, bytes_accessed=20 << 20, transcendentals=0
        ),
    )(length, near, queries, cache, keys_values, cache, keys_values)


def segment_backward(gate_open, grad_mixed, queries, keys_values, cache, probs):
    return pl.pallas_call(
        segment_grad_kernel,
        grid=(H,),
        in_specs=[
            SCALARS,
            head_columns(W),
            head_columns(W),
            head_columns(W),
            head_columns(W),
            head_columns(W, H),
            head_columns(W, H),
            per_head(2 * W, W),
        ],
        out_specs=[
            head_columns(W),
            head_columns(W),
            head_columns(W),
            per_head(1, 2 * NEAR),
            per_head(8, 2 * NEAR),
        ],
        out_shape=[
            jax.ShapeDtypeStruct((W, H * HD), F32),
            jax.ShapeDtypeStruct((W, H * HD), BF),
            jax.ShapeDtypeStruct((W, H * HD), BF),
            jax.ShapeDtypeStruct((H, 1, 2 * NEAR), F32),
            jax.ShapeDtypeStruct((H, 8, 2 * NEAR), F32),
        ],
        compiler_params=pltpu.CompilerParams(vmem_limit_bytes=32 << 20),
        cost_estimate=pl.CostEstimate(
            flops=16 * W * W * HD * H, bytes_accessed=20 << 20, transcendentals=0
        ),
    )(gate_open, grad_mixed, queries, cache, keys_values, cache, keys_values, probs)


def norm_forward(values, gain_row, shift_row):
    center = values - jnp.mean(values, axis=-1, keepdims=True)
    inverse = lax.rsqrt(jnp.mean(center * center, axis=-1, keepdims=True) + EPSILON)
    scaled = center * inverse
    return (scaled * gain_row + shift_row, scaled, inverse)


def norm_backward(grad_normed, scaled, inverse, gain_row):
    grad_scaled = grad_normed * gain_row
    mean_grad = jnp.mean(grad_scaled, axis=-1, keepdims=True)
    mean_cross = jnp.mean(grad_scaled * scaled, axis=-1, keepdims=True)
    return inverse * (grad_scaled - mean_grad - scaled * mean_cross)


def swap(value, turn):
    return jax.tree.map(
        lambda v: lax.ppermute(v, "mem", [(i, i ^ turn) for i in range(lax.axis_size("mem"))]), value
    )


def combine(outs, lses):
    total = jax.nn.logsumexp(jnp.stack(lses), axis=0)
    rows = outs[0].shape[0]
    result = 0.0
    for out, lse in zip(outs, lses):
        share = jnp.exp(lse - total).T[:, :, None]
        result = result + share * out.reshape(rows, H, HD).astype(F32)
    return result.reshape(rows, H * HD), total


def local(
    tokens,
    norm_gains,
    norm_shifts,
    w_qkv,
    w_out,
    w_up,
    w_down,
    rel_table,
    gate_bias,
    xl_cache,
    memory,
    slot_index,
    seg_len,
    cotangent,
):
    width = tokens.shape[1]
    count = tokens.shape[0]
    slot_count = memory.shape[0]
    groups = lax.axis_size("mem")
    me = lax.axis_index("mem")

    norms = jnp.pad(
        jnp.concatenate([norm_gains, norm_shifts], axis=0),
        ((0, 12), (0, 128 - norm_gains.shape[1])),
    )
    full_q, full_norms = gather_rows([w_qkv[:, :width], norms], ("zyx", "zxy"), 0)
    full_kv, full_out, full_up, full_down = gather_rows(
        [w_qkv[:, width:], w_out, w_up, w_down], ("zxy", "zyx", "zyx", "zxy"), 1
    )
    full_q, full_kv, full_out, full_up, full_down = [
        full.reshape(-1, full.shape[2]) for full in (full_q, full_kv, full_out, full_up, full_down)
    ]
    rows = full_norms[:, :4, : norm_gains.shape[1]].astype(F32)
    rows = rows.transpose(1, 0, 2).reshape(4, width)
    gain_rows, shift_rows = rows[:2], rows[2:]

    inputs = tokens.astype(F32)
    normed_one, scaled_one, inverse_one = norm_forward(inputs, gain_rows[0], shift_rows[0])
    normed_one = normed_one.astype(BF)
    queries = dot(normed_one, full_q).astype(BF)
    query_core, query_x = swap(queries, 1), swap(queries, 2)
    query_cross = swap(query_x, 1)

    table = memory.transpose(1, 0, 2)
    slot_rows = (slot_index - me * slot_count).reshape(groups, count, H, -1).transpose(0, 2, 3, 1)
    picks = [
        lax.dynamic_index_in_dim(slot_rows, me ^ turn, 0, keepdims=False) for turn in range(groups)
    ]
    out_own, out_core, lse_chip, probs_chip = recall(
        queries, query_core, table, jnp.concatenate(picks[:2], axis=-1)
    )
    out_x, out_cross, lse_far, probs_far = recall(
        query_x, query_cross, table, jnp.concatenate(picks[2:], axis=-1)
    )
    lse_chip, lse_far = lse_chip[:, 0], lse_far[:, 0]
    keys_values = dot(normed_one, full_kv).astype(BF)
    local_out, probs_local = segment_forward(
        queries, keys_values, xl_cache, near_bias(rel_table), seg_len
    )

    own_lse, own_out = lse_chip[:, :count], out_own
    core_out, core_lse = swap((out_core, lse_chip[:, count:]), 1)
    other_out, other_lse = swap((out_cross, lse_far[:, count:]), 1)
    pair_out, pair_lse = combine((out_x, other_out), (lse_far[:, :count], other_lse))
    far_out, far_lse = swap((pair_out.astype(BF), pair_lse), 2)
    recalled, total_lse = combine((own_out, core_out, far_out), (own_lse, core_lse, far_lse))

    gate_open = jax.nn.sigmoid(gate_bias)
    gate_row = jnp.repeat(gate_open, HD)[None]
    mixed_low = (gate_row * recalled + (1.0 - gate_row) * local_out).astype(BF)
    attended = inputs + dot(mixed_low, full_out)
    normed_two, scaled_two, inverse_two = norm_forward(attended, gain_rows[1], shift_rows[1])
    normed_two = normed_two.astype(BF)
    up_pre = dot(normed_two, full_up)
    hidden = jax.nn.gelu(up_pre).astype(BF)
    output = attended + dot(hidden, full_down)

    grad_output = cotangent.astype(F32)
    grad_down = jnp.einsum("tf,td->fd", hidden, cotangent, preferred_element_type=F32)
    grad_hidden = dot(cotangent, full_down, NT)
    grad_up_pre = jax.vjp(jax.nn.gelu, up_pre)[1](grad_hidden)[0].astype(BF)
    grad_up = jnp.einsum("td,tf->df", normed_two, grad_up_pre, preferred_element_type=F32)
    grad_normed_two = dot(grad_up_pre, full_up, NT)
    grad_attended = grad_output + norm_backward(
        grad_normed_two, scaled_two, inverse_two, gain_rows[1]
    )
    attended_low = grad_attended.astype(BF)
    grad_wout = jnp.einsum("td,te->de", mixed_low, attended_low, preferred_element_type=F32)
    grad_mixed = dot(attended_low, full_out, NT)
    grad_gate = (
        jnp.sum((grad_mixed * (recalled - local_out)).reshape(count, H, HD), axis=(0, 2))
        * gate_open
        * (1.0 - gate_open)
    )
    grad_recalled = (gate_row * grad_mixed).astype(BF)
    delta = jnp.sum(
        (grad_recalled.astype(F32) * recalled).reshape(count, H, HD), axis=-1
    ).T
    sent = (grad_recalled, jnp.concatenate([delta, total_lse], axis=0))
    sent_core, sent_x = swap(sent, 1), swap(sent, 2)
    sent_cross = swap(sent_x, 1)

    grad_query_local, grad_keys, grad_values, diagonals, totals = segment_backward(
        gate_open, grad_mixed, queries, keys_values, xl_cache, probs_local
    )
    grad_table = table_gradient(diagonals, totals)

    def recall_back(left, right, lse, probs):
        delta_rows = jnp.concatenate([left[1][:H], right[1][:H]], axis=1)
        total_rows = jnp.concatenate([left[1][H:], right[1][H:]], axis=1)
        return recall_grad(
            left[0],
            right[0],
            table,
            probs,
            delta_rows[:, None],
            jnp.exp(lse - total_rows)[:, None],
        )

    back_x, back_cross = recall_back(sent_x, sent_cross, lse_far, probs_far)
    back_own, back_core = recall_back(sent, sent_core, lse_chip, probs_chip)
    pair_back = (back_x.astype(F32) + swap(back_cross, 1).astype(F32)).astype(BF)
    grad_query = (
        grad_query_local
        + back_own.astype(F32)
        + swap(back_core, 1).astype(F32)
        + swap(pair_back, 2).astype(F32)
    )
    grad_qkv_low = jnp.concatenate([grad_query.astype(BF), grad_keys, grad_values], axis=1)
    grad_wqkv = jnp.einsum("td,te->de", normed_one, grad_qkv_low, preferred_element_type=F32)
    grad_normed_one = dot(grad_qkv_low[:, :width], full_q, NT) + dot(
        grad_qkv_low[:, width:], full_kv, NT
    )
    grad_tokens = grad_attended + norm_backward(
        grad_normed_one, scaled_one, inverse_one, gain_rows[0]
    )
    grad_norms = jnp.stack(
        [
            jnp.sum(grad_normed_one * scaled_one, axis=0),
            jnp.sum(grad_normed_two * scaled_two, axis=0),
            jnp.sum(grad_normed_one, axis=0),
            jnp.sum(grad_normed_two, axis=0),
        ]
    )
    devices = lax.axis_size("dp") * groups
    rest = jnp.pad(jnp.concatenate([grad_table.reshape(-1), grad_gate]), (0, 1024 - 264))
    small = jnp.concatenate([grad_norms.reshape(-1, 128), rest.reshape(-1, 128)], axis=0)
    share_qkv, share_out, share_up, share_down, small = scatter_sums(
        [
            g.astype(BF).reshape(devices, -1, g.shape[1])
            for g in (grad_wqkv, grad_wout, grad_up, grad_down)
        ],
        ("yxz", "xyz", "xyz", "yxz"),
        small,
        2,
    )
    own = norm_gains.shape[1]
    at = (lax.axis_index("dp") * groups + me) * own
    share_norms = lax.dynamic_slice_in_dim(small[:32].reshape(4, width), at, own, axis=1)
    rest = small[32:].reshape(-1)
    table_total, gate_total = rest[: BUCKETS * H].reshape(BUCKETS, H), rest[BUCKETS * H :][:H]
    return (
        output.astype(BF),
        grad_tokens,
        share_norms[:2],
        share_norms[2:],
        share_qkv,
        share_out,
        share_up,
        share_down,
        table_total,
        gate_total,
    )


def solution(mesh):
    shard = P(AXES, None)
    placed = (
        shard,
        P(None, AXES),
        P(None, AXES),
        shard,
        shard,
        shard,
        shard,
        P(),
        P(),
        shard,
        P(AXES, None, None),
        P("dp", None, "mem"),
        P(AXES),
        shard,
    )
    return jax.shard_map(
        local,
        mesh=mesh,
        in_specs=placed,
        out_specs=(
            shard,
            shard,
            P(None, AXES),
            P(None, AXES),
            shard,
            shard,
            shard,
            shard,
            P(),
            P(),
        ),
        check_vma=False,
    )
```

```python
import functools

import jax
import jax.numpy as jnp
import numpy as np
from jax import lax
from jax.experimental import pallas as pl
from jax.experimental.pallas import tpu as pltpu
from jax.sharding import PartitionSpec as P

H = 8
HD = 128
W = 512
BUCKETS = 32
NEAR = 128
EPSILON = 1e-05
NEGATIVE = -1e30
SCALE = HD ** (-0.5)
AXES = ("dp", "mem")
MESH = pl.DeviceIdType.MESH
HIGHEST = lax.Precision.HIGHEST
BF = jnp.bfloat16
F32 = jnp.float32
NT = (((1,), (1,)), ((), ()))
NN = (((1,), (0,)), ((), ()))


def dot(left, right, dims=NN):
    return lax.dot_general(left, right, dims, preferred_element_type=F32)


OWN, ALONG_Y, ALONG_X, ALONG_CORE = (0, 0, 0, 0), (0, 1, 0, 0), (0, 0, 1, 0), (0, 0, 0, 1)
ANYWHERE = pl.BlockSpec(memory_space=pl.ANY)
IN_VMEM = pl.BlockSpec(memory_space=pltpu.VMEM)
SCALARS = pl.BlockSpec(memory_space=pltpu.SMEM)


class Place:
    def __init__(self, n_hi):
        self.sizes = (n_hi, 2, 2, 2)
        dp, mem = lax.axis_index("dp"), lax.axis_index("mem")
        self.at = (dp // 2, dp % 2, mem // 2, mem % 2)

    def device(self, step):
        z, y, x, core = [(a + s) % n for a, s, n in zip(self.at, step, self.sizes)]
        return (z * 2 + y, x * 2 + core)

    def number(self, step):
        dp, mem = self.device(step)
        return dp * 4 + mem

    def plus(self, left, right):
        return tuple((a + b) % n for a, b, n in zip(left, right, self.sizes))

    def minus(self, left, right):
        return tuple((a - b) % n for a, b, n in zip(left, right, self.sizes))

    def partners(self):
        return [(z, 0, 0, 0) for z in range(1, self.sizes[0])] + [ALONG_Y, ALONG_X, ALONG_CORE]

    def greet(self):
        barrier = pltpu.get_barrier_semaphore()
        for partner in self.partners():
            pl.semaphore_signal(
                barrier, inc=1, device_id=self.device(partner), device_id_type=MESH
            )
        pl.semaphore_wait(barrier, len(self.partners()))

    def copy(self, src, dst, send, recv, device):
        copy = pltpu.make_async_remote_copy(
            src_ref=src,
            dst_ref=dst,
            send_sem=send,
            recv_sem=recv,
            device_id=device,
            device_id_type=MESH,
        )
        copy.start()
        return copy

    def arrived(self, ref, recv):
        pltpu.make_async_remote_copy(
            src_ref=ref,
            dst_ref=ref,
            send_sem=recv,
            recv_sem=recv,
            device_id=self.device(ALONG_CORE),
            device_id_type=MESH,
        ).wait_recv()


def near_first(n_hi):
    order = [0]
    for z in range(1, n_hi // 2 + 1):
        order += [k for k in dict.fromkeys((z, n_hi - z)) if k < n_hi]
    return order


class Gather:
    def __init__(self, place, orders, ins, outs, sems):
        self.place, self.ins, self.outs = place, ins, outs
        self.send_sem, self.recv_sem, self.own_sem = sems
        self.n = len(orders)
        self.first = [ALONG_Y if order == "zyx" else ALONG_X for order in orders]
        self.second = [ALONG_X if order == "zyx" else ALONG_Y for order in orders]
        self.sent = [[] for _ in orders]

    def spot(self, a, source):
        return self.outs[a].at[self.place.number(source)]

    def index(self, step):
        return ((step[0] * 2 + step[1]) * 2 + step[2]) * 2 + step[3]

    def copy(self, a, k):
        source, to = self.sent[a][k]
        place = self.place
        return pltpu.make_async_remote_copy(
            src_ref=self.ins[a] if source == OWN else self.spot(a, source),
            dst_ref=self.spot(a, source),
            send_sem=self.send_sem.at[a, k],
            recv_sem=self.recv_sem.at[a, self.index(place.minus(source, to))],
            device_id=place.device(to),
            device_id_type=MESH,
        )

    def send(self, a, source, to):
        self.sent[a].append((source, to))
        self.copy(a, len(self.sent[a]) - 1).start()

    def own(self, a):
        return pltpu.make_async_copy(self.ins[a], self.spot(a, OWN), self.own_sem.at[a])

    def arrived(self, a, source):
        self.place.arrived(self.spot(a, source), self.recv_sem.at[a, self.index(source)])

    def begin(self, a):
        for to in self.place.partners():
            self.send(a, OWN, to)
        self.own(a).start()

    def middle(self, a, z):
        at = (z, 0, 0, 0)
        if z:
            self.arrived(a, at)
            for to in (self.first[a], self.second[a], ALONG_CORE):
                self.send(a, at, to)
        source = self.place.plus(at, self.first[a])
        self.arrived(a, source)
        for to in (self.second[a], ALONG_CORE):
            self.send(a, source, to)

    def late(self, a, z):
        for step in (self.second[a], self.place.plus(self.first[a], self.second[a])):
            source = self.place.plus((z, 0, 0, 0), step)
            self.arrived(a, source)
            self.send(a, source, ALONG_CORE)

    def finish(self, a):
        for z in near_first(self.place.sizes[0]):
            for y in range(2):
                for x in range(2):
                    self.arrived(a, (z, y, x, 1))
        for k in range(len(self.sent[a])):
            self.copy(a, k).wait_send()
        self.own(a).wait()


def gather_sems(n, n_hi):
    sends = (n_hi - 1) + 3 + (n_hi - 1) * 3 + n_hi * 2 + n_hi * 2
    dma = pltpu.SemaphoreType.DMA
    return [dma((n, sends)), dma((n, n_hi * 8)), dma((n,))]


class Scatter:
    def __init__(self, place, orders, ins, outs, buffers, sems, small=None):
        self.place, self.ins, self.outs = place, ins, outs
        self.accs, self.from_core, self.from_first, self.from_second, self.from_z = buffers
        (
            self.load_sem,
            self.core_send,
            self.core_recv,
            self.first_send,
            self.first_recv,
            self.second_send,
            self.second_recv,
            self.z_send,
            self.z_recv,
        ) = sems[:9]
        self.small = small
        self.small_sems = sems[9:]
        self.n = len(orders)
        self.n_hi = place.sizes[0]
        self.first = [ALONG_X if order == "xyz" else ALONG_Y for order in orders]
        self.second = [ALONG_Y if order == "xyz" else ALONG_X for order in orders]
        self.started = []
        self.loads = {}

    def step(self, a, z, two, one):
        y, x = (two, one) if self.second[a] == ALONG_Y else (one, two)
        return (z, y, x, 0)

    def send(self, src, dst, send, recv, to):
        self.started.append(self.place.copy(src, dst, send, recv, self.place.device(to)))

    def begin(self, z, a):
        for two, one in ((1, 1), (0, 1), (1, 0), (0, 0)):
            s = (z * 2 + two) * 2 + one
            step = self.step(a, z, two, one)
            self.send(
                self.ins[a].at[self.place.number(step[:3] + (1,))],
                self.from_core[a].at[s],
                self.core_send.at[a, s],
                self.core_recv.at[a, s],
                ALONG_CORE,
            )
            load = pltpu.make_async_copy(
                self.ins[a].at[self.place.number(step)], self.accs[a].at[s], self.load_sem.at[a, s]
            )
            load.start()
            self.loads[a, s] = load

    def add(self, acc, got):
        width = min(acc.shape[1], 1024)

        def piece(k, carry):
            at = pl.ds(pl.multiple_of(k * width, width), width)
            acc[:, at] = (acc[:, at].astype(F32) + got[:, at].astype(F32)).astype(BF)
            return carry

        lax.fori_loop(0, acc.shape[1] // width, piece, 0)

    def core(self, z, a):
        for two, one in ((1, 1), (0, 1), (1, 0), (0, 0)):
            k = z * 2 + two
            s = k * 2 + one
            self.loads[a, s].wait()
            self.place.arrived(self.from_core[a].at[s], self.core_recv.at[a, s])
            self.add(self.accs[a].at[s], self.from_core[a].at[s])
            if one:
                self.send(
                    self.accs[a].at[s],
                    self.from_first[a].at[k],
                    self.first_send.at[a, k],
                    self.first_recv.at[a, k],
                    self.first[a],
                )

    def one(self, z, a):
        for two in (1, 0):
            k = z * 2 + two
            acc = self.accs[a].at[k * 2]
            self.place.arrived(self.from_first[a].at[k], self.first_recv.at[a, k])
            self.add(acc, self.from_first[a].at[k])
            if two:
                self.send(
                    acc,
                    self.from_second[a].at[z],
                    self.second_send.at[a, z],
                    self.second_recv.at[a, z],
                    self.second[a],
                )

    def two(self, z, a):
        acc = self.accs[a].at[z * 4]
        self.place.arrived(self.from_second[a].at[z], self.second_recv.at[a, z])
        self.add(acc, self.from_second[a].at[z])
        if z:
            self.send(
                acc,
                self.from_z[a].at[z - 1],
                self.z_send.at[a, z - 1],
                self.z_recv.at[a, z - 1],
                (z, 0, 0, 0),
            )

    def last(self, a):
        for z in range(1, self.n_hi):
            self.place.arrived(self.from_z[a].at[z - 1], self.z_recv.at[a, z - 1])
        out, acc, got = self.outs[a], self.accs[a].at[0], self.from_z[a]
        width = min(out.shape[1], 1024)

        def piece(k, carry):
            at = pl.ds(pl.multiple_of(k * width, width), width)
            total = acc[:, at].astype(F32)
            for z in range(1, self.n_hi):
                total = total + got[z - 1, :, at].astype(F32)
            out[:, at] = total
            return carry

        lax.fori_loop(0, out.shape[1] // width, piece, 0)

    def small_steps(self):
        return [ALONG_CORE, ALONG_X, ALONG_Y] + [1 << k for k in range((self.n_hi - 1).bit_length())]

    def small_begin(self):
        source, total, _ = self.small
        total[...] = source[...]
        self.small_send(0)

    def small_send(self, k):
        _, total, buffer = self.small
        step = self.small_steps()[k]
        z, y, x, core = self.place.at
        if isinstance(step, int):
            device = ((z + step - 2 * step * ((z // step) % 2)) * 2 + y, x * 2 + core)
        else:
            device = self.place.device(step)
        buffer[0, k] = total[...]
        send, recv = self.small_sems
        self.started.append(
            self.place.copy(buffer.at[0, k], buffer.at[1, k], send.at[k], recv.at[k], device)
        )

    def small_next(self, k):
        _, total, buffer = self.small
        self.place.arrived(buffer.at[1, k], self.small_sems[1].at[k])
        total[...] = total[...] + buffer[1, k]
        if k + 1 < len(self.small_steps()):
            self.small_send(k + 1)

    def finish(self):
        for copy in self.started:
            copy.wait_send()


def scatter_buffers(shapes, n_hi):
    counts = (n_hi * 4, n_hi * 4, n_hi * 2, n_hi, n_hi - 1)
    return [pltpu.VMEM((count,) + shape, BF) for count in counts for shape in shapes]


def scatter_sems(n, n_hi):
    counts = (n_hi * 4,) * 3 + (n_hi * 2,) * 2 + (n_hi,) * 2 + (n_hi - 1,) * 2
    return [pltpu.SemaphoreType.DMA((n, count)) for count in counts]


def scatter_kernel(n_hi, orders, *refs):
    n = len(orders)
    ins, small_in, outs, small_out = refs[:n], refs[n], refs[n + 1 : 2 * n + 1], refs[2 * n + 1]
    rest = refs[2 * n + 2 :]
    buffers = [rest[k * n : (k + 1) * n] for k in range(5)]
    place = Place(n_hi)
    place.greet()
    scatter = Scatter(
        place, orders, ins, outs, buffers, rest[5 * n + 1 :], (small_in, small_out, rest[5 * n])
    )
    order = near_first(n_hi)[::-1]
    rounds = len(scatter.small_steps())
    for k, z in enumerate(order):
        for a in range(n):
            scatter.begin(z, a)
        if k == 0:
            scatter.small_begin()
    for k in range(max(len(order) + 2, rounds)):
        for a in range(n):
            if k < len(order):
                scatter.core(order[k], a)
        for a in range(n):
            if 0 <= k - 1 < len(order):
                scatter.one(order[k - 1], a)
        for a in range(n):
            if 0 <= k - 2 < len(order):
                scatter.two(order[k - 2], a)
        if k < rounds:
            scatter.small_next(k)
    for a in range(n):
        scatter.last(a)
    scatter.finish()


def scatter_sums(arrays, orders, small, collective_id):
    n = len(arrays)
    n_hi = lax.axis_size("dp") // 2
    shapes = [a.shape[1:] for a in arrays]
    rounds = 3 + (n_hi - 1).bit_length()
    dma = pltpu.SemaphoreType.DMA
    return pl.pallas_call(
        functools.partial(scatter_kernel, n_hi, orders),
        out_shape=[jax.ShapeDtypeStruct(shape, F32) for shape in shapes]
        + [jax.ShapeDtypeStruct(small.shape, F32)],
        in_specs=[ANYWHERE] * n + [IN_VMEM],
        out_specs=[IN_VMEM] * (n + 1),
        scratch_shapes=scatter_buffers(shapes, n_hi)
        + [pltpu.VMEM((2, rounds) + small.shape, F32)]
        + scatter_sems(n, n_hi)
        + [dma((rounds,)), dma((rounds,))],
        compiler_params=pltpu.CompilerParams(
            collective_id=collective_id, has_side_effects=True, vmem_limit_bytes=56 << 20
        ),
    )(*arrays, small)


def pick_scores(queries, table_ref, chosen):
    slots, step = table_ref.shape[1], 256
    low, high = chosen & 7, chosen >> 3
    picked = jnp.zeros(chosen.shape, F32)
    for at in range(0, slots, step):
        scores = dot(table_ref[0, pl.ds(at, step), pl.ds(0, HD)], queries, NT)
        for row in range(0, step, 8):
            got = jnp.take_along_axis(scores[row : row + 8], low, axis=0)
            picked = jnp.where(high == (at + row) // 8, got, picked)
    return picked * SCALE


def recall_values(scores, table_ref, chosen, lse_ref, p_ref):
    slots, tokens, step = table_ref.shape[1], chosen.shape[1], 256
    top = jnp.max(scores, axis=0, keepdims=True)
    weights = jnp.exp(scores - top)
    total = jnp.sum(weights, axis=0, keepdims=True)
    lse_ref[0] = top + jnp.log(total)
    times = jnp.ones_like(weights)
    for turn in range(1, 8):
        times = times + jnp.where(pltpu.roll(chosen, turn, 0) == chosen, 1.0, 0.0)
    probs = (weights / total * times).astype(BF)
    rows = lax.broadcasted_iota(jnp.int32, (step, tokens), 0).astype(F32).astype(BF)
    out = jnp.zeros((HD, tokens), F32)
    values_t = table_ref[0, :, pl.ds(HD, HD)].T
    for at in range(0, slots, step):
        mine = jnp.where(chosen // step == at // step, chosen % step, -1).astype(F32).astype(BF)
        dense = jnp.zeros((step, tokens), BF)
        for j in range(8):
            dense = jnp.where(rows == mine[j : j + 1], probs[j : j + 1], dense)
        p_ref[0, pl.ds(at, step), :] = dense
        out = out + dot(values_t[:, at : at + step], dense)
    return out.T.astype(BF)


def attend_kernel(n_hi, orders, *refs):
    n = len(orders) - 2
    x_ref, table_ref, slot_ref = refs[:3]
    early_in, late_in = refs[3:5], refs[5 : 5 + n]
    normed_ref, q_ref, norms_ref, out_ref, lse_ref, p_ref, full_q = refs[5 + n : 12 + n]
    late_out = refs[12 + n : 12 + 2 * n]
    wq, norms, asked, keep_sem, q_send, q_recv = refs[12 + 2 * n : 18 + 2 * n]
    sems = refs[18 + 2 * n :]
    phase, head = pl.program_id(0), pl.program_id(1)
    tick = phase * H + head
    place = Place(n_hi)
    early = Gather(place, orders[:2], early_in, (wq, norms), sems[:3])
    late = Gather(place, orders[2:], late_in, late_out, sems[3:])
    zs = near_first(n_hi)
    rows = x_ref.shape[0]

    def ask(src, slot, to):
        return pltpu.make_async_remote_copy(
            src_ref=src,
            dst_ref=asked.at[slot],
            send_sem=q_send.at[slot],
            recv_sem=q_recv.at[slot],
            device_id=place.device(to),
            device_id_type=MESH,
        )

    def keep():
        return pltpu.make_async_copy(wq, full_q, keep_sem)

    @pl.when(tick == 0)
    def _():
        place.greet()
        for a in range(2):
            early.begin(a)
        x = x_ref[...].astype(F32)
        center = x - jnp.mean(x, axis=-1, keepdims=True)
        scaled = center * lax.rsqrt(jnp.mean(center * center, axis=-1, keepdims=True) + EPSILON)
        for z in zs:
            for a in range(2):
                early.middle(a, z)
        for z in zs:
            for a in range(2):
                early.late(a, z)
        for a in range(2):
            early.finish(a)
        keep().start()
        share = norms.shape[0] // H
        lanes = [
            functools.reduce(jnp.add, [norms[g * share + k].astype(F32) for k in range(share)])
            for g in range(H)
        ]
        norm_rows = jnp.concatenate(lanes, axis=1)
        norms_ref[...] = norm_rows
        normed = (scaled * norm_rows[0:1] + norm_rows[2:3]).astype(BF)
        normed_ref[...] = normed
        for at in range(0, wq.shape[2], 256):
            weights = wq[:, :, pl.ds(at, 256)]
            if weights.shape[1] % 16:
                weights = weights.astype(F32)
            weights = weights.reshape(-1, 256).astype(BF)
            q_ref[:, pl.ds(at, 256)] = dot(normed, weights).astype(BF)
        ask(q_ref, 1, ALONG_CORE).start()
        ask(q_ref, 2, ALONG_X).start()
        for a in range(n):
            late.begin(a)
        asked[0] = q_ref[...]
        place.arrived(asked.at[1], q_recv.at[1])

    events = []
    for a in range(n + 1):
        for z in zs:
            if a < n:
                events.append(functools.partial(late.middle, a, z))
            if a > 0:
                events.append(functools.partial(late.late, a - 1, z))
    ticks = 2 * H

    def slot(at):
        count = 2 * ticks - 2
        mine = events[len(events) * (at - 2) // count : len(events) * (at - 1) // count]
        if at >= 2 and mine:

            @pl.when(tick == at // 2)
            def _():
                for event in mine:
                    event()

    for at in range(0, 2 * ticks, 2):
        slot(at)

    @pl.when(tick == H)
    def _():
        place.arrived(asked.at[3], q_recv.at[3])

    queries = asked[pl.ds(phase * 2, 2), :, pl.ds(pl.multiple_of(head * HD, HD), HD)]
    chosen = slot_ref[0]
    scores = pick_scores(queries.reshape(2 * rows, HD), table_ref, chosen)

    @pl.when(tick == H - 2)
    def _():
        place.arrived(asked.at[2], q_recv.at[2])
        ask(asked.at[2], 3, ALONG_CORE).start()

    for at in range(1, 2 * ticks, 2):
        slot(at)
    out_ref[...] = recall_values(scores, table_ref, chosen, lse_ref, p_ref)

    @pl.when(tick == ticks - 1)
    def _():
        for a in range(n):
            late.finish(a)
        ask(q_ref, 1, ALONG_CORE).wait_send()
        ask(q_ref, 2, ALONG_X).wait_send()
        ask(asked.at[2], 3, ALONG_CORE).wait_send()
        keep().wait()


def attend(x, table, chosen, early, late, orders, collective_id):
    n, n_hi = len(late), lax.axis_size("dp") // 2
    devices = n_hi * 8
    (rows, width), slots = x.shape, table.shape[1]
    whole = pl.BlockSpec((rows, width), lambda p, h: (0, 0))
    dma = pltpu.SemaphoreType.DMA

    def gathered(a):
        return jax.ShapeDtypeStruct((devices,) + a.shape, a.dtype)

    return pl.pallas_call(
        functools.partial(attend_kernel, n_hi, orders),
        grid=(2, H),
        in_specs=[
            whole,
            pl.BlockSpec((1, slots, 2 * HD), lambda p, h: (h, 0, 0)),
            pl.BlockSpec((1, 8, 2 * rows), lambda p, h: (h, 0, p)),
        ]
        + [ANYWHERE] * (2 + n),
        out_specs=[
            whole,
            whole,
            pl.BlockSpec((16, width), lambda p, h: (0, 0)),
            pl.BlockSpec((2 * rows, HD), lambda p, h: (p, h)),
            pl.BlockSpec((1, 1, 2 * rows), lambda p, h: (h, 0, p)),
            pl.BlockSpec((1, slots, 2 * rows), lambda p, h: (p * H + h, 0, 0)),
        ]
        + [ANYWHERE] * (1 + n),
        out_shape=[
            jax.ShapeDtypeStruct(x.shape, BF),
            jax.ShapeDtypeStruct(x.shape, BF),
            jax.ShapeDtypeStruct((16, width), F32),
            jax.ShapeDtypeStruct((4 * rows, width), BF),
            jax.ShapeDtypeStruct((H, 1, 4 * rows), F32),
            jax.ShapeDtypeStruct((2 * H, slots, 2 * rows), BF),
            gathered(early[0]),
        ]
        + [gathered(a) for a in late],
        scratch_shapes=[
            pltpu.VMEM((devices,) + early[0].shape, BF),
            pltpu.VMEM((devices,) + early[1].shape, BF),
            pltpu.VMEM((4, rows, width), BF),
            dma(()),
            dma((4,)),
            dma((4,)),
        ]
        + gather_sems(2, n_hi)
        + gather_sems(n, n_hi),
        compiler_params=pltpu.CompilerParams(
            collective_id=collective_id, has_side_effects=True, vmem_limit_bytes=52 << 20
        ),
        cost_estimate=pl.CostEstimate(
            flops=16 * rows * slots * HD * H, bytes_accessed=128 << 20, transcendentals=0
        ),
    )(x, table, chosen, *early, *late)


def recall_grad_kernel(ga_ref, gb_ref, mem_ref, p_ref, delta_ref, share_ref, outa_ref, outb_ref):
    slots, tokens = p_ref.shape[1], p_ref.shape[2]
    half = tokens // 2
    grads = jnp.concatenate([ga_ref[...], gb_ref[...]], axis=0)
    delta = delta_ref[0]
    keys_t = mem_ref[0, :, pl.ds(0, HD)].T
    step = 512
    out = jnp.zeros((HD, tokens), F32)
    for at in range(0, slots, step):
        along = dot(mem_ref[0, pl.ds(at, step), pl.ds(HD, HD)], grads, NT)
        scores = (along - delta).astype(BF) * p_ref[0, pl.ds(at, step), :]
        out = out + dot(keys_t[:, at : at + step], scores)
    out = (out * (share_ref[0] * SCALE)).T.astype(BF)
    outa_ref[...] = out[:half]
    outb_ref[...] = out[half:]


def head_columns(rows, first=0):
    return pl.BlockSpec((rows, HD), lambda h: (0, first + h))


def per_head(*shape):
    return pl.BlockSpec((1,) + shape, lambda h: (h,) + (0,) * len(shape))


def recall_grad(grad_a, grad_b, table, probs, first, delta, share):
    rows, slots = grad_a.shape[0], table.shape[1]
    return pl.pallas_call(
        recall_grad_kernel,
        grid=(H,),
        in_specs=[
            head_columns(rows),
            head_columns(rows),
            per_head(slots, 2 * HD),
            pl.BlockSpec((1, slots, 2 * rows), lambda h: (first + h, 0, 0)),
            per_head(1, 2 * rows),
            per_head(1, 2 * rows),
        ],
        out_specs=[head_columns(rows), head_columns(rows)],
        out_shape=[jax.ShapeDtypeStruct(grad_a.shape, BF)] * 2,
        compiler_params=pltpu.CompilerParams(vmem_limit_bytes=48 << 20),
        cost_estimate=pl.CostEstimate(
            flops=8 * rows * slots * HD * H, bytes_accessed=64 << 20, transcendentals=0
        ),
    )(grad_a, grad_b, table, probs, delta, share)


def near_buckets():
    distance = np.arange(NEAR)
    exact = BUCKETS // 2
    far = exact + np.floor(
        np.log(np.maximum(distance, 1) / exact) / np.log(128.0 / exact) * exact
    )
    return np.where(distance < exact, distance, np.minimum(far, BUCKETS - 1)).astype(np.int32)


def near_hot():
    return near_buckets()[:, None] == np.arange(BUCKETS)[None, :]


def near_bias(rel_table):
    above = (rel_table - rel_table[-1:])[None]
    rows = jnp.sum(jnp.where(jnp.asarray(near_hot())[:, :, None], above, 0.0), axis=1)
    return jnp.pad(rows.T, ((0, 0), (0, NEAR)))[:, None, :]


def table_gradient(diagonals, totals):
    near = diagonals[:, 0, NEAR - 1 : 2 * NEAR - 1]
    sums = jnp.dot(near, jnp.asarray(near_hot(), F32), precision=HIGHEST)
    far = jnp.sum(totals, axis=(1, 2)) - jnp.sum(near, axis=1)
    return (sums + far[:, None] * (np.arange(BUCKETS) == BUCKETS - 1)).T


def segment_kernel(len_ref, near_ref, q_ref, kc_ref, kn_ref, vc_ref, vn_ref, out_ref, p_ref):
    length = len_ref[0]
    band = pltpu.roll(
        jnp.broadcast_to(near_ref[0], (NEAR, 2 * NEAR)), 0, 1, stride=1, stride_axis=0
    )
    key_ids = lax.broadcasted_iota(jnp.int32, (NEAR, NEAR), 0)
    query_ids = lax.broadcasted_iota(jnp.int32, (NEAR, NEAR), 1)
    on_diagonal = jnp.where(query_ids >= key_ids, band[:, :NEAR], NEGATIVE)
    beside = band[:, NEAR:]
    masked = jnp.full((NEAR, NEAR), NEGATIVE, F32)
    zero = jnp.zeros((NEAR, NEAR), F32)
    cache_t, values_t = vc_ref[...].T, vn_ref[...].T
    step = 2 * NEAR
    for at in range(W // step):
        count = 2 * (at + 1)
        queries = q_ref[pl.ds(step * at, step), :]
        cached = dot(kc_ref[...], queries, NT) * SCALE
        if at == 0:
            last = cached[W - NEAR :] + jnp.concatenate([beside, zero], axis=1)
            cached = jnp.concatenate([cached[: W - NEAR], last], axis=0)
        fresh = dot(kn_ref[pl.ds(0, NEAR * count), :], queries, NT) * SCALE
        rows = [cached]
        for k in range(count):
            block = fresh[NEAR * k : NEAR * (k + 1)]
            tiles = [
                masked if q < k else on_diagonal if q == k else beside if q == k + 1 else zero
                for q in (2 * at, 2 * at + 1)
            ]
            if any(tile is not zero for tile in tiles):
                block = block + jnp.concatenate(tiles, axis=1)
            ids = lax.broadcasted_iota(jnp.int32, (NEAR, step), 0) + NEAR * k
            rows.append(jnp.where(ids < length, block, NEGATIVE))
        scores = jnp.concatenate(rows, axis=0)
        weights = jnp.exp(scores - jnp.max(scores, axis=0, keepdims=True))
        probs = (weights * (1.0 / jnp.sum(weights, axis=0, keepdims=True))).astype(BF)
        p_ref[0, pl.ds(0, W + NEAR * count), pl.ds(step * at, step)] = probs
        out = dot(cache_t, probs[:W]) + dot(values_t[:, : NEAR * count], probs[W:])
        out_ref[pl.ds(step * at, step), :] = out.T


def segment_grad_kernel(
    open_ref, g_ref, q_ref, kc_ref, kn_ref, vc_ref, vn_ref, p_ref, gq_ref, gk_ref, gv_ref, diag_ref, tot_ref
):
    closed = 1.0 - open_ref[pl.program_id(0)]
    cache_t, keys_t = kc_ref[...].T, kn_ref[...].T
    on_diagonal = jnp.zeros((NEAR, NEAR), F32)
    beside = jnp.zeros((NEAR, NEAR), F32)
    step = 2 * NEAR
    total = jnp.zeros((8, step), F32)
    grad_keys, grad_values = [], []
    for at in range(W // step):
        count = 2 * (at + 1)
        grads = (closed * g_ref[pl.ds(step * at, step), :]).astype(BF)
        queries = q_ref[pl.ds(step * at, step), :]
        grad_probs = jnp.concatenate(
            [dot(vc_ref[...], grads, NT), dot(vn_ref[pl.ds(0, NEAR * count), :], grads, NT)], axis=0
        )
        probs = p_ref[0, pl.ds(0, W + NEAR * count), pl.ds(step * at, step)]
        wide = probs.astype(F32)
        product = wide * grad_probs
        grad_scores = product - wide * jnp.sum(product, axis=0, keepdims=True)
        low = grad_scores.astype(BF)
        grad_q = dot(cache_t, low[:W]) + dot(keys_t[:, : NEAR * count], low[W:])
        gq_ref[pl.ds(step * at, step), :] = (grad_q * SCALE).T
        grad_keys.append(dot(low[W:], queries) * SCALE)
        grad_values.append(dot(probs[W:], grads))
        if at == 0:
            beside = beside + grad_scores[W - NEAR : W, :NEAR]
        for k in range(count):
            for side, q in enumerate((2 * at, 2 * at + 1)):
                tile = grad_scores[W + NEAR * k : W + NEAR * (k + 1), NEAR * side : NEAR * (side + 1)]
                if q == k:
                    on_diagonal = on_diagonal + tile
                elif q == k + 1:
                    beside = beside + tile
        total = total + jnp.sum(grad_scores.reshape(-1, 8, step), axis=0)
    for ref, (early, late) in ((gk_ref, grad_keys), (gv_ref, grad_values)):
        ref[...] = jnp.concatenate([late[:step] + early, late[step:]], axis=0).astype(BF)
    down = lax.broadcasted_iota(jnp.int32, (NEAR, NEAR), 0)
    across = lax.broadcasted_iota(jnp.int32, (NEAR, NEAR), 1)
    turned = lax.dot_general(
        (down + across == NEAR - 1).astype(F32),
        jnp.concatenate([on_diagonal, beside], axis=1),
        NN,
        precision=HIGHEST,
        preferred_element_type=F32,
    )
    diagonals = pltpu.roll(turned, 0, 1, stride=1, stride_axis=0)
    diag_ref[0] = jnp.sum(diagonals, axis=0, keepdims=True)
    tot_ref[0] = total


def segment_forward(queries, keys_values, cache, near, length):
    return pl.pallas_call(
        segment_kernel,
        grid=(H,),
        in_specs=[
            SCALARS,
            per_head(1, 2 * NEAR),
            head_columns(W),
            head_columns(W),
            head_columns(W),
            head_columns(W, H),
            head_columns(W, H),
        ],
        out_specs=[head_columns(W), per_head(2 * W, W)],
        out_shape=[
            jax.ShapeDtypeStruct((W, H * HD), F32),
            jax.ShapeDtypeStruct((H, 2 * W, W), BF),
        ],
        compiler_params=pltpu.CompilerParams(vmem_limit_bytes=32 << 20),
        cost_estimate=pl.CostEstimate(
            flops=8 * W * W * HD * H, bytes_accessed=20 << 20, transcendentals=0
        ),
    )(length, near, queries, cache, keys_values, cache, keys_values)


def segment_backward(gate_open, grad_mixed, queries, keys_values, cache, probs):
    return pl.pallas_call(
        segment_grad_kernel,
        grid=(H,),
        in_specs=[
            SCALARS,
            head_columns(W),
            head_columns(W),
            head_columns(W),
            head_columns(W),
            head_columns(W, H),
            head_columns(W, H),
            per_head(2 * W, W),
        ],
        out_specs=[
            head_columns(W),
            head_columns(W),
            head_columns(W),
            per_head(1, 2 * NEAR),
            per_head(8, 2 * NEAR),
        ],
        out_shape=[
            jax.ShapeDtypeStruct((W, H * HD), F32),
            jax.ShapeDtypeStruct((W, H * HD), BF),
            jax.ShapeDtypeStruct((W, H * HD), BF),
            jax.ShapeDtypeStruct((H, 1, 2 * NEAR), F32),
            jax.ShapeDtypeStruct((H, 8, 2 * NEAR), F32),
        ],
        compiler_params=pltpu.CompilerParams(vmem_limit_bytes=32 << 20),
        cost_estimate=pl.CostEstimate(
            flops=16 * W * W * HD * H, bytes_accessed=20 << 20, transcendentals=0
        ),
    )(gate_open, grad_mixed, queries, cache, keys_values, cache, keys_values, probs)


def norm_forward(values, gain_row, shift_row):
    center = values - jnp.mean(values, axis=-1, keepdims=True)
    inverse = lax.rsqrt(jnp.mean(center * center, axis=-1, keepdims=True) + EPSILON)
    scaled = center * inverse
    return (scaled * gain_row + shift_row, scaled, inverse)


def norm_backward(grad_normed, scaled, inverse, gain_row):
    grad_scaled = grad_normed * gain_row
    mean_grad = jnp.mean(grad_scaled, axis=-1, keepdims=True)
    mean_cross = jnp.mean(grad_scaled * scaled, axis=-1, keepdims=True)
    return inverse * (grad_scaled - mean_grad - scaled * mean_cross)


def swap(value, turn):
    return jax.tree.map(
        lambda v: lax.ppermute(v, "mem", [(i, i ^ turn) for i in range(lax.axis_size("mem"))]), value
    )


def combine(outs, lses):
    total = jax.nn.logsumexp(jnp.stack(lses), axis=0)
    rows = outs[0].shape[0]
    result = 0.0
    for out, lse in zip(outs, lses):
        share = jnp.exp(lse - total).T[:, :, None]
        result = result + share * out.reshape(rows, H, HD).astype(F32)
    return result.reshape(rows, H * HD), total


def local(
    tokens,
    norm_gains,
    norm_shifts,
    w_qkv,
    w_out,
    w_up,
    w_down,
    rel_table,
    gate_bias,
    xl_cache,
    memory,
    slot_index,
    seg_len,
    cotangent,
):
    width = tokens.shape[1]
    count = tokens.shape[0]
    slot_count = memory.shape[0]
    groups = lax.axis_size("mem")
    me = lax.axis_index("mem")

    devices = lax.axis_size("dp") * groups
    number = lax.axis_index("dp") * groups + me
    own = norm_gains.shape[1]
    norms = jnp.pad(
        jnp.concatenate([norm_gains, norm_shifts], axis=0), ((0, 12), (0, 128 - own))
    )
    norms = jnp.roll(norms, number % (128 // own) * own, axis=1)
    table = memory.transpose(1, 0, 2)
    slot_rows = (slot_index - me * slot_count).reshape(groups, count, H, -1)
    picks = [
        lax.dynamic_index_in_dim(slot_rows, me ^ turn, 0, keepdims=False) for turn in range(groups)
    ]
    chosen = jnp.stack(picks).transpose(2, 3, 0, 1).reshape(H, -1, groups * count)
    normed_one, queries, norm_rows, out_all, lse_all, probs_all, *full = attend(
        tokens,
        table,
        chosen,
        (w_qkv[:, :width], norms),
        (w_qkv[:, width:], w_out, w_up, w_down),
        ("zyx", "zxy", "zxy", "zyx", "zyx", "zxy"),
        0,
    )
    full_q, full_kv, full_out, full_up, full_down = [f.reshape(-1, f.shape[2]) for f in full]
    gain_rows, shift_rows = norm_rows[:2], norm_rows[2:4]
    out_own, out_core, out_x, out_cross = jnp.split(out_all, groups)
    lse_chip, lse_far = lse_all[:, 0, : 2 * count], lse_all[:, 0, 2 * count :]

    inputs = tokens.astype(F32)
    _, scaled_one, inverse_one = norm_forward(inputs, gain_rows[0], shift_rows[0])
    keys_values = dot(normed_one, full_kv).astype(BF)
    local_out, probs_local = segment_forward(
        queries, keys_values, xl_cache, near_bias(rel_table), seg_len
    )

    own_lse, own_out = lse_chip[:, :count], out_own
    core_out, core_lse = swap((out_core, lse_chip[:, count:]), 1)
    other_out, other_lse = swap((out_cross, lse_far[:, count:]), 1)
    pair_out, pair_lse = combine((out_x, other_out), (lse_far[:, :count], other_lse))
    far_out, far_lse = swap((pair_out.astype(BF), pair_lse), 2)
    recalled, total_lse = combine((own_out, core_out, far_out), (own_lse, core_lse, far_lse))

    gate_open = jax.nn.sigmoid(gate_bias)
    gate_row = jnp.repeat(gate_open, HD)[None]
    mixed_low = (gate_row * recalled + (1.0 - gate_row) * local_out).astype(BF)
    attended = inputs + dot(mixed_low, full_out)
    normed_two, scaled_two, inverse_two = norm_forward(attended, gain_rows[1], shift_rows[1])
    normed_two = normed_two.astype(BF)
    up_pre = dot(normed_two, full_up)
    hidden = jax.nn.gelu(up_pre).astype(BF)
    output = attended + dot(hidden, full_down)

    grad_output = cotangent.astype(F32)
    grad_down = jnp.einsum("tf,td->fd", hidden, cotangent, preferred_element_type=F32)
    grad_hidden = dot(cotangent, full_down, NT)
    grad_up_pre = jax.vjp(jax.nn.gelu, up_pre)[1](grad_hidden)[0].astype(BF)
    grad_up = jnp.einsum("td,tf->df", normed_two, grad_up_pre, preferred_element_type=F32)
    grad_normed_two = dot(grad_up_pre, full_up, NT)
    grad_attended = grad_output + norm_backward(
        grad_normed_two, scaled_two, inverse_two, gain_rows[1]
    )
    attended_low = grad_attended.astype(BF)
    grad_wout = jnp.einsum("td,te->de", mixed_low, attended_low, preferred_element_type=F32)
    grad_mixed = dot(attended_low, full_out, NT)
    grad_gate = (
        jnp.sum((grad_mixed * (recalled - local_out)).reshape(count, H, HD), axis=(0, 2))
        * gate_open
        * (1.0 - gate_open)
    )
    grad_recalled = (gate_row * grad_mixed).astype(BF)
    delta = jnp.sum(
        (grad_recalled.astype(F32) * recalled).reshape(count, H, HD), axis=-1
    ).T
    sent = (grad_recalled, jnp.concatenate([delta, total_lse], axis=0))
    sent_core, sent_x = swap(sent, 1), swap(sent, 2)
    sent_cross = swap(sent_x, 1)

    grad_query_local, grad_keys, grad_values, diagonals, totals = segment_backward(
        gate_open, grad_mixed, queries, keys_values, xl_cache, probs_local
    )
    grad_table = table_gradient(diagonals, totals)

    def recall_back(left, right, lse, first):
        delta_rows = jnp.concatenate([left[1][:H], right[1][:H]], axis=1)
        total_rows = jnp.concatenate([left[1][H:], right[1][H:]], axis=1)
        return recall_grad(
            left[0],
            right[0],
            table,
            probs_all,
            first,
            delta_rows[:, None],
            jnp.exp(lse - total_rows)[:, None],
        )

    back_x, back_cross = recall_back(sent_x, sent_cross, lse_far, H)
    back_own, back_core = recall_back(sent, sent_core, lse_chip, 0)
    pair_back = (back_x.astype(F32) + swap(back_cross, 1).astype(F32)).astype(BF)
    grad_query = (
        grad_query_local
        + back_own.astype(F32)
        + swap(back_core, 1).astype(F32)
        + swap(pair_back, 2).astype(F32)
    )
    grad_qkv_low = jnp.concatenate([grad_query.astype(BF), grad_keys, grad_values], axis=1)
    grad_wqkv = jnp.einsum("td,te->de", normed_one, grad_qkv_low, preferred_element_type=F32)
    grad_normed_one = dot(grad_qkv_low[:, :width], full_q, NT) + dot(
        grad_qkv_low[:, width:], full_kv, NT
    )
    grad_tokens = grad_attended + norm_backward(
        grad_normed_one, scaled_one, inverse_one, gain_rows[0]
    )
    grad_norms = jnp.stack(
        [
            jnp.sum(grad_normed_one * scaled_one, axis=0),
            jnp.sum(grad_normed_two * scaled_two, axis=0),
            jnp.sum(grad_normed_one, axis=0),
            jnp.sum(grad_normed_two, axis=0),
        ]
    )
    rest = jnp.pad(jnp.concatenate([grad_table.reshape(-1), grad_gate]), (0, 1024 - 264))
    small = jnp.concatenate([grad_norms.reshape(-1, 128), rest.reshape(-1, 128)], axis=0)
    share_qkv, share_out, share_up, share_down, small = scatter_sums(
        [
            g.astype(BF).reshape(devices, -1, g.shape[1])
            for g in (grad_wqkv, grad_wout, grad_up, grad_down)
        ],
        ("yxz", "xyz", "xyz", "yxz"),
        small,
        2,
    )
    share_norms = lax.dynamic_slice_in_dim(
        small[:32].reshape(4, width), number * own, own, axis=1
    )
    rest = small[32:].reshape(-1)
    table_total, gate_total = rest[: BUCKETS * H].reshape(BUCKETS, H), rest[BUCKETS * H :][:H]
    return (
        output.astype(BF),
        grad_tokens,
        share_norms[:2],
        share_norms[2:],
        share_qkv,
        share_out,
        share_up,
        share_down,
        table_total,
        gate_total,
    )


def solution(mesh):
    shard = P(AXES, None)
    placed = (
        shard,
        P(None, AXES),
        P(None, AXES),
        shard,
        shard,
        shard,
        shard,
        P(),
        P(),
        shard,
        P(AXES, None, None),
        P("dp", None, "mem"),
        P(AXES),
        shard,
    )
    return jax.shard_map(
        local,
        mesh=mesh,
        in_specs=placed,
        out_specs=(
            shard,
            shard,
            P(None, AXES),
            P(None, AXES),
            shard,
            shard,
            shard,
            shard,
            P(),
            P(),
        ),
        check_vma=False,
    )
```

```python
import functools

import jax
import jax.numpy as jnp
import numpy as np
from jax import lax
from jax.experimental import pallas as pl
from jax.experimental.pallas import tpu as pltpu
from jax.sharding import PartitionSpec as P

H = 8
HD = 128
W = 512
BUCKETS = 32
NEAR = 128
EPSILON = 1e-05
NEGATIVE = -1e30
SCALE = HD ** (-0.5)
AXES = ("dp", "mem")
MESH = pl.DeviceIdType.MESH
HIGHEST = lax.Precision.HIGHEST
BF = jnp.bfloat16
F32 = jnp.float32
NT = (((1,), (1,)), ((), ()))
NN = (((1,), (0,)), ((), ()))


def dot(left, right, dims=NN):
    return lax.dot_general(left, right, dims, preferred_element_type=F32)


OWN, ALONG_Y, ALONG_X, ALONG_CORE = (0, 0, 0, 0), (0, 1, 0, 0), (0, 0, 1, 0), (0, 0, 0, 1)
ANYWHERE = pl.BlockSpec(memory_space=pl.ANY)
IN_VMEM = pl.BlockSpec(memory_space=pltpu.VMEM)
SCALARS = pl.BlockSpec(memory_space=pltpu.SMEM)


class Place:
    def __init__(self, n_hi):
        self.sizes = (n_hi, 2, 2, 2)
        dp, mem = lax.axis_index("dp"), lax.axis_index("mem")
        self.at = (dp // 2, dp % 2, mem // 2, mem % 2)

    def device(self, step):
        z, y, x, core = [(a + s) % n for a, s, n in zip(self.at, step, self.sizes)]
        return (z * 2 + y, x * 2 + core)

    def number(self, step):
        dp, mem = self.device(step)
        return dp * 4 + mem

    def plus(self, left, right):
        return tuple((a + b) % n for a, b, n in zip(left, right, self.sizes))

    def minus(self, left, right):
        return tuple((a - b) % n for a, b, n in zip(left, right, self.sizes))

    def partners(self):
        return [(z, 0, 0, 0) for z in range(1, self.sizes[0])] + [ALONG_Y, ALONG_X, ALONG_CORE]

    def greet(self):
        barrier = pltpu.get_barrier_semaphore()
        for partner in self.partners():
            pl.semaphore_signal(
                barrier, inc=1, device_id=self.device(partner), device_id_type=MESH
            )
        pl.semaphore_wait(barrier, len(self.partners()))

    def arrived(self, ref, recv):
        pltpu.make_async_remote_copy(
            src_ref=ref,
            dst_ref=ref,
            send_sem=recv,
            recv_sem=recv,
            device_id=self.device(ALONG_CORE),
            device_id_type=MESH,
        ).wait_recv()


def near_first(n_hi):
    order = [0]
    for z in range(1, n_hi // 2 + 1):
        order += [k for k in dict.fromkeys((z, n_hi - z)) if k < n_hi]
    return order


class Gather:
    LEFT, RIGHT, Y, X, CORE = "left", "right", ALONG_Y, ALONG_X, ALONG_CORE

    def __init__(self, place, orders, ins, outs, sems):
        self.place, self.ins, self.outs = place, ins, outs
        self.send_sem, self.recv_sem, self.own_sem = sems
        self.n = len(orders)
        self.orders = [["zyx".index(axis) for axis in order] for order in orders]
        self.sent = [[] for _ in orders]

    def exists(self, steps):
        z, n = self.place.at[0], self.place.sizes[0]
        return z + steps >= 0 if steps < 0 else z + steps < n

    def device(self, to):
        z, y, x, core = self.place.at
        if to in (self.LEFT, self.RIGHT):
            return ((z + (1 if to == self.RIGHT else -1)) * 2 + y, x * 2 + core)
        return self.place.device(to)

    def spot(self, a, source):
        z, y, x, core = self.place.at
        dp = (z + source[0]) * 2 + (y + source[1]) % 2
        return self.outs[a].at[dp * 4 + (x + source[2]) % 2 * 2 + (core + source[3]) % 2]

    def recv(self, a, source, to=None):
        z = self.place.at[0] + source[0]
        rest = list(source[1:])
        if to is not None and to not in (self.LEFT, self.RIGHT):
            rest = [(have - step) % 2 for have, step in zip(rest, to[1:])]
        return self.recv_sem.at[a, ((z * 2 + rest[0]) * 2 + rest[1]) * 2 + rest[2]]

    def copy(self, a, k):
        source, to = self.sent[a][k]
        return pltpu.make_async_remote_copy(
            src_ref=self.ins[a] if source == OWN else self.spot(a, source),
            dst_ref=self.spot(a, source),
            send_sem=self.send_sem.at[a, k],
            recv_sem=self.recv(a, source, to),
            device_id=self.device(to),
            device_id_type=MESH,
        )

    def when(self, conditions, run):
        conditions = [c for c in conditions if c is not None]
        if conditions:
            pl.when(functools.reduce(jnp.logical_and, conditions))(run)
        else:
            run()

    def limits(self, source, to):
        ends = {self.LEFT: -1, self.RIGHT: 1}
        return [
            self.exists(source[0]) if source[0] else None,
            self.exists(ends[to]) if to in ends else None,
        ]

    def send(self, a, source, to):
        self.sent[a].append((source, to))
        k = len(self.sent[a]) - 1
        self.when(self.limits(source, to)[1:], lambda: self.copy(a, k).start())

    def own(self, a):
        return pltpu.make_async_copy(self.ins[a], self.spot(a, OWN), self.own_sem.at[a])

    def arrived(self, a, source):
        self.place.arrived(self.spot(a, source), self.recv(a, source))

    def onward(self, a, source):
        order = self.orders[a]
        came = max([order.index(axis) for axis in range(3) if source[axis]], default=-1)
        to = []
        if came >= 0 and order[came] == 0:
            to.append(self.RIGHT if source[0] < 0 else self.LEFT)
        for axis in order[came + 1 :]:
            to += ((self.LEFT, self.RIGHT), (self.Y,), (self.X,))[axis]
        return to + [self.CORE]

    def begin(self, a):
        for to in self.onward(a, OWN):
            self.send(a, OWN, to)
        self.own(a).start()

    def level(self, a, hops):
        for rest in ((0, 0), (1, 0), (0, 1), (1, 1)):
            distance = hops - sum(rest)
            if not 0 <= distance < self.place.sizes[0]:
                continue
            for steps in dict.fromkeys((-distance, distance)):

                def run(source=(steps,) + rest + (0,)):
                    self.arrived(a, source)
                    for to in self.onward(a, source):
                        self.send(a, source, to)

                self.when([self.exists(steps) if steps else None], run)

    def levels(self):
        return range(1, self.place.sizes[0] + 2)

    def finish(self, a):
        place = self.place
        for z in range(place.sizes[0]):
            for y in range(2):
                for x in range(2):
                    source = (z - place.at[0], y, x, 1)
                    place.arrived(self.spot(a, source), self.recv(a, source))
        for k in range(len(self.sent[a])):
            self.when(self.limits(*self.sent[a][k]), lambda k=k: self.copy(a, k).wait_send())
        self.own(a).wait()


def gather_sems(n, n_hi):
    sends = 5 + (8 * n_hi - 5) * 4
    dma = pltpu.SemaphoreType.DMA
    return [dma((n, sends)), dma((n, n_hi * 8)), dma((n,))]


def piece_width(columns):
    return next(w for w in (1024, 768, 512, 384, 256, 128) if columns % w == 0)


class Scatter:
    def __init__(self, place, orders, ins, outs, buffers, sems, small=None):
        self.place, self.ins, self.outs = place, ins, outs
        self.accs, self.from_core, self.from_first, self.from_second, self.from_z = buffers
        (
            self.load_sem,
            self.core_send,
            self.core_recv,
            self.first_send,
            self.first_recv,
            self.second_send,
            self.second_recv,
            self.z_send,
            self.z_recv,
        ) = sems[:9]
        self.small = small
        self.small_sems = sems[9:]
        self.n = len(orders)
        self.n_hi = place.sizes[0]
        self.first = [ALONG_X if order == "xyz" else ALONG_Y for order in orders]
        self.second = [ALONG_Y if order == "xyz" else ALONG_X for order in orders]
        self.started = []

    def step(self, a, z, two, one):
        y, x = (two, one) if self.second[a] == ALONG_Y else (one, two)
        return (z, y, x, 0)

    def send(self, ends, device):
        def build():
            src, dst, send, recv = ends()
            return pltpu.make_async_remote_copy(
                src_ref=src,
                dst_ref=dst,
                send_sem=send,
                recv_sem=recv,
                device_id=device(),
                device_id_type=MESH,
            )

        build().start()
        self.started.append(build)

    def load(self, a, z, two, one):
        s = (z * 2 + two) * 2 + one
        return pltpu.make_async_copy(
            self.ins[a].at[self.place.number(self.step(a, z, two, one))],
            self.accs[a].at[s],
            self.load_sem.at[a, s],
        )

    def begin(self, z, a):
        for two, one in ((1, 1), (0, 1), (1, 0), (0, 0)):
            s = (z * 2 + two) * 2 + one
            step = self.step(a, z, two, one)[:3] + (1,)
            self.send(
                lambda s=s, step=step: (
                    self.ins[a].at[self.place.number(step)],
                    self.from_core[a].at[s],
                    self.core_send.at[a, s],
                    self.core_recv.at[a, s],
                ),
                lambda: self.place.device(ALONG_CORE),
            )
            self.load(a, z, two, one).start()

    def add(self, acc, got):
        width = piece_width(acc.shape[1])

        def piece(k, carry):
            at = pl.ds(pl.multiple_of(k * width, width), width)
            acc[:, at] = (acc[:, at].astype(F32) + got[:, at].astype(F32)).astype(BF)
            return carry

        lax.fori_loop(0, acc.shape[1] // width, piece, 0)

    def core(self, z, a):
        for two, one in ((1, 1), (0, 1), (1, 0), (0, 0)):
            k = z * 2 + two
            s = k * 2 + one
            self.load(a, z, two, one).wait()
            self.place.arrived(self.from_core[a].at[s], self.core_recv.at[a, s])
            self.add(self.accs[a].at[s], self.from_core[a].at[s])
            if one:
                self.send(
                    lambda s=s, k=k: (
                        self.accs[a].at[s],
                        self.from_first[a].at[k],
                        self.first_send.at[a, k],
                        self.first_recv.at[a, k],
                    ),
                    lambda: self.place.device(self.first[a]),
                )

    def one(self, z, a):
        for two in (1, 0):
            k = z * 2 + two
            acc = self.accs[a].at[k * 2]
            self.place.arrived(self.from_first[a].at[k], self.first_recv.at[a, k])
            self.add(acc, self.from_first[a].at[k])
            if two:
                self.send(
                    lambda k=k: (
                        self.accs[a].at[k * 2],
                        self.from_second[a].at[z],
                        self.second_send.at[a, z],
                        self.second_recv.at[a, z],
                    ),
                    lambda: self.place.device(self.second[a]),
                )

    def two(self, z, a):
        acc = self.accs[a].at[z * 4]
        self.place.arrived(self.from_second[a].at[z], self.second_recv.at[a, z])
        self.add(acc, self.from_second[a].at[z])
        if z:
            self.send(
                lambda: (
                    self.accs[a].at[z * 4],
                    self.from_z[a].at[z - 1],
                    self.z_send.at[a, z - 1],
                    self.z_recv.at[a, z - 1],
                ),
                lambda: self.place.device((z, 0, 0, 0)),
            )

    def last(self, a):
        for z in range(1, self.n_hi):
            self.place.arrived(self.from_z[a].at[z - 1], self.z_recv.at[a, z - 1])
        out, acc, got = self.outs[a], self.accs[a].at[0], self.from_z[a]
        width = piece_width(out.shape[1])

        def piece(k, carry):
            at = pl.ds(pl.multiple_of(k * width, width), width)
            total = acc[:, at].astype(F32)
            for z in range(1, self.n_hi):
                total = total + got[z - 1, :, at].astype(F32)
            out[:, at] = total
            return carry

        lax.fori_loop(0, out.shape[1] // width, piece, 0)

    def small_steps(self):
        return [ALONG_CORE, ALONG_X, ALONG_Y] + [1 << k for k in range((self.n_hi - 1).bit_length())]

    def small_begin(self):
        source, total, _ = self.small
        total[...] = source[...]
        self.small_send(0)

    def small_device(self, k):
        step = self.small_steps()[k]
        z, y, x, core = self.place.at
        if isinstance(step, int):
            return ((z + step - 2 * step * ((z // step) % 2)) * 2 + y, x * 2 + core)
        return self.place.device(step)

    def small_send(self, k):
        _, total, buffer = self.small
        buffer[0, k] = total[...]
        send, recv = self.small_sems
        self.send(
            lambda: (buffer.at[0, k], buffer.at[1, k], send.at[k], recv.at[k]),
            lambda: self.small_device(k),
        )

    def small_next(self, k):
        _, total, buffer = self.small
        self.place.arrived(buffer.at[1, k], self.small_sems[1].at[k])
        total[...] = total[...] + buffer[1, k]
        if k + 1 < len(self.small_steps()):
            self.small_send(k + 1)

    def finish(self):
        for build in self.started:
            build().wait_send()


def scatter_buffers(shapes, n_hi):
    counts = (n_hi * 4, n_hi * 4, n_hi * 2, n_hi, n_hi - 1)
    return [pltpu.VMEM((count,) + shape, BF) for count in counts for shape in shapes]


def scatter_sems(n, n_hi):
    counts = (n_hi * 4,) * 3 + (n_hi * 2,) * 2 + (n_hi,) * 2 + (n_hi - 1,) * 2
    return [pltpu.SemaphoreType.DMA((n, count)) for count in counts]


def scatter_kernel(n_hi, orders, *refs):
    n = len(orders)
    ins, small_in, outs, small_out = refs[:n], refs[n], refs[n + 1 : 2 * n + 1], refs[2 * n + 1]
    rest = refs[2 * n + 2 :]
    buffers = [rest[k * n : (k + 1) * n] for k in range(5)]
    place = Place(n_hi)
    place.greet()
    scatter = Scatter(
        place, orders, ins, outs, buffers, rest[5 * n + 1 :], (small_in, small_out, rest[5 * n])
    )
    order = near_first(n_hi)[::-1]
    rounds = len(scatter.small_steps())
    for k, z in enumerate(order):
        for a in range(n):
            scatter.begin(z, a)
        if k == 0:
            scatter.small_begin()
    for k in range(max(len(order) + 2, rounds)):
        for a in range(n):
            if k < len(order):
                scatter.core(order[k], a)
        for a in range(n):
            if 0 <= k - 1 < len(order):
                scatter.one(order[k - 1], a)
        for a in range(n):
            if 0 <= k - 2 < len(order):
                scatter.two(order[k - 2], a)
        if k < rounds:
            scatter.small_next(k)
    for a in range(n):
        scatter.last(a)
    scatter.finish()


def scatter_sums(arrays, orders, small, collective_id):
    n = len(arrays)
    n_hi = lax.axis_size("dp") // 2
    shapes = [a.shape[1:] for a in arrays]
    rounds = 3 + (n_hi - 1).bit_length()
    dma = pltpu.SemaphoreType.DMA
    return pl.pallas_call(
        functools.partial(scatter_kernel, n_hi, orders),
        out_shape=[jax.ShapeDtypeStruct(shape, F32) for shape in shapes]
        + [jax.ShapeDtypeStruct(small.shape, F32)],
        in_specs=[ANYWHERE] * n + [IN_VMEM],
        out_specs=[IN_VMEM] * (n + 1),
        scratch_shapes=scatter_buffers(shapes, n_hi)
        + [pltpu.VMEM((2, rounds) + small.shape, F32)]
        + scatter_sems(n, n_hi)
        + [dma((rounds,)), dma((rounds,))],
        compiler_params=pltpu.CompilerParams(
            collective_id=collective_id, has_side_effects=True, vmem_limit_bytes=56 << 20
        ),
    )(*arrays, small)


FIRST_STOP, LAST_STOP = 2, 62
AHEAD = 0


def pick_scores(queries, table_ref, chosen, pause):
    slots, step = table_ref.shape[1], 256
    low, high = chosen & 7, chosen >> 3
    picked = jnp.zeros(chosen.shape, F32)
    for at in range(0, slots, step):
        scores = dot(table_ref[0, pl.ds(at, step), pl.ds(0, HD)], queries, NT)
        for row in range(0, step, 8):
            got = jnp.take_along_axis(scores[row : row + 8], low, axis=0)
            picked = jnp.where(high == (at + row) // 8, got, picked)
        if at + step == slots // 2:
            pause()
    return picked * SCALE


def recall_values(scores, table_ref, chosen, lse_ref, p_ref, pause):
    slots, tokens, step = table_ref.shape[1], chosen.shape[1], 256
    top = jnp.max(scores, axis=0, keepdims=True)
    weights = jnp.exp(scores - top)
    total = jnp.sum(weights, axis=0, keepdims=True)
    lse_ref[0] = top + jnp.log(total)
    times = jnp.ones_like(weights)
    for turn in range(1, 8):
        times = times + jnp.where(pltpu.roll(chosen, turn, 0) == chosen, 1.0, 0.0)
    probs = (weights / total * times).astype(BF)
    rows = lax.broadcasted_iota(jnp.int32, (step, tokens), 0).astype(F32).astype(BF)
    out = jnp.zeros((HD, tokens), F32)
    values_t = table_ref[0, :, pl.ds(HD, HD)].T
    for at in range(0, slots, step):
        mine = jnp.where(chosen // step == at // step, chosen % step, -1).astype(F32).astype(BF)
        dense = jnp.zeros((step, tokens), BF)
        for j in range(8):
            dense = jnp.where(rows == mine[j : j + 1], probs[j : j + 1], dense)
        p_ref[0, pl.ds(at, step), :] = dense
        out = out + dot(values_t[:, at : at + step], dense)
        if at + step == slots // 2:
            pause()
    return out.T.astype(BF)


def attend_kernel(n_hi, orders, *refs):
    n = len(orders) - 2
    x_ref, table_ref, slot_ref = refs[:3]
    early_in, late_in = refs[3:5], refs[5 : 5 + n]
    normed_ref, q_ref, norms_ref, out_ref, lse_ref, p_ref, full_q = refs[5 + n : 12 + n]
    late_out = refs[12 + n : 12 + 2 * n]
    wq, norms, asked, keep_sem, q_send, q_recv = refs[12 + 2 * n : 18 + 2 * n]
    sems = refs[18 + 2 * n :]
    phase, head = pl.program_id(0), pl.program_id(1)
    tick = phase * H + head
    place = Place(n_hi)
    early = Gather(place, orders[:2], early_in, (wq, norms), sems[:3])
    late = Gather(place, orders[2:], late_in, late_out, sems[3:])
    rows = x_ref.shape[0]

    def ask(src, slot, to):
        return pltpu.make_async_remote_copy(
            src_ref=src,
            dst_ref=asked.at[slot],
            send_sem=q_send.at[slot],
            recv_sem=q_recv.at[slot],
            device_id=place.device(to),
            device_id_type=MESH,
        )

    def keep():
        return pltpu.make_async_copy(wq, full_q, keep_sem)

    @pl.when(tick == 0)
    def _():
        place.greet()
        for a in range(2):
            early.begin(a)
        for a in range(AHEAD):
            late.begin(a)
        x = x_ref[...].astype(F32)
        center = x - jnp.mean(x, axis=-1, keepdims=True)
        scaled = center * lax.rsqrt(jnp.mean(center * center, axis=-1, keepdims=True) + EPSILON)
        for hops in early.levels():
            for a in range(2):
                early.level(a, hops)
        for a in range(2):
            early.finish(a)
        keep().start()
        share = norms.shape[0] // H
        lanes = [
            functools.reduce(jnp.add, [norms[g * share + k].astype(F32) for k in range(share)])
            for g in range(H)
        ]
        norm_rows = jnp.concatenate(lanes, axis=1)
        norms_ref[...] = norm_rows
        normed = (scaled * norm_rows[0:1] + norm_rows[2:3]).astype(BF)
        normed_ref[...] = normed
        for at in range(0, wq.shape[2], 256):
            weights = wq[:, :, pl.ds(at, 256)]
            if weights.shape[1] % 16:
                weights = weights.astype(F32)
            weights = weights.reshape(-1, 256).astype(BF)
            q_ref[:, pl.ds(at, 256)] = dot(normed, weights).astype(BF)
        ask(q_ref, 1, ALONG_CORE).start()
        ask(q_ref, 2, ALONG_X).start()
        for a in range(AHEAD, n):
            late.begin(a)
        asked[0] = q_ref[...]
        place.arrived(asked.at[1], q_recv.at[1])

    events = [
        functools.partial(late.level, a, hops) for hops in late.levels() for a in range(n)
    ]
    ticks = 2 * H
    stops = 4 * ticks
    stop_of = [FIRST_STOP + k * (LAST_STOP - FIRST_STOP) // len(events) for k in range(len(events))]

    def pause(part):
        for at in range(part, stops, 4):
            mine = [event for event, stop in zip(events, stop_of) if stop == at]
            if mine:

                @pl.when(tick == at // 4)
                def _():
                    for event in mine:
                        event()

    pause(0)

    @pl.when(tick == H)
    def _():
        place.arrived(asked.at[3], q_recv.at[3])

    queries = asked[pl.ds(phase * 2, 2), :, pl.ds(pl.multiple_of(head * HD, HD), HD)]
    chosen = slot_ref[0]
    scores = pick_scores(queries.reshape(2 * rows, HD), table_ref, chosen, lambda: pause(1))

    @pl.when(tick == H - 2)
    def _():
        place.arrived(asked.at[2], q_recv.at[2])
        ask(asked.at[2], 3, ALONG_CORE).start()

    pause(2)
    out_ref[...] = recall_values(scores, table_ref, chosen, lse_ref, p_ref, lambda: pause(3))

    @pl.when(tick == ticks - 1)
    def _():
        for a in range(n):
            late.finish(a)
        ask(q_ref, 1, ALONG_CORE).wait_send()
        ask(q_ref, 2, ALONG_X).wait_send()
        ask(asked.at[2], 3, ALONG_CORE).wait_send()
        keep().wait()


def attend(x, table, chosen, early, late, orders, collective_id):
    n, n_hi = len(late), lax.axis_size("dp") // 2
    devices = n_hi * 8
    (rows, width), slots = x.shape, table.shape[1]
    whole = pl.BlockSpec((rows, width), lambda p, h: (0, 0))
    dma = pltpu.SemaphoreType.DMA

    def gathered(a):
        return jax.ShapeDtypeStruct((devices,) + a.shape, a.dtype)

    return pl.pallas_call(
        functools.partial(attend_kernel, n_hi, orders),
        grid=(2, H),
        in_specs=[
            whole,
            pl.BlockSpec((1, slots, 2 * HD), lambda p, h: (h, 0, 0)),
            pl.BlockSpec((1, 8, 2 * rows), lambda p, h: (h, 0, p)),
        ]
        + [ANYWHERE] * (2 + n),
        out_specs=[
            whole,
            whole,
            pl.BlockSpec((16, width), lambda p, h: (0, 0)),
            pl.BlockSpec((2 * rows, HD), lambda p, h: (p, h)),
            pl.BlockSpec((1, 1, 2 * rows), lambda p, h: (h, 0, p)),
            pl.BlockSpec((1, slots, 2 * rows), lambda p, h: (p * H + h, 0, 0)),
        ]
        + [ANYWHERE] * (1 + n),
        out_shape=[
            jax.ShapeDtypeStruct(x.shape, BF),
            jax.ShapeDtypeStruct(x.shape, BF),
            jax.ShapeDtypeStruct((16, width), F32),
            jax.ShapeDtypeStruct((4 * rows, width), BF),
            jax.ShapeDtypeStruct((H, 1, 4 * rows), F32),
            jax.ShapeDtypeStruct((2 * H, slots, 2 * rows), BF),
            gathered(early[0]),
        ]
        + [gathered(a) for a in late],
        scratch_shapes=[
            pltpu.VMEM((devices,) + early[0].shape, BF),
            pltpu.VMEM((devices,) + early[1].shape, BF),
            pltpu.VMEM((4, rows, width), BF),
            dma(()),
            dma((4,)),
            dma((4,)),
        ]
        + gather_sems(2, n_hi)
        + gather_sems(n, n_hi),
        compiler_params=pltpu.CompilerParams(
            collective_id=collective_id, has_side_effects=True, vmem_limit_bytes=52 << 20
        ),
        cost_estimate=pl.CostEstimate(
            flops=16 * rows * slots * HD * H, bytes_accessed=128 << 20, transcendentals=0
        ),
    )(x, table, chosen, *early, *late)


def head_columns(rows, first=0):
    return pl.BlockSpec((rows, HD), lambda h: (0, first + h))


def per_head(*shape):
    return pl.BlockSpec((1,) + shape, lambda h: (h,) + (0,) * len(shape))


def near_buckets():
    distance = np.arange(NEAR)
    exact = BUCKETS // 2
    far = exact + np.floor(
        np.log(np.maximum(distance, 1) / exact) / np.log(128.0 / exact) * exact
    )
    return np.where(distance < exact, distance, np.minimum(far, BUCKETS - 1)).astype(np.int32)


def near_hot():
    return near_buckets()[:, None] == np.arange(BUCKETS)[None, :]


def near_bias(rel_table):
    above = (rel_table - rel_table[-1:])[None]
    rows = jnp.sum(jnp.where(jnp.asarray(near_hot())[:, :, None], above, 0.0), axis=1)
    return jnp.pad(rows.T, ((0, 0), (0, NEAR)))[:, None, :]


def table_gradient(diagonals, totals):
    near = diagonals[:, 0, NEAR - 1 : 2 * NEAR - 1]
    sums = jnp.dot(near, jnp.asarray(near_hot(), F32), precision=HIGHEST)
    far = jnp.sum(totals, axis=(1, 2)) - jnp.sum(near, axis=1)
    return (sums + far[:, None] * (np.arange(BUCKETS) == BUCKETS - 1)).T


def segment_kernel(len_ref, near_ref, q_ref, kc_ref, kn_ref, vc_ref, vn_ref, out_ref, p_ref):
    length = len_ref[0]
    band = pltpu.roll(
        jnp.broadcast_to(near_ref[0], (NEAR, 2 * NEAR)), 0, 1, stride=1, stride_axis=0
    )
    key_ids = lax.broadcasted_iota(jnp.int32, (NEAR, NEAR), 0)
    query_ids = lax.broadcasted_iota(jnp.int32, (NEAR, NEAR), 1)
    on_diagonal = jnp.where(query_ids >= key_ids, band[:, :NEAR], NEGATIVE)
    beside = band[:, NEAR:]
    masked = jnp.full((NEAR, NEAR), NEGATIVE, F32)
    zero = jnp.zeros((NEAR, NEAR), F32)
    cache_t, values_t = vc_ref[...].T, vn_ref[...].T
    step = 2 * NEAR
    for at in range(W // step):
        count = 2 * (at + 1)
        queries = q_ref[pl.ds(step * at, step), :]
        cached = dot(kc_ref[...], queries, NT) * SCALE
        if at == 0:
            last = cached[W - NEAR :] + jnp.concatenate([beside, zero], axis=1)
            cached = jnp.concatenate([cached[: W - NEAR], last], axis=0)
        fresh = dot(kn_ref[pl.ds(0, NEAR * count), :], queries, NT) * SCALE
        rows = [cached]
        for k in range(count):
            block = fresh[NEAR * k : NEAR * (k + 1)]
            tiles = [
                masked if q < k else on_diagonal if q == k else beside if q == k + 1 else zero
                for q in (2 * at, 2 * at + 1)
            ]
            if any(tile is not zero for tile in tiles):
                block = block + jnp.concatenate(tiles, axis=1)
            ids = lax.broadcasted_iota(jnp.int32, (NEAR, step), 0) + NEAR * k
            rows.append(jnp.where(ids < length, block, NEGATIVE))
        scores = jnp.concatenate(rows, axis=0)
        weights = jnp.exp(scores - jnp.max(scores, axis=0, keepdims=True))
        probs = (weights * (1.0 / jnp.sum(weights, axis=0, keepdims=True))).astype(BF)
        p_ref[0, pl.ds(0, W + NEAR * count), pl.ds(step * at, step)] = probs
        out = dot(cache_t, probs[:W]) + dot(values_t[:, : NEAR * count], probs[W:])
        out_ref[pl.ds(step * at, step), :] = out.T


def segment_grad(
    g_ref, q_ref, kc_ref, kn_ref, vc_ref, vn_ref, p_ref, put_q, gk_ref, gv_ref, diag_ref, tot_ref
):
    cache_t, keys_t = kc_ref[...].T, kn_ref[...].T
    on_diagonal = jnp.zeros((NEAR, NEAR), F32)
    beside = jnp.zeros((NEAR, NEAR), F32)
    step = 2 * NEAR
    total = jnp.zeros((8, step), F32)
    grad_keys, grad_values = [], []
    for at in range(W // step):
        count = 2 * (at + 1)
        grads = g_ref[pl.ds(step * at, step), :]
        queries = q_ref[pl.ds(step * at, step), :]
        grad_probs = jnp.concatenate(
            [dot(vc_ref[...], grads, NT), dot(vn_ref[pl.ds(0, NEAR * count), :], grads, NT)], axis=0
        )
        probs = p_ref[0, pl.ds(0, W + NEAR * count), pl.ds(step * at, step)]
        wide = probs.astype(F32)
        product = wide * grad_probs
        grad_scores = product - wide * jnp.sum(product, axis=0, keepdims=True)
        low = grad_scores.astype(BF)
        grad_q = dot(cache_t, low[:W]) + dot(keys_t[:, : NEAR * count], low[W:])
        put_q(step * at, (grad_q * SCALE).T)
        grad_keys.append(dot(low[W:], queries) * SCALE)
        grad_values.append(dot(probs[W:], grads))
        if at == 0:
            beside = beside + grad_scores[W - NEAR : W, :NEAR]
        for k in range(count):
            for side, q in enumerate((2 * at, 2 * at + 1)):
                tile = grad_scores[W + NEAR * k : W + NEAR * (k + 1), NEAR * side : NEAR * (side + 1)]
                if q == k:
                    on_diagonal = on_diagonal + tile
                elif q == k + 1:
                    beside = beside + tile
        total = total + jnp.sum(grad_scores.reshape(-1, 8, step), axis=0)
    for ref, (early, late) in ((gk_ref, grad_keys), (gv_ref, grad_values)):
        ref[...] = jnp.concatenate([late[:step] + early, late[step:]], axis=0).astype(BF)
    down = lax.broadcasted_iota(jnp.int32, (NEAR, NEAR), 0)
    across = lax.broadcasted_iota(jnp.int32, (NEAR, NEAR), 1)
    turned = lax.dot_general(
        (down + across == NEAR - 1).astype(F32),
        jnp.concatenate([on_diagonal, beside], axis=1),
        NN,
        precision=HIGHEST,
        preferred_element_type=F32,
    )
    diagonals = pltpu.roll(turned, 0, 1, stride=1, stride_axis=0)
    diag_ref[0] = jnp.sum(diagonals, axis=0, keepdims=True)
    tot_ref[0] = total


def segment_forward(queries, keys_values, cache, near, length):
    return pl.pallas_call(
        segment_kernel,
        grid=(H,),
        in_specs=[
            SCALARS,
            per_head(1, 2 * NEAR),
            head_columns(W),
            head_columns(W),
            head_columns(W),
            head_columns(W, H),
            head_columns(W, H),
        ],
        out_specs=[head_columns(W), per_head(2 * W, W)],
        out_shape=[
            jax.ShapeDtypeStruct((W, H * HD), F32),
            jax.ShapeDtypeStruct((H, 2 * W, W), BF),
        ],
        compiler_params=pltpu.CompilerParams(vmem_limit_bytes=32 << 20),
        cost_estimate=pl.CostEstimate(
            flops=8 * W * W * HD * H, bytes_accessed=20 << 20, transcendentals=0
        ),
    )(length, near, queries, cache, keys_values, cache, keys_values)


def recall_back(grads, table_ref, p_ref, delta, share):
    slots, step = table_ref.shape[1], 512
    keys_t = table_ref[0, :, pl.ds(0, HD)].T
    out = jnp.zeros((HD, grads.shape[0]), F32)
    for at in range(0, slots, step):
        along = dot(table_ref[0, pl.ds(at, step), pl.ds(HD, HD)], grads, NT)
        scores = (along - delta).astype(BF) * p_ref[0, pl.ds(at, step), :]
        out = out + dot(keys_t[:, at : at + step], scores)
    return (out * (share * SCALE)).T.astype(BF)


def attend_grad_kernel(n_hi, orders, *refs):
    n = len(orders)
    grec_ref, aux_ref, glocal_ref, q_ref, kc_ref, kn_ref, vc_ref, vn_ref, plocal_ref = refs[:9]
    table_ref, p_ref, lse_ref = refs[9:12]
    grads_in, rest = refs[12 : 12 + n], refs[12 + n :]
    gq_ref, gk_ref, gv_ref, diag_ref, tot_ref = rest[:5]
    sums_out, rest = rest[5 : 5 + n], rest[5 + n :]
    asked, aux, back, returned, glocal_q = rest[:5]
    ask_send, ask_recv, aux_send, aux_recv, back_send, back_recv = rest[5:11]
    buffers = [rest[11 + k * n : 11 + (k + 1) * n] for k in range(5)]
    place = Place(n_hi)
    scatter = Scatter(place, orders, grads_in, sums_out, buffers, rest[11 + 5 * n :])
    tick = pl.program_id(0)
    ticks = 3 * H
    order = near_first(n_hi)[::-1]

    def remote(src, dst, send, recv, to):
        return pltpu.make_async_remote_copy(
            src_ref=src,
            dst_ref=dst,
            send_sem=send,
            recv_sem=recv,
            device_id=place.device(to),
            device_id_type=MESH,
        )

    def ask(slot, to):
        first = slot < 3
        return [
            remote(
                grec_ref if first else asked.at[2],
                asked.at[slot],
                ask_send.at[slot],
                ask_recv.at[slot],
                to,
            ),
            remote(
                aux_ref if first else aux.at[2],
                aux.at[slot],
                aux_send.at[slot],
                aux_recv.at[slot],
                to,
            ),
        ]

    def asked_arrived(slot):
        place.arrived(asked.at[slot], ask_recv.at[slot])
        place.arrived(aux.at[slot], aux_recv.at[slot])

    def give(slot, to):
        return remote(
            back.at[(1, 3, 2)[slot]], returned.at[slot], back_send.at[slot], back_recv.at[slot], to
        )

    @pl.when(tick == 0)
    def _():
        place.greet()
        for slot, to in ((1, ALONG_CORE), (2, ALONG_X)):
            for copy in ask(slot, to):
                copy.start()
        for z in order:
            for a in range(n):
                scatter.begin(z, a)
        asked[0] = grec_ref[...]
        aux[0] = aux_ref[...]

    events = []
    for k in range(n_hi + 2):
        for delay, event in enumerate((scatter.core, scatter.one, scatter.two)):
            if 0 <= k - delay < n_hi:
                events += [functools.partial(event, order[k - delay], a) for a in range(n)]
    for at in range(1, ticks):
        mine = events[len(events) * (at - 1) // (ticks - 1) : len(events) * at // (ticks - 1)]

        @pl.when(tick == at)
        def _(mine=mine):
            for event in mine:
                event()

    @pl.when(tick < H)
    def _():
        segment_grad(
            glocal_ref, q_ref, kc_ref, kn_ref, vc_ref, vn_ref, plocal_ref,
            lambda at, value: glocal_q.__setitem__(
                (pl.ds(at, value.shape[0]), pl.ds(pl.multiple_of(tick * HD, HD), HD)), value
            ),
            gk_ref, gv_ref, diag_ref, tot_ref,
        )

    @pl.when(tick == H)
    def _():
        asked_arrived(1)

    @pl.when(tick == H + 2)
    def _():
        asked_arrived(2)
        for copy in ask(3, ALONG_CORE):
            copy.start()

    @pl.when(tick == 2 * H)
    def _():
        asked_arrived(3)
        give(0, ALONG_CORE).start()

    @pl.when(tick >= H)
    def _():
        phase = tick // H - 1
        head = tick % H
        lanes = pl.ds(pl.multiple_of(head * HD, HD), HD)
        pair = pl.ds(phase * 2, 2)
        grads = asked[pair, :, lanes].reshape(-1, HD)
        delta = jnp.concatenate([aux[phase * 2 + k, pl.ds(head, 1), :] for k in range(2)], axis=1)
        total = jnp.concatenate(
            [aux[phase * 2 + k, pl.ds(H + head, 1), :] for k in range(2)], axis=1
        )
        share = jnp.exp(lse_ref[0] - total)
        result = recall_back(grads, table_ref, p_ref, delta, share)
        back[pair, :, lanes] = result.reshape(2, -1, HD)

    @pl.when(tick == ticks - 1)
    def _():
        give(1, ALONG_CORE).start()
        place.arrived(returned.at[1], back_recv.at[1])
        back[2] = (back[2].astype(F32) + returned[1].astype(F32)).astype(BF)
        give(2, ALONG_X).start()
        for a in range(n):
            scatter.last(a)
        place.arrived(returned.at[0], back_recv.at[0])
        place.arrived(returned.at[2], back_recv.at[2])
        gq_ref[...] = (
            glocal_q[...]
            + back[0].astype(F32)
            + returned[0].astype(F32)
            + returned[2].astype(F32)
        ).astype(BF)
        scatter.finish()
        for slot, to in ((1, ALONG_CORE), (2, ALONG_X), (3, ALONG_CORE)):
            for copy in ask(slot, to):
                copy.wait_send()
        for slot, to in ((0, ALONG_CORE), (1, ALONG_CORE), (2, ALONG_X)):
            give(slot, to).wait_send()


def attend_grad(
    grad_recalled, aux, grad_local, queries, keys_values, cache, probs_local, table, probs, lses,
    grads, orders, collective_id,
):
    n, n_hi = len(grads), lax.axis_size("dp") // 2
    (rows, width), slots = queries.shape, table.shape[1]
    shapes = [g.shape[1:] for g in grads]
    dma = pltpu.SemaphoreType.DMA

    def column(first=0):
        return pl.BlockSpec((rows, HD), lambda t: (0, first + jnp.minimum(t, H - 1)))

    def head(*shape):
        return pl.BlockSpec((1,) + shape, lambda t: (jnp.minimum(t, H - 1),) + (0,) * len(shape))

    def later(t):
        return jnp.maximum(t - H, 0)

    return pl.pallas_call(
        functools.partial(attend_grad_kernel, n_hi, orders),
        grid=(3 * H,),
        in_specs=[
            IN_VMEM,
            IN_VMEM,
            column(),
            column(),
            column(),
            column(),
            column(H),
            column(H),
            head(2 * W, W),
            pl.BlockSpec((1, slots, 2 * HD), lambda t: (later(t) % H, 0, 0)),
            pl.BlockSpec((1, slots, 2 * rows), lambda t: (later(t), 0, 0)),
            pl.BlockSpec((1, 1, 2 * rows), lambda t: (later(t) % H, 0, later(t) // H)),
        ]
        + [ANYWHERE] * n,
        out_specs=[IN_VMEM, column(), column(), head(1, 2 * NEAR), head(8, 2 * NEAR)]
        + [IN_VMEM] * n,
        out_shape=[
            jax.ShapeDtypeStruct((rows, width), BF),
            jax.ShapeDtypeStruct((rows, width), BF),
            jax.ShapeDtypeStruct((rows, width), BF),
            jax.ShapeDtypeStruct((H, 1, 2 * NEAR), F32),
            jax.ShapeDtypeStruct((H, 8, 2 * NEAR), F32),
        ]
        + [jax.ShapeDtypeStruct(shape, F32) for shape in shapes],
        scratch_shapes=[
            pltpu.VMEM((4, rows, width), BF),
            pltpu.VMEM((4,) + aux.shape, F32),
            pltpu.VMEM((4, rows, width), BF),
            pltpu.VMEM((3, rows, width), BF),
            pltpu.VMEM((rows, width), F32),
        ]
        + [dma((4,))] * 4
        + [dma((3,))] * 2
        + scatter_buffers(shapes, n_hi)
        + scatter_sems(n, n_hi),
        compiler_params=pltpu.CompilerParams(
            collective_id=collective_id, has_side_effects=True, vmem_limit_bytes=62 << 20
        ),
        cost_estimate=pl.CostEstimate(
            flops=16 * rows * slots * HD * H, bytes_accessed=128 << 20, transcendentals=0
        ),
    )(
        grad_recalled, aux, grad_local, queries, cache, keys_values, cache, keys_values,
        probs_local, table, probs, lses, *grads,
    )


def feed_kernel(
    parts_ref, lse_ref, local_ref, x_ref, cot_ref, gate_ref, norms_ref, wo_ref, up_ref, down_ref,
    out_ref, gatt_ref, gwo_ref, gup_ref, gdown_ref, glocal_ref, grec_ref, aux_ref, sums_ref,
    recalled, mixed_t, attended, scaled, inverse, normed, normed_t, acc, gacc,
):
    step, last = pl.program_id(0), pl.num_programs(0) - 1
    rows, width = x_ref.shape
    gate = gate_ref[...]

    @pl.when(step == 0)
    def _():
        lses = [lse_ref[k] for k in range(3)]
        top = functools.reduce(jnp.maximum, lses)
        total = top + jnp.log(sum(jnp.exp(lse - top) for lse in lses))
        aux_ref[H:, :] = total
        shares = [jnp.exp(lse - total).T for lse in lses]
        for h in range(H):
            at = pl.ds(h * HD, HD)
            recalled[:, at] = sum(
                shares[k][:, h : h + 1] * parts_ref[k, :, at].astype(F32) for k in range(3)
            )
        mixed = (gate * recalled[...] + (1.0 - gate) * local_ref[...]).astype(BF)
        mixed_t[...] = mixed.T
        here = x_ref[...].astype(F32) + dot(mixed, wo_ref[...])
        attended[...] = here
        center = here - jnp.mean(here, axis=-1, keepdims=True)
        inv = lax.rsqrt(jnp.mean(center * center, axis=-1, keepdims=True) + EPSILON)
        inverse[...] = inv
        scaled[...] = center * inv
        n2 = (scaled[...] * norms_ref[1:2] + norms_ref[3:4]).astype(BF)
        normed[...] = n2
        normed_t[...] = n2.T
        acc[...] = jnp.zeros(acc.shape, F32)
        gacc[...] = jnp.zeros(gacc.shape, F32)

    up = dot(normed[...], up_ref[...])
    root = np.sqrt(2 / np.pi).astype(np.float32)
    square = up * up
    bend = jnp.tanh(root * (up + 0.044715 * (square * up)))
    hidden = (0.5 * up * (1.0 + bend)).astype(BF)
    slope = 0.5 * (1.0 + bend) + 0.5 * up * (1.0 - bend * bend) * (
        root * (1.0 + (3 * 0.044715) * square)
    )
    grad_up = (dot(cot_ref[...], down_ref[...], NT) * slope).astype(BF)
    acc[...] += dot(hidden, down_ref[...])
    gacc[...] += dot(grad_up, up_ref[...], NT)
    gdown_ref[...] = dot(hidden.T, cot_ref[...]).astype(BF)
    gup_ref[...] = dot(normed_t[...], grad_up).astype(BF)

    @pl.when(step == last)
    def _():
        out_ref[...] = (attended[...] + acc[...]).astype(BF)
        grad = gacc[...]
        sums_ref[0:1] = jnp.sum(grad * scaled[...], axis=0, keepdims=True)
        sums_ref[1:2] = jnp.sum(grad, axis=0, keepdims=True)
        grad = grad * norms_ref[1:2]
        mean_grad = jnp.mean(grad, axis=-1, keepdims=True)
        mean_cross = jnp.mean(grad * scaled[...], axis=-1, keepdims=True)
        grad = cot_ref[...].astype(F32) + inverse[...] * (
            grad - mean_grad - scaled[...] * mean_cross
        )
        gatt_ref[...] = grad
        low = grad.astype(BF)
        gwo_ref[...] = dot(mixed_t[...], low).astype(BF)
        gmixed = dot(low, wo_ref[...], NT)
        sums_ref[2:3] = jnp.sum(gmixed * (recalled[...] - local_ref[...]), axis=0, keepdims=True)
        sums_ref[3:] = jnp.zeros((5, width), F32)
        glocal_ref[...] = ((1.0 - gate) * gmixed).astype(BF)
        grec = (gate * gmixed).astype(BF)
        grec_ref[...] = grec
        product = grec.astype(F32) * recalled[...]
        delta = [
            jnp.sum(product[:, h * HD : (h + 1) * HD], axis=1, keepdims=True) for h in range(H)
        ]
        aux_ref[:H, :] = jnp.concatenate(delta, axis=1).T


def feed(parts, lses, local_out, x, cotangent, gate_row, norm_rows, w_out, w_up, w_down):
    rows, width = x.shape
    hidden = w_up.shape[1]
    block = 512
    full = jax.ShapeDtypeStruct
    return pl.pallas_call(
        feed_kernel,
        grid=(hidden // block,),
        in_specs=[IN_VMEM] * 8
        + [
            pl.BlockSpec((width, block), lambda k: (0, k)),
            pl.BlockSpec((block, width), lambda k: (k, 0)),
        ],
        out_specs=[IN_VMEM] * 3
        + [
            pl.BlockSpec((width, block), lambda k: (0, k)),
            pl.BlockSpec((block, width), lambda k: (k, 0)),
        ]
        + [IN_VMEM] * 4,
        out_shape=[
            full((rows, width), BF),
            full((rows, width), F32),
            full((width, width), BF),
            full((width, hidden), BF),
            full((hidden, width), BF),
            full((rows, width), BF),
            full((rows, width), BF),
            full((2 * H, rows), F32),
            full((8, width), F32),
        ],
        scratch_shapes=[
            pltpu.VMEM((rows, width), F32),
            pltpu.VMEM((width, rows), BF),
            pltpu.VMEM((rows, width), F32),
            pltpu.VMEM((rows, width), F32),
            pltpu.VMEM((rows, 1), F32),
            pltpu.VMEM((rows, width), BF),
            pltpu.VMEM((width, rows), BF),
            pltpu.VMEM((rows, width), F32),
            pltpu.VMEM((rows, width), F32),
        ],
        compiler_params=pltpu.CompilerParams(vmem_limit_bytes=56 << 20),
        cost_estimate=pl.CostEstimate(
            flops=12 * rows * width * hidden, bytes_accessed=36 << 20, transcendentals=0
        ),
    )(parts, lses, local_out, x, cotangent, gate_row, norm_rows, w_out, w_up, w_down)


def norm_forward(values, gain_row, shift_row):
    center = values - jnp.mean(values, axis=-1, keepdims=True)
    inverse = lax.rsqrt(jnp.mean(center * center, axis=-1, keepdims=True) + EPSILON)
    scaled = center * inverse
    return (scaled * gain_row + shift_row, scaled, inverse)


def norm_backward(grad_normed, scaled, inverse, gain_row):
    grad_scaled = grad_normed * gain_row
    mean_grad = jnp.mean(grad_scaled, axis=-1, keepdims=True)
    mean_cross = jnp.mean(grad_scaled * scaled, axis=-1, keepdims=True)
    return inverse * (grad_scaled - mean_grad - scaled * mean_cross)


def swap(value, turn):
    return jax.tree.map(
        lambda v: lax.ppermute(v, "mem", [(i, i ^ turn) for i in range(lax.axis_size("mem"))]), value
    )


def combine(outs, lses):
    total = jax.nn.logsumexp(jnp.stack(lses), axis=0)
    rows = outs[0].shape[0]
    result = 0.0
    for out, lse in zip(outs, lses):
        share = jnp.exp(lse - total).T[:, :, None]
        result = result + share * out.reshape(rows, H, HD).astype(F32)
    return result.reshape(rows, H * HD), total


def local(
    tokens,
    norm_gains,
    norm_shifts,
    w_qkv,
    w_out,
    w_up,
    w_down,
    rel_table,
    gate_bias,
    xl_cache,
    memory,
    slot_index,
    seg_len,
    cotangent,
):
    width = tokens.shape[1]
    count = tokens.shape[0]
    slot_count = memory.shape[0]
    groups = lax.axis_size("mem")
    me = lax.axis_index("mem")

    devices = lax.axis_size("dp") * groups
    number = lax.axis_index("dp") * groups + me
    own = norm_gains.shape[1]
    norms = jnp.pad(
        jnp.concatenate([norm_gains, norm_shifts], axis=0), ((0, 12), (0, 128 - own))
    )
    norms = jnp.roll(norms, number % (128 // own) * own, axis=1)
    table = memory.transpose(1, 0, 2)
    slot_rows = (slot_index - me * slot_count).reshape(groups, count, H, -1)
    picks = [
        lax.dynamic_index_in_dim(slot_rows, me ^ turn, 0, keepdims=False) for turn in range(groups)
    ]
    chosen = jnp.stack(picks).transpose(2, 3, 0, 1).reshape(H, -1, groups * count)
    normed_one, queries, norm_rows, out_all, lse_all, probs_all, *full = attend(
        tokens,
        table,
        chosen,
        (w_qkv[:, :width], norms),
        (w_qkv[:, width:], w_out, w_up, w_down),
        ("zyx", "zxy", "xyz", "xyz", "zyx", "zxy"),
        0,
    )
    full_q, full_kv, full_out, full_up, full_down = [f.reshape(-1, f.shape[2]) for f in full]
    gain_rows, shift_rows = norm_rows[:2], norm_rows[2:4]
    out_own, out_core, out_x, out_cross = jnp.split(out_all, groups)
    lse_chip, lse_far = lse_all[:, 0, : 2 * count], lse_all[:, 0, 2 * count :]

    inputs = tokens.astype(F32)
    _, scaled_one, inverse_one = norm_forward(inputs, gain_rows[0], shift_rows[0])
    keys_values = dot(normed_one, full_kv).astype(BF)
    local_out, probs_local = segment_forward(
        queries, keys_values, xl_cache, near_bias(rel_table), seg_len
    )

    own_lse, own_out = lse_chip[:, :count], out_own
    core_out, core_lse = swap((out_core, lse_chip[:, count:]), 1)
    other_out, other_lse = swap((out_cross, lse_far[:, count:]), 1)
    pair_out, pair_lse = combine((out_x, other_out), (lse_far[:, :count], other_lse))
    far_out, far_lse = swap((pair_out.astype(BF), pair_lse), 2)
    gate_open = jax.nn.sigmoid(gate_bias)
    output, grad_attended, grad_wout, grad_up, grad_down, grad_local, grad_recalled, aux, sums = feed(
        jnp.stack([own_out, core_out, far_out]),
        jnp.stack([own_lse, core_lse, far_lse]),
        local_out,
        tokens,
        cotangent,
        jnp.repeat(gate_open, HD)[None],
        norm_rows,
        full_out,
        full_up,
        full_down,
    )
    grad_gate = jnp.sum(sums[2].reshape(H, HD), axis=1) * gate_open * (1.0 - gate_open)
    grad_query, grad_keys, grad_values, diagonals, totals, share_out, share_up, share_down = attend_grad(
        grad_recalled,
        aux,
        grad_local,
        queries,
        keys_values,
        xl_cache,
        probs_local,
        table,
        probs_all,
        lse_all,
        [g.reshape(devices, -1, g.shape[1]) for g in (grad_wout, grad_up, grad_down)],
        ("yxz", "yxz", "xyz"),
        1,
    )
    grad_table = table_gradient(diagonals, totals)
    grad_qkv_low = jnp.concatenate([grad_query, grad_keys, grad_values], axis=1)
    grad_wqkv = jnp.einsum("td,te->de", normed_one, grad_qkv_low, preferred_element_type=F32)
    grad_normed_one = dot(grad_qkv_low[:, :width], full_q, NT) + dot(
        grad_qkv_low[:, width:], full_kv, NT
    )
    grad_tokens = grad_attended + norm_backward(
        grad_normed_one, scaled_one, inverse_one, gain_rows[0]
    )
    grad_norms = jnp.stack(
        [
            jnp.sum(grad_normed_one * scaled_one, axis=0),
            sums[0],
            jnp.sum(grad_normed_one, axis=0),
            sums[1],
        ]
    )
    rest = jnp.pad(jnp.concatenate([grad_table.reshape(-1), grad_gate]), (0, 1024 - 264))
    small = jnp.concatenate([grad_norms.reshape(-1, 128), rest.reshape(-1, 128)], axis=0)
    half = grad_wqkv.shape[1] // 2
    share_left, share_right, small = scatter_sums(
        [
            g.astype(BF).reshape(devices, -1, half)
            for g in (grad_wqkv[:, :half], grad_wqkv[:, half:])
        ],
        ("yxz", "xyz"),
        small,
        2,
    )
    share_qkv = jnp.concatenate([share_left, share_right], axis=1)
    share_norms = lax.dynamic_slice_in_dim(
        small[:32].reshape(4, width), number * own, own, axis=1
    )
    rest = small[32:].reshape(-1)
    table_total, gate_total = rest[: BUCKETS * H].reshape(BUCKETS, H), rest[BUCKETS * H :][:H]
    return (
        output,
        grad_tokens,
        share_norms[:2],
        share_norms[2:],
        share_qkv,
        share_out,
        share_up,
        share_down,
        table_total,
        gate_total,
    )


def solution(mesh):
    shard = P(AXES, None)
    placed = (
        shard,
        P(None, AXES),
        P(None, AXES),
        shard,
        shard,
        shard,
        shard,
        P(),
        P(),
        shard,
        P(AXES, None, None),
        P("dp", None, "mem"),
        P(AXES),
        shard,
    )
    return jax.shard_map(
        local,
        mesh=mesh,
        in_specs=placed,
        out_specs=(
            shard,
            shard,
            P(None, AXES),
            P(None, AXES),
            shard,
            shard,
            shard,
            shard,
            P(),
            P(),
        ),
        check_vma=False,
    )
```

```python
import functools

import jax
import jax.numpy as jnp
import numpy as np
from jax import lax
from jax.experimental import pallas as pl
from jax.experimental.pallas import tpu as pltpu
from jax.sharding import PartitionSpec as P

H = 8
HD = 128
W = 512
BUCKETS = 32
NEAR = 128
EPSILON = 1e-05
NEGATIVE = -1e30
SCALE = HD ** (-0.5)
AXES = ("dp", "mem")
MESH = pl.DeviceIdType.MESH
HIGHEST = lax.Precision.HIGHEST
BF = jnp.bfloat16
F32 = jnp.float32
NT = (((1,), (1,)), ((), ()))
NN = (((1,), (0,)), ((), ()))


def dot(left, right, dims=NN):
    return lax.dot_general(left, right, dims, preferred_element_type=F32)


OWN, ALONG_Y, ALONG_X, ALONG_CORE = (0, 0, 0, 0), (0, 1, 0, 0), (0, 0, 1, 0), (0, 0, 0, 1)
ANYWHERE = pl.BlockSpec(memory_space=pl.ANY)
IN_VMEM = pl.BlockSpec(memory_space=pltpu.VMEM)
SCALARS = pl.BlockSpec(memory_space=pltpu.SMEM)


class Place:
    def __init__(self, n_hi):
        self.sizes = (n_hi, 2, 2, 2)
        dp, mem = lax.axis_index("dp"), lax.axis_index("mem")
        self.at = (dp // 2, dp % 2, mem // 2, mem % 2)

    def device(self, step):
        z, y, x, core = [(a + s) % n for a, s, n in zip(self.at, step, self.sizes)]
        return (z * 2 + y, x * 2 + core)

    def number(self, step):
        dp, mem = self.device(step)
        return dp * 4 + mem

    def plus(self, left, right):
        return tuple((a + b) % n for a, b, n in zip(left, right, self.sizes))

    def minus(self, left, right):
        return tuple((a - b) % n for a, b, n in zip(left, right, self.sizes))

    def partners(self):
        return [(z, 0, 0, 0) for z in range(1, self.sizes[0])] + [ALONG_Y, ALONG_X, ALONG_CORE]

    def greet(self):
        barrier = pltpu.get_barrier_semaphore()
        for partner in self.partners():
            pl.semaphore_signal(
                barrier, inc=1, device_id=self.device(partner), device_id_type=MESH
            )
        pl.semaphore_wait(barrier, len(self.partners()))

    def arrived(self, ref, recv):
        pltpu.make_async_remote_copy(
            src_ref=ref,
            dst_ref=ref,
            send_sem=recv,
            recv_sem=recv,
            device_id=self.device(ALONG_CORE),
            device_id_type=MESH,
        ).wait_recv()


def near_first(n_hi):
    order = [0]
    for z in range(1, n_hi // 2 + 1):
        order += [k for k in dict.fromkeys((z, n_hi - z)) if k < n_hi]
    return order


class Gather:
    LEFT, RIGHT, Y, X, CORE = "left", "right", ALONG_Y, ALONG_X, ALONG_CORE

    def __init__(self, place, orders, ins, outs, sems):
        self.place, self.ins, self.outs = place, ins, outs
        self.send_sem, self.recv_sem, self.own_sem = sems
        self.n = len(orders)
        self.orders = [["zyx".index(axis) for axis in order] for order in orders]
        self.sent = [[] for _ in orders]

    def exists(self, steps):
        z, n = self.place.at[0], self.place.sizes[0]
        return z + steps >= 0 if steps < 0 else z + steps < n

    def device(self, to):
        z, y, x, core = self.place.at
        if to in (self.LEFT, self.RIGHT):
            return ((z + (1 if to == self.RIGHT else -1)) * 2 + y, x * 2 + core)
        return self.place.device(to)

    def spot(self, a, source):
        z, y, x, core = self.place.at
        dp = (z + source[0]) * 2 + (y + source[1]) % 2
        return self.outs[a].at[dp * 4 + (x + source[2]) % 2 * 2 + (core + source[3]) % 2]

    def recv(self, a, source, to=None):
        z = self.place.at[0] + source[0]
        rest = list(source[1:])
        if to is not None and to not in (self.LEFT, self.RIGHT):
            rest = [(have - step) % 2 for have, step in zip(rest, to[1:])]
        return self.recv_sem.at[a, ((z * 2 + rest[0]) * 2 + rest[1]) * 2 + rest[2]]

    def copy(self, a, k):
        source, to = self.sent[a][k]
        return pltpu.make_async_remote_copy(
            src_ref=self.ins[a] if source == OWN else self.spot(a, source),
            dst_ref=self.spot(a, source),
            send_sem=self.send_sem.at[a, k],
            recv_sem=self.recv(a, source, to),
            device_id=self.device(to),
            device_id_type=MESH,
        )

    def when(self, conditions, run):
        conditions = [c for c in conditions if c is not None]
        if conditions:
            pl.when(functools.reduce(jnp.logical_and, conditions))(run)
        else:
            run()

    def limits(self, source, to):
        ends = {self.LEFT: -1, self.RIGHT: 1}
        return [
            self.exists(source[0]) if source[0] else None,
            self.exists(ends[to]) if to in ends else None,
        ]

    def send(self, a, source, to):
        self.sent[a].append((source, to))
        k = len(self.sent[a]) - 1
        self.when(self.limits(source, to)[1:], lambda: self.copy(a, k).start())

    def own(self, a):
        return pltpu.make_async_copy(self.ins[a], self.spot(a, OWN), self.own_sem.at[a])

    def arrived(self, a, source):
        self.place.arrived(self.spot(a, source), self.recv(a, source))

    def onward(self, a, source):
        order = self.orders[a]
        came = max([order.index(axis) for axis in range(3) if source[axis]], default=-1)
        to = []
        if came >= 0 and order[came] == 0:
            to.append(self.RIGHT if source[0] < 0 else self.LEFT)
        for axis in order[came + 1 :]:
            to += ((self.LEFT, self.RIGHT), (self.Y,), (self.X,))[axis]
        return to + [self.CORE]

    def begin(self, a):
        for to in self.onward(a, OWN):
            self.send(a, OWN, to)
        self.own(a).start()

    def level(self, a, hops):
        for rest in ((0, 0), (1, 0), (0, 1), (1, 1)):
            distance = hops - sum(rest)
            if not 0 <= distance < self.place.sizes[0]:
                continue
            for steps in dict.fromkeys((-distance, distance)):

                def run(source=(steps,) + rest + (0,)):
                    self.arrived(a, source)
                    for to in self.onward(a, source):
                        self.send(a, source, to)

                self.when([self.exists(steps) if steps else None], run)

    def levels(self):
        return range(1, self.place.sizes[0] + 2)

    def finish(self, a):
        place = self.place
        for z in range(place.sizes[0]):
            for y in range(2):
                for x in range(2):
                    source = (z - place.at[0], y, x, 1)
                    place.arrived(self.spot(a, source), self.recv(a, source))
        for k in range(len(self.sent[a])):
            self.when(self.limits(*self.sent[a][k]), lambda k=k: self.copy(a, k).wait_send())
        self.own(a).wait()


def gather_sems(n, n_hi):
    sends = 5 + (8 * n_hi - 5) * 4
    dma = pltpu.SemaphoreType.DMA
    return [dma((n, sends)), dma((n, n_hi * 8)), dma((n,))]


def piece_width(columns):
    return next(w for w in (1024, 768, 512, 384, 256, 128) if columns % w == 0)


class Scatter:
    def __init__(self, place, orders, ins, outs, buffers, sems, small=None):
        self.place, self.ins, self.outs = place, ins, outs
        self.accs, self.from_core, self.from_first, self.from_second, self.from_z = buffers
        (
            self.load_sem,
            self.core_send,
            self.core_recv,
            self.first_send,
            self.first_recv,
            self.second_send,
            self.second_recv,
            self.z_send,
            self.z_recv,
        ) = sems[:9]
        self.small = small
        self.small_sems = sems[9:]
        self.n = len(orders)
        self.n_hi = place.sizes[0]
        self.first = [ALONG_X if order == "xyz" else ALONG_Y for order in orders]
        self.second = [ALONG_Y if order == "xyz" else ALONG_X for order in orders]
        self.started = []

    def step(self, a, z, two, one):
        y, x = (two, one) if self.second[a] == ALONG_Y else (one, two)
        return (z, y, x, 0)

    def send(self, ends, device):
        def build():
            src, dst, send, recv = ends()
            return pltpu.make_async_remote_copy(
                src_ref=src,
                dst_ref=dst,
                send_sem=send,
                recv_sem=recv,
                device_id=device(),
                device_id_type=MESH,
            )

        build().start()
        self.started.append(build)

    def load(self, a, z, two, one):
        s = (z * 2 + two) * 2 + one
        return pltpu.make_async_copy(
            self.ins[a].at[self.place.number(self.step(a, z, two, one))],
            self.accs[a].at[s],
            self.load_sem.at[a, s],
        )

    def begin(self, z, a):
        for two, one in ((1, 1), (0, 1), (1, 0), (0, 0)):
            s = (z * 2 + two) * 2 + one
            step = self.step(a, z, two, one)[:3] + (1,)
            self.send(
                lambda s=s, step=step: (
                    self.ins[a].at[self.place.number(step)],
                    self.from_core[a].at[s],
                    self.core_send.at[a, s],
                    self.core_recv.at[a, s],
                ),
                lambda: self.place.device(ALONG_CORE),
            )
            self.load(a, z, two, one).start()

    def add(self, acc, got):
        width = piece_width(acc.shape[1])

        def piece(k, carry):
            at = pl.ds(pl.multiple_of(k * width, width), width)
            acc[:, at] = (acc[:, at].astype(F32) + got[:, at].astype(F32)).astype(BF)
            return carry

        lax.fori_loop(0, acc.shape[1] // width, piece, 0)

    def core(self, z, a):
        for two, one in ((1, 1), (0, 1), (1, 0), (0, 0)):
            k = z * 2 + two
            s = k * 2 + one
            self.load(a, z, two, one).wait()
            self.place.arrived(self.from_core[a].at[s], self.core_recv.at[a, s])
            self.add(self.accs[a].at[s], self.from_core[a].at[s])
            if one:
                self.send(
                    lambda s=s, k=k: (
                        self.accs[a].at[s],
                        self.from_first[a].at[k],
                        self.first_send.at[a, k],
                        self.first_recv.at[a, k],
                    ),
                    lambda: self.place.device(self.first[a]),
                )

    def one(self, z, a):
        for two in (1, 0):
            k = z * 2 + two
            acc = self.accs[a].at[k * 2]
            self.place.arrived(self.from_first[a].at[k], self.first_recv.at[a, k])
            self.add(acc, self.from_first[a].at[k])
            if two:
                self.send(
                    lambda k=k: (
                        self.accs[a].at[k * 2],
                        self.from_second[a].at[z],
                        self.second_send.at[a, z],
                        self.second_recv.at[a, z],
                    ),
                    lambda: self.place.device(self.second[a]),
                )

    def two(self, z, a):
        acc = self.accs[a].at[z * 4]
        self.place.arrived(self.from_second[a].at[z], self.second_recv.at[a, z])
        self.add(acc, self.from_second[a].at[z])
        if z:
            self.send(
                lambda: (
                    self.accs[a].at[z * 4],
                    self.from_z[a].at[z - 1],
                    self.z_send.at[a, z - 1],
                    self.z_recv.at[a, z - 1],
                ),
                lambda: self.place.device((z, 0, 0, 0)),
            )

    def last(self, a):
        for z in range(1, self.n_hi):
            self.place.arrived(self.from_z[a].at[z - 1], self.z_recv.at[a, z - 1])
        out, acc, got = self.outs[a], self.accs[a].at[0], self.from_z[a]
        width = piece_width(out.shape[1])

        def piece(k, carry):
            at = pl.ds(pl.multiple_of(k * width, width), width)
            total = acc[:, at].astype(F32)
            for z in range(1, self.n_hi):
                total = total + got[z - 1, :, at].astype(F32)
            out[:, at] = total
            return carry

        lax.fori_loop(0, out.shape[1] // width, piece, 0)

    def small_steps(self):
        return [ALONG_CORE, ALONG_X, ALONG_Y] + [1 << k for k in range((self.n_hi - 1).bit_length())]

    def small_begin(self):
        source, total, _ = self.small
        total[...] = source[...]
        self.small_send(0)

    def small_device(self, k):
        step = self.small_steps()[k]
        z, y, x, core = self.place.at
        if isinstance(step, int):
            return ((z + step - 2 * step * ((z // step) % 2)) * 2 + y, x * 2 + core)
        return self.place.device(step)

    def small_send(self, k):
        _, total, buffer = self.small
        buffer[0, k] = total[...]
        send, recv = self.small_sems
        self.send(
            lambda: (buffer.at[0, k], buffer.at[1, k], send.at[k], recv.at[k]),
            lambda: self.small_device(k),
        )

    def small_next(self, k):
        _, total, buffer = self.small
        self.place.arrived(buffer.at[1, k], self.small_sems[1].at[k])
        total[...] = total[...] + buffer[1, k]
        if k + 1 < len(self.small_steps()):
            self.small_send(k + 1)

    def finish(self):
        for build in self.started:
            build().wait_send()


def scatter_buffers(shapes, n_hi):
    counts = (n_hi * 4, n_hi * 4, n_hi * 2, n_hi, n_hi - 1)
    return [pltpu.VMEM((count,) + shape, BF) for count in counts for shape in shapes]


def scatter_sems(n, n_hi):
    counts = (n_hi * 4,) * 3 + (n_hi * 2,) * 2 + (n_hi,) * 2 + (n_hi - 1,) * 2
    return [pltpu.SemaphoreType.DMA((n, count)) for count in counts]


def scatter_kernel(n_hi, orders, *refs):
    n = len(orders)
    ins, small_in, outs, small_out = refs[:n], refs[n], refs[n + 1 : 2 * n + 1], refs[2 * n + 1]
    rest = refs[2 * n + 2 :]
    buffers = [rest[k * n : (k + 1) * n] for k in range(5)]
    place = Place(n_hi)
    place.greet()
    scatter = Scatter(
        place, orders, ins, outs, buffers, rest[5 * n + 1 :], (small_in, small_out, rest[5 * n])
    )
    order = near_first(n_hi)[::-1]
    rounds = len(scatter.small_steps())
    for k, z in enumerate(order):
        for a in range(n):
            scatter.begin(z, a)
        if k == 0:
            scatter.small_begin()
    for k in range(max(len(order) + 2, rounds)):
        for a in range(n):
            if k < len(order):
                scatter.core(order[k], a)
        for a in range(n):
            if 0 <= k - 1 < len(order):
                scatter.one(order[k - 1], a)
        for a in range(n):
            if 0 <= k - 2 < len(order):
                scatter.two(order[k - 2], a)
        if k < rounds:
            scatter.small_next(k)
    for a in range(n):
        scatter.last(a)
    scatter.finish()


def scatter_sums(arrays, orders, small, collective_id):
    n = len(arrays)
    n_hi = lax.axis_size("dp") // 2
    shapes = [a.shape[1:] for a in arrays]
    rounds = 3 + (n_hi - 1).bit_length()
    dma = pltpu.SemaphoreType.DMA
    return pl.pallas_call(
        functools.partial(scatter_kernel, n_hi, orders),
        out_shape=[jax.ShapeDtypeStruct(shape, F32) for shape in shapes]
        + [jax.ShapeDtypeStruct(small.shape, F32)],
        in_specs=[ANYWHERE] * n + [IN_VMEM],
        out_specs=[IN_VMEM] * (n + 1),
        scratch_shapes=scatter_buffers(shapes, n_hi)
        + [pltpu.VMEM((2, rounds) + small.shape, F32)]
        + scatter_sems(n, n_hi)
        + [dma((rounds,)), dma((rounds,))],
        compiler_params=pltpu.CompilerParams(
            collective_id=collective_id, has_side_effects=True, vmem_limit_bytes=56 << 20
        ),
    )(*arrays, small)


FIRST_STOP, FIRST_SPAN, LAST_SPAN = 2, 60, 88


def pick_scores(queries, table_ref, chosen, pause):
    slots, step = table_ref.shape[1], 256
    low, high = chosen & 7, chosen >> 3
    picked = jnp.zeros(chosen.shape, F32)
    for at in range(0, slots, step):
        scores = dot(table_ref[0, pl.ds(at, step), pl.ds(0, HD)], queries, NT)
        for row in range(0, step, 8):
            got = jnp.take_along_axis(scores[row : row + 8], low, axis=0)
            picked = jnp.where(high == (at + row) // 8, got, picked)
        if at + step == slots // 2:
            pause()
    return picked * SCALE


def recall_values(scores, table_ref, chosen, put_lse, p_ref, pause):
    slots, tokens, step = table_ref.shape[1], chosen.shape[1], 256
    top = jnp.max(scores, axis=0, keepdims=True)
    weights = jnp.exp(scores - top)
    total = jnp.sum(weights, axis=0, keepdims=True)
    put_lse(top + jnp.log(total))
    times = jnp.ones_like(weights)
    for turn in range(1, 8):
        times = times + jnp.where(pltpu.roll(chosen, turn, 0) == chosen, 1.0, 0.0)
    probs = (weights / total * times).astype(BF)
    rows = lax.broadcasted_iota(jnp.int32, (step, tokens), 0).astype(F32).astype(BF)
    out = jnp.zeros((HD, tokens), F32)
    values_t = table_ref[0, :, pl.ds(HD, HD)].T
    for at in range(0, slots, step):
        mine = jnp.where(chosen // step == at // step, chosen % step, -1).astype(F32).astype(BF)
        dense = jnp.zeros((step, tokens), BF)
        for j in range(8):
            dense = jnp.where(rows == mine[j : j + 1], probs[j : j + 1], dense)
        p_ref[0, pl.ds(at, step), :] = dense
        out = out + dot(values_t[:, at : at + step], dense)
        if at + step == slots // 2:
            pause()
    return out.T.astype(BF)


def rows_of(blocks, at, count):
    block = blocks[:, :, pl.ds(at, count)]
    if block.shape[1] % 16:
        block = block.astype(F32)
    return block.reshape(-1, count).astype(BF)


def combined(outs, lses):
    top = functools.reduce(jnp.maximum, lses)
    total = top + jnp.log(sum(jnp.exp(lse - top) for lse in lses))
    shares = [jnp.exp(lse - total).T for lse in lses]
    heads = [
        sum(
            share[:, h : h + 1] * out[:, h * HD : (h + 1) * HD].astype(F32)
            for share, out in zip(shares, outs)
        )
        for h in range(H)
    ]
    return heads, total


def attend_kernel(n_hi, orders, *refs):
    n = len(orders) - 2
    len_ref, near_ref, x_ref, table_ref, slot_ref, kc_ref, vc_ref = refs[:7]
    early_in, late_in, refs = refs[7:9], refs[9 : 9 + n], refs[9 + n :]
    normed_ref, q_ref, kv_ref, norms_ref, lse_ref, p_ref, local_ref, plocal_ref = refs[:8]
    parts_ref, lses_ref, full_q, full_kv = refs[8:12]
    late_out, refs = refs[12 : 11 + n], refs[11 + n :]
    wq, wkv, norms, asked, outs, landed, lses, landed_lses = refs[:8]
    keep_sem, q_send, q_recv, back_send, back_recv, lse_send, lse_recv = refs[8:15]
    sems = refs[15:]
    phase, head = pl.program_id(0), pl.program_id(1)
    tick = phase * H + head
    ticks = 2 * H
    place = Place(n_hi)
    early = Gather(place, orders[:2], early_in, (wq, norms), sems[:3])
    late = Gather(place, orders[2:], late_in, (wkv,) + tuple(late_out), sems[3:])
    rows, width = x_ref.shape
    lanes = pl.ds(pl.multiple_of(head * HD, HD), HD)

    def remote(src, dst, send, recv, to):
        return pltpu.make_async_remote_copy(
            src_ref=src,
            dst_ref=dst,
            send_sem=send,
            recv_sem=recv,
            device_id=place.device(to),
            device_id_type=MESH,
        )

    def ask(slot, to):
        src = q_ref if slot < 3 else asked.at[2]
        return remote(src, asked.at[slot], q_send.at[slot], q_recv.at[slot], to)

    def give(slot, to):
        part = (1, 3, 2)[slot]
        return [
            remote(outs.at[part], landed.at[slot], back_send.at[slot], back_recv.at[slot], to),
            remote(lses.at[part], landed_lses.at[slot], lse_send.at[slot], lse_recv.at[slot], to),
        ]

    def given(slot):
        place.arrived(landed.at[slot], back_recv.at[slot])
        place.arrived(landed_lses.at[slot], lse_recv.at[slot])

    def keep(k):
        return pltpu.make_async_copy((wq, wkv)[k], (full_q, full_kv)[k], keep_sem.at[k])

    @pl.when(tick == 0)
    def _():
        place.greet()
        for a in range(2):
            early.begin(a)
        x = x_ref[...].astype(F32)
        center = x - jnp.mean(x, axis=-1, keepdims=True)
        scaled = center * lax.rsqrt(jnp.mean(center * center, axis=-1, keepdims=True) + EPSILON)
        for hops in early.levels():
            for a in range(2):
                early.level(a, hops)
        for a in range(2):
            early.finish(a)
        keep(0).start()
        share = norms.shape[0] // H
        groups = [
            functools.reduce(jnp.add, [norms[g * share + k].astype(F32) for k in range(share)])
            for g in range(H)
        ]
        norm_rows = jnp.concatenate(groups, axis=1)
        norms_ref[...] = norm_rows
        normed = (scaled * norm_rows[0:1] + norm_rows[2:3]).astype(BF)
        normed_ref[...] = normed
        for at in range(0, width, 256):
            q_ref[:, pl.ds(at, 256)] = dot(normed, rows_of(wq, at, 256)).astype(BF)
        ask(1, ALONG_CORE).start()
        ask(2, ALONG_X).start()
        for a in range(n):
            late.begin(a)
        asked[0] = q_ref[...]
        place.arrived(asked.at[1], q_recv.at[1])

    events = []
    for level, hops in enumerate(late.levels()):
        for a in range(n):
            span = FIRST_SPAN if a == 0 else LAST_SPAN
            stop = FIRST_STOP + (level * n + a) * span // (n * len(late.levels()))
            events.append((min(stop, 4 * ticks - 1 if a == 0 else 12 * H - 1), (a, hops)))

    def pause(part, first=0, end=4 * ticks):
        for at in range(first + part, end, 4):
            mine = [event for stop, event in events if stop == at]
            if mine:

                @pl.when(tick == at // 4)
                def _(mine=mine):
                    for event in mine:
                        late.level(*event)

    @pl.when(tick == H)
    def _():
        for copy in give(0, ALONG_CORE):
            copy.start()
        place.arrived(asked.at[3], q_recv.at[3])

    @pl.when(phase < 2)
    def _():
        pause(0)
        queries = asked[pl.ds(phase * 2, 2), :, lanes].reshape(2 * rows, HD)
        chosen = slot_ref[0]
        scores = pick_scores(queries, table_ref, chosen, lambda: pause(1))

        @pl.when(tick == H - 2)
        def _():
            place.arrived(asked.at[2], q_recv.at[2])
            ask(3, ALONG_CORE).start()

        pause(2)

        def put_lse(row):
            lse_ref[0] = row
            for k in range(2):
                lses[phase * 2 + k, pl.ds(head, 1), :] = row[:, k * rows : (k + 1) * rows]

        out = recall_values(scores, table_ref, chosen, put_lse, p_ref, lambda: pause(3))
        outs[pl.ds(phase * 2, 2), :, lanes] = out.reshape(2, rows, HD)

    @pl.when(tick == ticks)
    def _():
        for copy in give(1, ALONG_CORE):
            copy.start()
        late.finish(0)
        keep(1).start()
        for at in range(0, 2 * width, 256):
            kv_ref[:, pl.ds(at, 256)] = dot(normed_ref[...], rows_of(wkv, at, 256)).astype(BF)
        given(1)
        heads, total = combined((outs[2], landed[1]), (lses[2], landed_lses[1]))
        for h in range(H):
            outs[2, :, pl.ds(h * HD, HD)] = heads[h].astype(BF)
        lses[2] = total
        for copy in give(2, ALONG_X):
            copy.start()

    @pl.when(phase == 2)
    def _():
        for part in range(4):
            pause(part, 4 * ticks, 12 * H)
        fresh = pl.ds(pl.multiple_of(width + head * HD, HD), HD)
        segment_forward(
            len_ref[0],
            near_ref[0],
            q_ref[:, lanes],
            kc_ref[...],
            kv_ref[:, lanes],
            vc_ref[...],
            kv_ref[:, fresh],
            local_ref,
            plocal_ref,
        )

    @pl.when(tick == ticks + H - 1)
    def _():
        given(0)
        given(2)
        for k, (part, lse) in enumerate(
            ((outs[0], lses[0]), (landed[0], landed_lses[0]), (landed[2], landed_lses[2]))
        ):
            parts_ref[k] = part
            lses_ref[k] = lse
        for a in range(1, n):
            late.finish(a)
        for slot, to in ((1, ALONG_CORE), (2, ALONG_X), (3, ALONG_CORE)):
            ask(slot, to).wait_send()
        for slot, to in ((0, ALONG_CORE), (1, ALONG_CORE), (2, ALONG_X)):
            for copy in give(slot, to):
                copy.wait_send()
        for k in range(2):
            keep(k).wait()


def attend(length, near, x, table, chosen, cache, early, late, orders, collective_id):
    n, n_hi = len(late), lax.axis_size("dp") // 2
    devices = n_hi * 8
    (rows, width), slots = x.shape, table.shape[1]
    dma = pltpu.SemaphoreType.DMA
    shape = jax.ShapeDtypeStruct

    def gathered(a):
        return shape((devices,) + a.shape, a.dtype)

    def asked_head(p, h):
        return jnp.where(p < 2, h, H - 1)

    def segment_head(p, h):
        return jnp.where(p < 2, 0, h)

    def column(first=0):
        return pl.BlockSpec((rows, HD), lambda p, h: (0, first + segment_head(p, h)))

    return pl.pallas_call(
        functools.partial(attend_kernel, n_hi, orders),
        grid=(3, H),
        in_specs=[
            SCALARS,
            pl.BlockSpec((1, 1, 2 * NEAR), lambda p, h: (segment_head(p, h), 0, 0)),
            IN_VMEM,
            pl.BlockSpec((1, slots, 2 * HD), lambda p, h: (asked_head(p, h), 0, 0)),
            pl.BlockSpec((1, 8, 2 * rows), lambda p, h: (asked_head(p, h), 0, jnp.minimum(p, 1))),
            column(),
            column(H),
        ]
        + [ANYWHERE] * (2 + n),
        out_specs=[
            IN_VMEM,
            IN_VMEM,
            IN_VMEM,
            IN_VMEM,
            pl.BlockSpec((1, 1, 2 * rows), lambda p, h: (asked_head(p, h), 0, jnp.minimum(p, 1))),
            pl.BlockSpec(
                (1, slots, 2 * rows), lambda p, h: (jnp.minimum(p * H + h, 2 * H - 1), 0, 0)
            ),
            column(),
            pl.BlockSpec((1, 2 * W, W), lambda p, h: (segment_head(p, h), 0, 0)),
            IN_VMEM,
            IN_VMEM,
        ]
        + [ANYWHERE] * (1 + n),
        out_shape=[
            shape((rows, width), BF),
            shape((rows, width), BF),
            shape((rows, 2 * width), BF),
            shape((16, width), F32),
            shape((H, 1, 4 * rows), F32),
            shape((2 * H, slots, 2 * rows), BF),
            shape((rows, width), F32),
            shape((H, 2 * W, W), BF),
            shape((3, rows, width), BF),
            shape((3, H, rows), F32),
            gathered(early[0]),
        ]
        + [gathered(a) for a in late],
        scratch_shapes=[
            pltpu.VMEM((devices,) + early[0].shape, BF),
            pltpu.VMEM((devices,) + late[0].shape, BF),
            pltpu.VMEM((devices,) + early[1].shape, BF),
            pltpu.VMEM((4, rows, width), BF),
            pltpu.VMEM((4, rows, width), BF),
            pltpu.VMEM((3, rows, width), BF),
            pltpu.VMEM((4, H, rows), F32),
            pltpu.VMEM((3, H, rows), F32),
            dma((2,)),
            dma((4,)),
            dma((4,)),
            dma((3,)),
            dma((3,)),
            dma((3,)),
            dma((3,)),
        ]
        + gather_sems(2, n_hi)
        + gather_sems(n, n_hi),
        compiler_params=pltpu.CompilerParams(
            collective_id=collective_id, has_side_effects=True, vmem_limit_bytes=60 << 20
        ),
        cost_estimate=pl.CostEstimate(
            flops=16 * rows * slots * HD * H, bytes_accessed=128 << 20, transcendentals=0
        ),
    )(length, near, x, table, chosen, cache, cache, *early, *late)


def near_buckets():
    distance = np.arange(NEAR)
    exact = BUCKETS // 2
    far = exact + np.floor(
        np.log(np.maximum(distance, 1) / exact) / np.log(128.0 / exact) * exact
    )
    return np.where(distance < exact, distance, np.minimum(far, BUCKETS - 1)).astype(np.int32)


def near_hot():
    return near_buckets()[:, None] == np.arange(BUCKETS)[None, :]


def near_bias(rel_table):
    above = (rel_table - rel_table[-1:])[None]
    rows = jnp.sum(jnp.where(jnp.asarray(near_hot())[:, :, None], above, 0.0), axis=1)
    return jnp.pad(rows.T, ((0, 0), (0, NEAR)))[:, None, :]


def table_gradient(diagonals, totals):
    near = diagonals[:, 0, NEAR - 1 : 2 * NEAR - 1]
    sums = jnp.dot(near, jnp.asarray(near_hot(), F32), precision=HIGHEST)
    far = jnp.sum(totals, axis=(1, 2)) - jnp.sum(near, axis=1)
    return (sums + far[:, None] * (np.arange(BUCKETS) == BUCKETS - 1)).T


def segment_forward(length, near, q, cached_keys, keys, cached_values, values, out_ref, p_ref):
    band = pltpu.roll(
        jnp.broadcast_to(near, (NEAR, 2 * NEAR)), 0, 1, stride=1, stride_axis=0
    )
    key_ids = lax.broadcasted_iota(jnp.int32, (NEAR, NEAR), 0)
    query_ids = lax.broadcasted_iota(jnp.int32, (NEAR, NEAR), 1)
    on_diagonal = jnp.where(query_ids >= key_ids, band[:, :NEAR], NEGATIVE)
    beside = band[:, NEAR:]
    masked = jnp.full((NEAR, NEAR), NEGATIVE, F32)
    zero = jnp.zeros((NEAR, NEAR), F32)
    cache_t, values_t = cached_values.T, values.T
    step = 2 * NEAR
    for at in range(W // step):
        count = 2 * (at + 1)
        queries = q[step * at : step * (at + 1)]
        cached = dot(cached_keys, queries, NT) * SCALE
        if at == 0:
            last = cached[W - NEAR :] + jnp.concatenate([beside, zero], axis=1)
            cached = jnp.concatenate([cached[: W - NEAR], last], axis=0)
        fresh = dot(keys[: NEAR * count], queries, NT) * SCALE
        rows = [cached]
        for k in range(count):
            block = fresh[NEAR * k : NEAR * (k + 1)]
            tiles = [
                masked if q < k else on_diagonal if q == k else beside if q == k + 1 else zero
                for q in (2 * at, 2 * at + 1)
            ]
            if any(tile is not zero for tile in tiles):
                block = block + jnp.concatenate(tiles, axis=1)
            ids = lax.broadcasted_iota(jnp.int32, (NEAR, step), 0) + NEAR * k
            rows.append(jnp.where(ids < length, block, NEGATIVE))
        scores = jnp.concatenate(rows, axis=0)
        weights = jnp.exp(scores - jnp.max(scores, axis=0, keepdims=True))
        probs = (weights * (1.0 / jnp.sum(weights, axis=0, keepdims=True))).astype(BF)
        p_ref[0, pl.ds(0, W + NEAR * count), pl.ds(step * at, step)] = probs
        out = dot(cache_t, probs[:W]) + dot(values_t[:, : NEAR * count], probs[W:])
        out_ref[pl.ds(step * at, step), :] = out.T


def segment_grad(
    g_ref, q_ref, kc_ref, kn_ref, vc_ref, vn_ref, p_ref, put_q, gk_ref, gv_ref, diag_ref, tot_ref
):
    cache_t, keys_t = kc_ref[...].T, kn_ref[...].T
    on_diagonal = jnp.zeros((NEAR, NEAR), F32)
    beside = jnp.zeros((NEAR, NEAR), F32)
    step = 2 * NEAR
    total = jnp.zeros((8, step), F32)
    grad_keys, grad_values = [], []
    for at in range(W // step):
        count = 2 * (at + 1)
        grads = g_ref[pl.ds(step * at, step), :]
        queries = q_ref[pl.ds(step * at, step), :]
        grad_probs = jnp.concatenate(
            [dot(vc_ref[...], grads, NT), dot(vn_ref[pl.ds(0, NEAR * count), :], grads, NT)], axis=0
        )
        probs = p_ref[0, pl.ds(0, W + NEAR * count), pl.ds(step * at, step)]
        wide = probs.astype(F32)
        product = wide * grad_probs
        grad_scores = product - wide * jnp.sum(product, axis=0, keepdims=True)
        low = grad_scores.astype(BF)
        grad_q = dot(cache_t, low[:W]) + dot(keys_t[:, : NEAR * count], low[W:])
        put_q(step * at, (grad_q * SCALE).T)
        grad_keys.append(dot(low[W:], queries) * SCALE)
        grad_values.append(dot(probs[W:], grads))
        if at == 0:
            beside = beside + grad_scores[W - NEAR : W, :NEAR]
        for k in range(count):
            for side, q in enumerate((2 * at, 2 * at + 1)):
                tile = grad_scores[W + NEAR * k : W + NEAR * (k + 1), NEAR * side : NEAR * (side + 1)]
                if q == k:
                    on_diagonal = on_diagonal + tile
                elif q == k + 1:
                    beside = beside + tile
        total = total + jnp.sum(grad_scores.reshape(-1, 8, step), axis=0)
    for ref, (early, late) in ((gk_ref, grad_keys), (gv_ref, grad_values)):
        ref[...] = jnp.concatenate([late[:step] + early, late[step:]], axis=0).astype(BF)
    down = lax.broadcasted_iota(jnp.int32, (NEAR, NEAR), 0)
    across = lax.broadcasted_iota(jnp.int32, (NEAR, NEAR), 1)
    turned = lax.dot_general(
        (down + across == NEAR - 1).astype(F32),
        jnp.concatenate([on_diagonal, beside], axis=1),
        NN,
        precision=HIGHEST,
        preferred_element_type=F32,
    )
    diagonals = pltpu.roll(turned, 0, 1, stride=1, stride_axis=0)
    diag_ref[0] = jnp.sum(diagonals, axis=0, keepdims=True)
    tot_ref[0] = total


def recall_back(grads, table_ref, p_ref, delta, share):
    slots, step = table_ref.shape[1], 512
    keys_t = table_ref[0, :, pl.ds(0, HD)].T
    out = jnp.zeros((HD, grads.shape[0]), F32)
    for at in range(0, slots, step):
        along = dot(table_ref[0, pl.ds(at, step), pl.ds(HD, HD)], grads, NT)
        scores = (along - delta).astype(BF) * p_ref[0, pl.ds(at, step), :]
        out = out + dot(keys_t[:, at : at + step], scores)
    return (out * (share * SCALE)).T.astype(BF)


def attend_grad_kernel(n_hi, orders, *refs):
    n = len(orders)
    grec_ref, aux_ref, glocal_ref, q_ref, kc_ref, kn_ref, vc_ref, vn_ref, plocal_ref = refs[:9]
    table_ref, p_ref, lse_ref = refs[9:12]
    grads_in, rest = refs[12 : 12 + n], refs[12 + n :]
    gq_ref, gk_ref, gv_ref, diag_ref, tot_ref = rest[:5]
    sums_out, rest = rest[5 : 5 + n], rest[5 + n :]
    asked, aux, back, returned, glocal_q = rest[:5]
    ask_send, ask_recv, aux_send, aux_recv, back_send, back_recv = rest[5:11]
    buffers = [rest[11 + k * n : 11 + (k + 1) * n] for k in range(5)]
    place = Place(n_hi)
    scatter = Scatter(place, orders, grads_in, sums_out, buffers, rest[11 + 5 * n :])
    tick = pl.program_id(0)
    ticks = 3 * H
    order = near_first(n_hi)[::-1]

    def remote(src, dst, send, recv, to):
        return pltpu.make_async_remote_copy(
            src_ref=src,
            dst_ref=dst,
            send_sem=send,
            recv_sem=recv,
            device_id=place.device(to),
            device_id_type=MESH,
        )

    def ask(slot, to):
        first = slot < 3
        return [
            remote(
                grec_ref if first else asked.at[2],
                asked.at[slot],
                ask_send.at[slot],
                ask_recv.at[slot],
                to,
            ),
            remote(
                aux_ref if first else aux.at[2],
                aux.at[slot],
                aux_send.at[slot],
                aux_recv.at[slot],
                to,
            ),
        ]

    def asked_arrived(slot):
        place.arrived(asked.at[slot], ask_recv.at[slot])
        place.arrived(aux.at[slot], aux_recv.at[slot])

    def give(slot, to):
        return remote(
            back.at[(1, 3, 2)[slot]], returned.at[slot], back_send.at[slot], back_recv.at[slot], to
        )

    @pl.when(tick == 0)
    def _():
        place.greet()
        for slot, to in ((1, ALONG_CORE), (2, ALONG_X)):
            for copy in ask(slot, to):
                copy.start()
        for z in order:
            for a in range(n):
                scatter.begin(z, a)
        asked[0] = grec_ref[...]
        aux[0] = aux_ref[...]
        asked_arrived(1)

    events = []
    for k in range(n_hi + 2):
        for delay, event in enumerate((scatter.core, scatter.one, scatter.two)):
            if 0 <= k - delay < n_hi:
                events += [functools.partial(event, order[k - delay], a) for a in range(n)]
    for at in range(1, ticks):
        mine = events[len(events) * (at - 1) // (ticks - 1) : len(events) * at // (ticks - 1)]

        @pl.when(tick == at)
        def _(mine=mine):
            for event in mine:
                event()

    @pl.when(tick == H - 2)
    def _():
        asked_arrived(2)
        for copy in ask(3, ALONG_CORE):
            copy.start()

    @pl.when(tick == H)
    def _():
        asked_arrived(3)
        give(0, ALONG_CORE).start()

    @pl.when(tick < 2 * H)
    def _():
        phase = tick // H
        head = tick % H
        lanes = pl.ds(pl.multiple_of(head * HD, HD), HD)
        pair = pl.ds(phase * 2, 2)
        grads = asked[pair, :, lanes].reshape(-1, HD)
        delta = jnp.concatenate([aux[phase * 2 + k, pl.ds(head, 1), :] for k in range(2)], axis=1)
        total = jnp.concatenate(
            [aux[phase * 2 + k, pl.ds(H + head, 1), :] for k in range(2)], axis=1
        )
        share = jnp.exp(lse_ref[0] - total)
        result = recall_back(grads, table_ref, p_ref, delta, share)
        back[pair, :, lanes] = result.reshape(2, -1, HD)

    @pl.when(tick == 2 * H)
    def _():
        give(1, ALONG_CORE).start()

    @pl.when(tick == 2 * H + 1)
    def _():
        place.arrived(returned.at[1], back_recv.at[1])
        back[2] = (back[2].astype(F32) + returned[1].astype(F32)).astype(BF)
        give(2, ALONG_X).start()

    @pl.when(tick >= 2 * H)
    def _():
        lanes = pl.ds(pl.multiple_of((tick - 2 * H) * HD, HD), HD)

        def put_q(at, value):
            glocal_q[pl.ds(at, value.shape[0]), lanes] = value

        segment_grad(
            glocal_ref, q_ref, kc_ref, kn_ref, vc_ref, vn_ref, plocal_ref,
            put_q, gk_ref, gv_ref, diag_ref, tot_ref,
        )

    @pl.when(tick == ticks - 1)
    def _():
        for a in range(n):
            scatter.last(a)
        place.arrived(returned.at[0], back_recv.at[0])
        place.arrived(returned.at[2], back_recv.at[2])
        gq_ref[...] = (
            glocal_q[...]
            + back[0].astype(F32)
            + returned[0].astype(F32)
            + returned[2].astype(F32)
        ).astype(BF)
        scatter.finish()
        for slot, to in ((1, ALONG_CORE), (2, ALONG_X), (3, ALONG_CORE)):
            for copy in ask(slot, to):
                copy.wait_send()
        for slot, to in ((0, ALONG_CORE), (1, ALONG_CORE), (2, ALONG_X)):
            give(slot, to).wait_send()


def attend_grad(
    grad_recalled, aux, grad_local, queries, keys_values, cache, probs_local, table, probs, lses,
    grads, orders, collective_id,
):
    n, n_hi = len(grads), lax.axis_size("dp") // 2
    (rows, width), slots = queries.shape, table.shape[1]
    shapes = [g.shape[1:] for g in grads]
    dma = pltpu.SemaphoreType.DMA

    def column(first=0):
        return pl.BlockSpec((rows, HD), lambda t: (0, first + segment_head(t)))

    def head(*shape):
        return pl.BlockSpec((1,) + shape, lambda t: (segment_head(t),) + (0,) * len(shape))

    def segment_head(t):
        return jnp.maximum(t - 2 * H, 0)

    def asked(t):
        return jnp.minimum(t, 2 * H - 1)

    return pl.pallas_call(
        functools.partial(attend_grad_kernel, n_hi, orders),
        grid=(3 * H,),
        in_specs=[
            IN_VMEM,
            IN_VMEM,
            column(),
            column(),
            column(),
            column(),
            column(H),
            column(H),
            head(2 * W, W),
            pl.BlockSpec((1, slots, 2 * HD), lambda t: (asked(t) % H, 0, 0)),
            pl.BlockSpec((1, slots, 2 * rows), lambda t: (asked(t), 0, 0)),
            pl.BlockSpec((1, 1, 2 * rows), lambda t: (asked(t) % H, 0, asked(t) // H)),
        ]
        + [ANYWHERE] * n,
        out_specs=[IN_VMEM, column(), column(), head(1, 2 * NEAR), head(8, 2 * NEAR)]
        + [IN_VMEM] * n,
        out_shape=[
            jax.ShapeDtypeStruct((rows, width), BF),
            jax.ShapeDtypeStruct((rows, width), BF),
            jax.ShapeDtypeStruct((rows, width), BF),
            jax.ShapeDtypeStruct((H, 1, 2 * NEAR), F32),
            jax.ShapeDtypeStruct((H, 8, 2 * NEAR), F32),
        ]
        + [jax.ShapeDtypeStruct(shape, F32) for shape in shapes],
        scratch_shapes=[
            pltpu.VMEM((4, rows, width), BF),
            pltpu.VMEM((4,) + aux.shape, F32),
            pltpu.VMEM((4, rows, width), BF),
            pltpu.VMEM((3, rows, width), BF),
            pltpu.VMEM((rows, width), F32),
        ]
        + [dma((4,))] * 4
        + [dma((3,))] * 2
        + scatter_buffers(shapes, n_hi)
        + scatter_sems(n, n_hi),
        compiler_params=pltpu.CompilerParams(
            collective_id=collective_id, has_side_effects=True, vmem_limit_bytes=62 << 20
        ),
        cost_estimate=pl.CostEstimate(
            flops=16 * rows * slots * HD * H, bytes_accessed=128 << 20, transcendentals=0
        ),
    )(
        grad_recalled, aux, grad_local, queries, cache, keys_values, cache, keys_values,
        probs_local, table, probs, lses, *grads,
    )


def feed_kernel(
    parts_ref, lse_ref, local_ref, x_ref, cot_ref, gate_ref, norms_ref, wo_ref, up_ref, down_ref,
    out_ref, gatt_ref, gwo_ref, gup_ref, gdown_ref, glocal_ref, grec_ref, aux_ref, sums_ref,
    recalled, mixed_t, attended, scaled, inverse, normed, normed_t, acc, gacc,
):
    step, last = pl.program_id(0), pl.num_programs(0) - 1
    rows, width = x_ref.shape
    gate = gate_ref[...]

    @pl.when(step == 0)
    def _():
        heads, total = combined([parts_ref[k] for k in range(3)], [lse_ref[k] for k in range(3)])
        aux_ref[H:, :] = total
        for h in range(H):
            recalled[:, pl.ds(h * HD, HD)] = heads[h]
        mixed = (gate * recalled[...] + (1.0 - gate) * local_ref[...]).astype(BF)
        mixed_t[...] = mixed.T
        here = x_ref[...].astype(F32) + dot(mixed, wo_ref[...])
        attended[...] = here
        center = here - jnp.mean(here, axis=-1, keepdims=True)
        inv = lax.rsqrt(jnp.mean(center * center, axis=-1, keepdims=True) + EPSILON)
        inverse[...] = inv
        scaled[...] = center * inv
        n2 = (scaled[...] * norms_ref[1:2] + norms_ref[3:4]).astype(BF)
        normed[...] = n2
        normed_t[...] = n2.T
        acc[...] = jnp.zeros(acc.shape, F32)
        gacc[...] = jnp.zeros(gacc.shape, F32)

    up = dot(normed[...], up_ref[...])
    root = np.sqrt(2 / np.pi).astype(np.float32)
    square = up * up
    bend = jnp.tanh(root * (up + 0.044715 * (square * up)))
    hidden = (0.5 * up * (1.0 + bend)).astype(BF)
    slope = 0.5 * (1.0 + bend) + 0.5 * up * (1.0 - bend * bend) * (
        root * (1.0 + (3 * 0.044715) * square)
    )
    grad_up = (dot(cot_ref[...], down_ref[...], NT) * slope).astype(BF)
    acc[...] += dot(hidden, down_ref[...])
    gacc[...] += dot(grad_up, up_ref[...], NT)
    gdown_ref[...] = dot(hidden.T, cot_ref[...]).astype(BF)
    gup_ref[...] = dot(normed_t[...], grad_up).astype(BF)

    @pl.when(step == last)
    def _():
        out_ref[...] = (attended[...] + acc[...]).astype(BF)
        grad = gacc[...]
        sums_ref[0:1] = jnp.sum(grad * scaled[...], axis=0, keepdims=True)
        sums_ref[1:2] = jnp.sum(grad, axis=0, keepdims=True)
        grad = grad * norms_ref[1:2]
        mean_grad = jnp.mean(grad, axis=-1, keepdims=True)
        mean_cross = jnp.mean(grad * scaled[...], axis=-1, keepdims=True)
        grad = cot_ref[...].astype(F32) + inverse[...] * (
            grad - mean_grad - scaled[...] * mean_cross
        )
        gatt_ref[...] = grad
        low = grad.astype(BF)
        gwo_ref[...] = dot(mixed_t[...], low).astype(BF)
        gmixed = dot(low, wo_ref[...], NT)
        sums_ref[2:3] = jnp.sum(gmixed * (recalled[...] - local_ref[...]), axis=0, keepdims=True)
        sums_ref[3:] = jnp.zeros((5, width), F32)
        glocal_ref[...] = ((1.0 - gate) * gmixed).astype(BF)
        grec = (gate * gmixed).astype(BF)
        grec_ref[...] = grec
        product = grec.astype(F32) * recalled[...]
        delta = [
            jnp.sum(product[:, h * HD : (h + 1) * HD], axis=1, keepdims=True) for h in range(H)
        ]
        aux_ref[:H, :] = jnp.concatenate(delta, axis=1).T


def feed(parts, lses, local_out, x, cotangent, gate_row, norm_rows, w_out, w_up, w_down):
    rows, width = x.shape
    hidden = w_up.shape[1]
    block = 512
    full = jax.ShapeDtypeStruct
    return pl.pallas_call(
        feed_kernel,
        grid=(hidden // block,),
        in_specs=[IN_VMEM] * 8
        + [
            pl.BlockSpec((width, block), lambda k: (0, k)),
            pl.BlockSpec((block, width), lambda k: (k, 0)),
        ],
        out_specs=[IN_VMEM] * 3
        + [
            pl.BlockSpec((width, block), lambda k: (0, k)),
            pl.BlockSpec((block, width), lambda k: (k, 0)),
        ]
        + [IN_VMEM] * 4,
        out_shape=[
            full((rows, width), BF),
            full((rows, width), F32),
            full((width, width), BF),
            full((width, hidden), BF),
            full((hidden, width), BF),
            full((rows, width), BF),
            full((rows, width), BF),
            full((2 * H, rows), F32),
            full((8, width), F32),
        ],
        scratch_shapes=[
            pltpu.VMEM((rows, width), F32),
            pltpu.VMEM((width, rows), BF),
            pltpu.VMEM((rows, width), F32),
            pltpu.VMEM((rows, width), F32),
            pltpu.VMEM((rows, 1), F32),
            pltpu.VMEM((rows, width), BF),
            pltpu.VMEM((width, rows), BF),
            pltpu.VMEM((rows, width), F32),
            pltpu.VMEM((rows, width), F32),
        ],
        compiler_params=pltpu.CompilerParams(vmem_limit_bytes=56 << 20),
        cost_estimate=pl.CostEstimate(
            flops=12 * rows * width * hidden, bytes_accessed=36 << 20, transcendentals=0
        ),
    )(parts, lses, local_out, x, cotangent, gate_row, norm_rows, w_out, w_up, w_down)


def norm_forward(values, gain_row, shift_row):
    center = values - jnp.mean(values, axis=-1, keepdims=True)
    inverse = lax.rsqrt(jnp.mean(center * center, axis=-1, keepdims=True) + EPSILON)
    scaled = center * inverse
    return (scaled * gain_row + shift_row, scaled, inverse)


def norm_backward(grad_normed, scaled, inverse, gain_row):
    grad_scaled = grad_normed * gain_row
    mean_grad = jnp.mean(grad_scaled, axis=-1, keepdims=True)
    mean_cross = jnp.mean(grad_scaled * scaled, axis=-1, keepdims=True)
    return inverse * (grad_scaled - mean_grad - scaled * mean_cross)


def local(
    tokens,
    norm_gains,
    norm_shifts,
    w_qkv,
    w_out,
    w_up,
    w_down,
    rel_table,
    gate_bias,
    xl_cache,
    memory,
    slot_index,
    seg_len,
    cotangent,
):
    width = tokens.shape[1]
    count = tokens.shape[0]
    slot_count = memory.shape[0]
    groups = lax.axis_size("mem")
    me = lax.axis_index("mem")

    devices = lax.axis_size("dp") * groups
    number = lax.axis_index("dp") * groups + me
    own = norm_gains.shape[1]
    norms = jnp.pad(
        jnp.concatenate([norm_gains, norm_shifts], axis=0), ((0, 12), (0, 128 - own))
    )
    norms = jnp.roll(norms, number % (128 // own) * own, axis=1)
    table = memory.transpose(1, 0, 2)
    slot_rows = (slot_index - me * slot_count).reshape(groups, count, H, -1)
    picks = [
        lax.dynamic_index_in_dim(slot_rows, me ^ turn, 0, keepdims=False) for turn in range(groups)
    ]
    chosen = jnp.stack(picks).transpose(2, 3, 0, 1).reshape(H, -1, groups * count)
    (
        normed_one,
        queries,
        keys_values,
        norm_rows,
        lse_all,
        probs_all,
        local_out,
        probs_local,
        parts,
        lses,
        *full,
    ) = attend(
        seg_len,
        near_bias(rel_table),
        tokens,
        table,
        chosen,
        xl_cache,
        (w_qkv[:, :width], norms),
        (w_qkv[:, width:], w_out, w_up, w_down),
        ("zyx", "zxy", "xyz", "xyz", "zyx", "zxy"),
        0,
    )
    full_q, full_kv, full_out, full_up, full_down = [f.reshape(-1, f.shape[2]) for f in full]
    gain_rows, shift_rows = norm_rows[:2], norm_rows[2:4]

    inputs = tokens.astype(F32)
    _, scaled_one, inverse_one = norm_forward(inputs, gain_rows[0], shift_rows[0])
    gate_open = jax.nn.sigmoid(gate_bias)
    output, grad_attended, grad_wout, grad_up, grad_down, grad_local, grad_recalled, aux, sums = feed(
        parts,
        lses,
        local_out,
        tokens,
        cotangent,
        jnp.repeat(gate_open, HD)[None],
        norm_rows,
        full_out,
        full_up,
        full_down,
    )
    grad_gate = jnp.sum(sums[2].reshape(H, HD), axis=1) * gate_open * (1.0 - gate_open)
    grad_query, grad_keys, grad_values, diagonals, totals, share_out, share_up, share_down = attend_grad(
        grad_recalled,
        aux,
        grad_local,
        queries,
        keys_values,
        xl_cache,
        probs_local,
        table,
        probs_all,
        lse_all,
        [g.reshape(devices, -1, g.shape[1]) for g in (grad_wout, grad_up, grad_down)],
        ("yxz", "yxz", "xyz"),
        1,
    )
    grad_table = table_gradient(diagonals, totals)
    grad_qkv_low = jnp.concatenate([grad_query, grad_keys, grad_values], axis=1)
    grad_wqkv = jnp.einsum("td,te->de", normed_one, grad_qkv_low, preferred_element_type=F32)
    grad_normed_one = dot(grad_qkv_low[:, :width], full_q, NT) + dot(
        grad_qkv_low[:, width:], full_kv, NT
    )
    grad_tokens = grad_attended + norm_backward(
        grad_normed_one, scaled_one, inverse_one, gain_rows[0]
    )
    grad_norms = jnp.stack(
        [
            jnp.sum(grad_normed_one * scaled_one, axis=0),
            sums[0],
            jnp.sum(grad_normed_one, axis=0),
            sums[1],
        ]
    )
    rest = jnp.pad(jnp.concatenate([grad_table.reshape(-1), grad_gate]), (0, 1024 - 264))
    small = jnp.concatenate([grad_norms.reshape(-1, 128), rest.reshape(-1, 128)], axis=0)
    half = grad_wqkv.shape[1] // 2
    share_left, share_right, small = scatter_sums(
        [
            g.astype(BF).reshape(devices, -1, half)
            for g in (grad_wqkv[:, :half], grad_wqkv[:, half:])
        ],
        ("yxz", "xyz"),
        small,
        2,
    )
    share_qkv = jnp.concatenate([share_left, share_right], axis=1)
    share_norms = lax.dynamic_slice_in_dim(
        small[:32].reshape(4, width), number * own, own, axis=1
    )
    rest = small[32:].reshape(-1)
    table_total, gate_total = rest[: BUCKETS * H].reshape(BUCKETS, H), rest[BUCKETS * H :][:H]
    return (
        output,
        grad_tokens,
        share_norms[:2],
        share_norms[2:],
        share_qkv,
        share_out,
        share_up,
        share_down,
        table_total,
        gate_total,
    )


def solution(mesh):
    shard = P(AXES, None)
    placed = (
        shard,
        P(None, AXES),
        P(None, AXES),
        shard,
        shard,
        shard,
        shard,
        P(),
        P(),
        shard,
        P(AXES, None, None),
        P("dp", None, "mem"),
        P(AXES),
        shard,
    )
    return jax.shard_map(
        local,
        mesh=mesh,
        in_specs=placed,
        out_specs=(
            shard,
            shard,
            P(None, AXES),
            P(None, AXES),
            shard,
            shard,
            shard,
            shard,
            P(),
            P(),
        ),
        check_vma=False,
    )
```

```python
import functools

import jax
import jax.numpy as jnp
import numpy as np
from jax import lax
from jax.experimental import pallas as pl
from jax.experimental.pallas import tpu as pltpu
from jax.sharding import PartitionSpec as P

H = 8
HD = 128
W = 512
BUCKETS = 32
NEAR = 128
EPSILON = 1e-05
NEGATIVE = -1e30
SCALE = HD ** (-0.5)
AXES = ("dp", "mem")
MESH = pl.DeviceIdType.MESH
HIGHEST = lax.Precision.HIGHEST
BF = jnp.bfloat16
F32 = jnp.float32
NT = (((1,), (1,)), ((), ()))
NN = (((1,), (0,)), ((), ()))


def dot(left, right, dims=NN):
    return lax.dot_general(left, right, dims, preferred_element_type=F32)


OWN, ALONG_Y, ALONG_X, ALONG_CORE = (0, 0, 0, 0), (0, 1, 0, 0), (0, 0, 1, 0), (0, 0, 0, 1)
ANYWHERE = pl.BlockSpec(memory_space=pl.ANY)
IN_VMEM = pl.BlockSpec(memory_space=pltpu.VMEM)
SCALARS = pl.BlockSpec(memory_space=pltpu.SMEM)


class Place:
    def __init__(self, n_hi):
        self.sizes = (n_hi, 2, 2, 2)
        dp, mem = lax.axis_index("dp"), lax.axis_index("mem")
        self.at = (dp // 2, dp % 2, mem // 2, mem % 2)

    def device(self, step):
        z, y, x, core = [(a + s) % n for a, s, n in zip(self.at, step, self.sizes)]
        return (z * 2 + y, x * 2 + core)

    def number(self, step):
        dp, mem = self.device(step)
        return dp * 4 + mem

    def plus(self, left, right):
        return tuple((a + b) % n for a, b, n in zip(left, right, self.sizes))

    def minus(self, left, right):
        return tuple((a - b) % n for a, b, n in zip(left, right, self.sizes))

    def partners(self):
        return [(z, 0, 0, 0) for z in range(1, self.sizes[0])] + [ALONG_Y, ALONG_X, ALONG_CORE]

    def greet(self):
        barrier = pltpu.get_barrier_semaphore()
        for partner in self.partners():
            pl.semaphore_signal(
                barrier, inc=1, device_id=self.device(partner), device_id_type=MESH
            )
        pl.semaphore_wait(barrier, len(self.partners()))

    def arrived(self, ref, recv):
        pltpu.make_async_remote_copy(
            src_ref=ref,
            dst_ref=ref,
            send_sem=recv,
            recv_sem=recv,
            device_id=self.device(ALONG_CORE),
            device_id_type=MESH,
        ).wait_recv()


def near_first(n_hi):
    order = [0]
    for z in range(1, n_hi // 2 + 1):
        order += [k for k in dict.fromkeys((z, n_hi - z)) if k < n_hi]
    return order


class Gather:
    LEFT, RIGHT, Y, X, CORE = "left", "right", ALONG_Y, ALONG_X, ALONG_CORE

    def __init__(self, place, orders, ins, outs, sems):
        self.place, self.ins, self.outs = place, ins, outs
        self.send_sem, self.recv_sem, self.own_sem = sems
        self.n = len(orders)
        self.orders = [["zyx".index(axis) for axis in order] for order in orders]
        self.sent = [[] for _ in orders]

    def exists(self, steps):
        z, n = self.place.at[0], self.place.sizes[0]
        return z + steps >= 0 if steps < 0 else z + steps < n

    def device(self, to):
        z, y, x, core = self.place.at
        if to in (self.LEFT, self.RIGHT):
            return ((z + (1 if to == self.RIGHT else -1)) * 2 + y, x * 2 + core)
        return self.place.device(to)

    def spot(self, a, source):
        z, y, x, core = self.place.at
        dp = (z + source[0]) * 2 + (y + source[1]) % 2
        return self.outs[a].at[dp * 4 + (x + source[2]) % 2 * 2 + (core + source[3]) % 2]

    def recv(self, a, source, to=None):
        z = self.place.at[0] + source[0]
        rest = list(source[1:])
        if to is not None and to not in (self.LEFT, self.RIGHT):
            rest = [(have - step) % 2 for have, step in zip(rest, to[1:])]
        return self.recv_sem.at[a, ((z * 2 + rest[0]) * 2 + rest[1]) * 2 + rest[2]]

    def copy(self, a, k):
        source, to = self.sent[a][k]
        return pltpu.make_async_remote_copy(
            src_ref=self.ins[a] if source == OWN else self.spot(a, source),
            dst_ref=self.spot(a, source),
            send_sem=self.send_sem.at[a, k],
            recv_sem=self.recv(a, source, to),
            device_id=self.device(to),
            device_id_type=MESH,
        )

    def when(self, conditions, run):
        conditions = [c for c in conditions if c is not None]
        if conditions:
            pl.when(functools.reduce(jnp.logical_and, conditions))(run)
        else:
            run()

    def limits(self, source, to):
        ends = {self.LEFT: -1, self.RIGHT: 1}
        return [
            self.exists(source[0]) if source[0] else None,
            self.exists(ends[to]) if to in ends else None,
        ]

    def send(self, a, source, to):
        self.sent[a].append((source, to))
        k = len(self.sent[a]) - 1
        self.when(self.limits(source, to)[1:], lambda: self.copy(a, k).start())

    def own(self, a):
        return pltpu.make_async_copy(self.ins[a], self.spot(a, OWN), self.own_sem.at[a])

    def arrived(self, a, source):
        self.place.arrived(self.spot(a, source), self.recv(a, source))

    def onward(self, a, source):
        order = self.orders[a]
        came = max([order.index(axis) for axis in range(3) if source[axis]], default=-1)
        to = []
        if came >= 0 and order[came] == 0:
            to.append(self.RIGHT if source[0] < 0 else self.LEFT)
        for axis in order[came + 1 :]:
            to += ((self.LEFT, self.RIGHT), (self.Y,), (self.X,))[axis]
        return to + [self.CORE]

    def begin(self, a):
        for to in self.onward(a, OWN):
            self.send(a, OWN, to)
        self.own(a).start()

    def level(self, a, hops):
        for rest in ((0, 0), (1, 0), (0, 1), (1, 1)):
            distance = hops - sum(rest)
            if not 0 <= distance < self.place.sizes[0]:
                continue
            for steps in dict.fromkeys((-distance, distance)):

                def run(source=(steps,) + rest + (0,)):
                    self.arrived(a, source)
                    for to in self.onward(a, source):
                        self.send(a, source, to)

                self.when([self.exists(steps) if steps else None], run)

    def levels(self):
        return range(1, self.place.sizes[0] + 2)

    def finish(self, a):
        place = self.place
        for z in range(place.sizes[0]):
            for y in range(2):
                for x in range(2):
                    source = (z - place.at[0], y, x, 1)
                    place.arrived(self.spot(a, source), self.recv(a, source))
        for k in range(len(self.sent[a])):
            self.when(self.limits(*self.sent[a][k]), lambda k=k: self.copy(a, k).wait_send())
        self.own(a).wait()


def gather_sems(n, n_hi):
    sends = 5 + (8 * n_hi - 5) * 4
    dma = pltpu.SemaphoreType.DMA
    return [dma((n, sends)), dma((n, n_hi * 8)), dma((n,))]


def piece_width(columns):
    return next(w for w in (1024, 768, 512, 384, 256, 128) if columns % w == 0)


class Scatter:
    def __init__(self, place, orders, ins, outs, buffers, sems, small=None):
        self.place, self.ins, self.outs = place, ins, outs
        self.accs, self.from_core, self.from_first, self.from_second, self.from_z = buffers
        (
            self.load_sem,
            self.core_send,
            self.core_recv,
            self.first_send,
            self.first_recv,
            self.second_send,
            self.second_recv,
            self.z_send,
            self.z_recv,
        ) = sems[:9]
        self.small = small
        self.small_sems = sems[9:]
        self.n = len(orders)
        self.n_hi = place.sizes[0]
        self.first = [ALONG_X if order == "xyz" else ALONG_Y for order in orders]
        self.second = [ALONG_Y if order == "xyz" else ALONG_X for order in orders]
        self.started = []

    def step(self, a, z, two, one):
        y, x = (two, one) if self.second[a] == ALONG_Y else (one, two)
        return (z, y, x, 0)

    def send(self, ends, device):
        def build():
            src, dst, send, recv = ends()
            return pltpu.make_async_remote_copy(
                src_ref=src,
                dst_ref=dst,
                send_sem=send,
                recv_sem=recv,
                device_id=device(),
                device_id_type=MESH,
            )

        build().start()
        self.started.append(build)

    def load(self, a, z, two, one):
        s = (z * 2 + two) * 2 + one
        return pltpu.make_async_copy(
            self.ins[a].at[self.place.number(self.step(a, z, two, one))],
            self.accs[a].at[s],
            self.load_sem.at[a, s],
        )

    def begin(self, z, a):
        for two, one in ((1, 1), (0, 1), (1, 0), (0, 0)):
            s = (z * 2 + two) * 2 + one
            step = self.step(a, z, two, one)[:3] + (1,)
            self.send(
                lambda s=s, step=step: (
                    self.ins[a].at[self.place.number(step)],
                    self.from_core[a].at[s],
                    self.core_send.at[a, s],
                    self.core_recv.at[a, s],
                ),
                lambda: self.place.device(ALONG_CORE),
            )
            self.load(a, z, two, one).start()

    def add(self, acc, got):
        width = piece_width(acc.shape[1])

        def piece(k, carry):
            at = pl.ds(pl.multiple_of(k * width, width), width)
            acc[:, at] = (acc[:, at].astype(F32) + got[:, at].astype(F32)).astype(BF)
            return carry

        lax.fori_loop(0, acc.shape[1] // width, piece, 0)

    def core(self, z, a):
        for two, one in ((1, 1), (0, 1), (1, 0), (0, 0)):
            k = z * 2 + two
            s = k * 2 + one
            self.load(a, z, two, one).wait()
            self.place.arrived(self.from_core[a].at[s], self.core_recv.at[a, s])
            self.add(self.accs[a].at[s], self.from_core[a].at[s])
            if one:
                self.send(
                    lambda s=s, k=k: (
                        self.accs[a].at[s],
                        self.from_first[a].at[k],
                        self.first_send.at[a, k],
                        self.first_recv.at[a, k],
                    ),
                    lambda: self.place.device(self.first[a]),
                )

    def one(self, z, a):
        for two in (1, 0):
            k = z * 2 + two
            acc = self.accs[a].at[k * 2]
            self.place.arrived(self.from_first[a].at[k], self.first_recv.at[a, k])
            self.add(acc, self.from_first[a].at[k])
            if two:
                self.send(
                    lambda k=k: (
                        self.accs[a].at[k * 2],
                        self.from_second[a].at[z],
                        self.second_send.at[a, z],
                        self.second_recv.at[a, z],
                    ),
                    lambda: self.place.device(self.second[a]),
                )

    def two(self, z, a):
        acc = self.accs[a].at[z * 4]
        self.place.arrived(self.from_second[a].at[z], self.second_recv.at[a, z])
        self.add(acc, self.from_second[a].at[z])
        if z:
            self.send(
                lambda: (
                    self.accs[a].at[z * 4],
                    self.from_z[a].at[z - 1],
                    self.z_send.at[a, z - 1],
                    self.z_recv.at[a, z - 1],
                ),
                lambda: self.place.device((z, 0, 0, 0)),
            )

    def last(self, a):
        for z in range(1, self.n_hi):
            self.place.arrived(self.from_z[a].at[z - 1], self.z_recv.at[a, z - 1])
        out, acc, got = self.outs[a], self.accs[a].at[0], self.from_z[a]
        width = piece_width(out.shape[1])

        def piece(k, carry):
            at = pl.ds(pl.multiple_of(k * width, width), width)
            total = acc[:, at].astype(F32)
            for z in range(1, self.n_hi):
                total = total + got[z - 1, :, at].astype(F32)
            out[:, at] = total
            return carry

        lax.fori_loop(0, out.shape[1] // width, piece, 0)

    def small_steps(self):
        return [ALONG_CORE, ALONG_X, ALONG_Y] + [1 << k for k in range((self.n_hi - 1).bit_length())]

    def small_begin(self):
        source, total, _ = self.small
        total[...] = source[...]
        self.small_send(0)

    def small_device(self, k):
        step = self.small_steps()[k]
        z, y, x, core = self.place.at
        if isinstance(step, int):
            return ((z + step - 2 * step * ((z // step) % 2)) * 2 + y, x * 2 + core)
        return self.place.device(step)

    def small_send(self, k):
        _, total, buffer = self.small
        buffer[0, k] = total[...]
        send, recv = self.small_sems
        self.send(
            lambda: (buffer.at[0, k], buffer.at[1, k], send.at[k], recv.at[k]),
            lambda: self.small_device(k),
        )

    def small_next(self, k):
        _, total, buffer = self.small
        self.place.arrived(buffer.at[1, k], self.small_sems[1].at[k])
        total[...] = total[...] + buffer[1, k]
        if k + 1 < len(self.small_steps()):
            self.small_send(k + 1)

    def finish(self):
        for build in self.started:
            build().wait_send()


def scatter_buffers(shapes, n_hi):
    counts = (n_hi * 4, n_hi * 4, n_hi * 2, n_hi, n_hi - 1)
    return [pltpu.VMEM((count,) + shape, BF) for count in counts for shape in shapes]


def scatter_sems(n, n_hi):
    counts = (n_hi * 4,) * 3 + (n_hi * 2,) * 2 + (n_hi,) * 2 + (n_hi - 1,) * 2
    return [pltpu.SemaphoreType.DMA((n, count)) for count in counts]


FIRST_STOP, FIRST_SPAN, LAST_SPAN, STOP_EVERY = 2, 60, 88, 2


def pick_scores(queries, table_ref, chosen, pause):
    slots, step = table_ref.shape[1], 256
    low, high = chosen & 7, chosen >> 3
    picked = jnp.zeros(chosen.shape, F32)
    for at in range(0, slots, step):
        scores = dot(table_ref[0, pl.ds(at, step), pl.ds(0, HD)], queries, NT)
        for row in range(0, step, 8):
            got = jnp.take_along_axis(scores[row : row + 8], low, axis=0)
            picked = jnp.where(high == (at + row) // 8, got, picked)
        if at + step == slots // 2:
            pause()
    return picked * SCALE


def recall_values(scores, table_ref, chosen, put_lse, p_ref, pause):
    slots, tokens, step = table_ref.shape[1], chosen.shape[1], 256
    top = jnp.max(scores, axis=0, keepdims=True)
    weights = jnp.exp(scores - top)
    total = jnp.sum(weights, axis=0, keepdims=True)
    put_lse(top + jnp.log(total))
    times = jnp.ones_like(weights)
    for turn in range(1, 8):
        times = times + jnp.where(pltpu.roll(chosen, turn, 0) == chosen, 1.0, 0.0)
    probs = (weights / total * times).astype(BF)
    rows = lax.broadcasted_iota(jnp.int32, (step, tokens), 0).astype(F32).astype(BF)
    out = jnp.zeros((HD, tokens), F32)
    values_t = table_ref[0, :, pl.ds(HD, HD)].T
    for at in range(0, slots, step):
        mine = jnp.where(chosen // step == at // step, chosen % step, -1).astype(F32).astype(BF)
        dense = jnp.zeros((step, tokens), BF)
        for j in range(8):
            dense = jnp.where(rows == mine[j : j + 1], probs[j : j + 1], dense)
        p_ref[0, pl.ds(at, step), :] = dense
        out = out + dot(values_t[:, at : at + step], dense)
        if at + step == slots // 2:
            pause()
    return out.T.astype(BF)


def rows_of(blocks, at, count):
    block = blocks[:, :, pl.ds(at, count)]
    if block.shape[1] % 16:
        block = block.astype(F32)
    return block.reshape(-1, count).astype(BF)


def combined(outs, lses):
    top = functools.reduce(jnp.maximum, lses)
    total = top + jnp.log(sum(jnp.exp(lse - top) for lse in lses))
    shares = [jnp.exp(lse - total).T for lse in lses]
    heads = [
        sum(
            share[:, h : h + 1] * out[:, h * HD : (h + 1) * HD].astype(F32)
            for share, out in zip(shares, outs)
        )
        for h in range(H)
    ]
    return heads, total


def attend_kernel(n_hi, orders, *refs):
    n = len(orders) - 2
    len_ref, near_ref, x_ref, table_ref, slot_ref, kc_ref, vc_ref = refs[:7]
    rows, width = x_ref.shape
    w_qkv, refs = refs[7], refs[8:]
    early_in = (w_qkv.at[:, pl.ds(0, width)], refs[0])
    late_in = (w_qkv.at[:, pl.ds(width, 2 * width)],) + tuple(refs[1:n])
    refs = refs[n:]
    normed_ref, q_ref, kv_ref, norms_ref, lse_ref, p_ref, local_ref, plocal_ref = refs[:8]
    parts_ref, lses_ref, full_q, full_kv = refs[8:12]
    late_out, refs = refs[12 : 11 + n], refs[11 + n :]
    wq, wkv, norms, asked, outs, landed, lses, landed_lses = refs[:8]
    keep_sem, q_send, q_recv, back_send, back_recv, lse_send, lse_recv = refs[8:15]
    sems = refs[15:]
    phase, head = pl.program_id(0), pl.program_id(1)
    tick = phase * H + head
    ticks = 2 * H
    place = Place(n_hi)
    early = Gather(place, orders[:2], early_in, (wq, norms), sems[:3])
    late = Gather(place, orders[2:], late_in, (wkv,) + tuple(late_out), sems[3:])
    lanes = pl.ds(pl.multiple_of(head * HD, HD), HD)

    def remote(src, dst, send, recv, to):
        return pltpu.make_async_remote_copy(
            src_ref=src,
            dst_ref=dst,
            send_sem=send,
            recv_sem=recv,
            device_id=place.device(to),
            device_id_type=MESH,
        )

    def ask(slot, to):
        src = q_ref if slot < 3 else asked.at[2]
        return remote(src, asked.at[slot], q_send.at[slot], q_recv.at[slot], to)

    def give(slot, to):
        part = (1, 3, 2)[slot]
        return [
            remote(outs.at[part], landed.at[slot], back_send.at[slot], back_recv.at[slot], to),
            remote(lses.at[part], landed_lses.at[slot], lse_send.at[slot], lse_recv.at[slot], to),
        ]

    def given(slot):
        place.arrived(landed.at[slot], back_recv.at[slot])
        place.arrived(landed_lses.at[slot], lse_recv.at[slot])

    def keep(k):
        return pltpu.make_async_copy((wq, wkv)[k], (full_q, full_kv)[k], keep_sem.at[k])

    @pl.when(tick == 0)
    def _():
        place.greet()
        for a in range(2):
            early.begin(a)
        x = x_ref[...].astype(F32)
        center = x - jnp.mean(x, axis=-1, keepdims=True)
        scaled = center * lax.rsqrt(jnp.mean(center * center, axis=-1, keepdims=True) + EPSILON)
        for hops in early.levels():
            for a in range(2):
                early.level(a, hops)
        for a in range(2):
            early.finish(a)
        keep(0).start()
        share = norms.shape[0] // H
        groups = [
            functools.reduce(jnp.add, [norms[g * share + k].astype(F32) for k in range(share)])
            for g in range(H)
        ]
        norm_rows = jnp.concatenate(groups, axis=1)
        norms_ref[...] = norm_rows
        normed = (scaled * norm_rows[0:1] + norm_rows[2:3]).astype(BF)
        normed_ref[...] = normed
        for at in range(0, width, 256):
            q_ref[:, pl.ds(at, 256)] = dot(normed, rows_of(wq, at, 256)).astype(BF)
        ask(1, ALONG_CORE).start()
        ask(2, ALONG_X).start()
        for a in range(n):
            late.begin(a)
        asked[0] = q_ref[...]
        place.arrived(asked.at[1], q_recv.at[1])

    events = []
    for level, hops in enumerate(late.levels()):
        for a in range(n):
            span = FIRST_SPAN if a == 0 else LAST_SPAN
            stop = FIRST_STOP + (level * n + a) * span // (n * len(late.levels()))
            stop = stop // STOP_EVERY * STOP_EVERY
            events.append((min(stop, 4 * ticks - 1 if a == 0 else 12 * H - 1), (a, hops)))

    def pause(part, first=0, end=4 * ticks):
        for at in range(first + part, end, 4):
            mine = [event for stop, event in events if stop == at]
            if mine:

                @pl.when(tick == at // 4)
                def _(mine=mine):
                    for event in mine:
                        late.level(*event)

    @pl.when(tick == H)
    def _():
        for copy in give(0, ALONG_CORE):
            copy.start()
        place.arrived(asked.at[3], q_recv.at[3])

    @pl.when(phase < 2)
    def _():
        pause(0)
        queries = asked[pl.ds(phase * 2, 2), :, lanes].reshape(2 * rows, HD)
        chosen = slot_ref[0]
        scores = pick_scores(queries, table_ref, chosen, lambda: pause(1))

        @pl.when(tick == H - 2)
        def _():
            place.arrived(asked.at[2], q_recv.at[2])
            ask(3, ALONG_CORE).start()

        pause(2)

        def put_lse(row):
            lse_ref[0] = row
            for k in range(2):
                lses[phase * 2 + k, pl.ds(head, 1), :] = row[:, k * rows : (k + 1) * rows]

        out = recall_values(scores, table_ref, chosen, put_lse, p_ref, lambda: pause(3))
        outs[pl.ds(phase * 2, 2), :, lanes] = out.reshape(2, rows, HD)

    @pl.when(tick == ticks)
    def _():
        for copy in give(1, ALONG_CORE):
            copy.start()
        late.finish(0)
        keep(1).start()
        for at in range(0, 2 * width, 256):
            kv_ref[:, pl.ds(at, 256)] = dot(normed_ref[...], rows_of(wkv, at, 256)).astype(BF)
        given(1)
        heads, total = combined((outs[2], landed[1]), (lses[2], landed_lses[1]))
        for h in range(H):
            outs[2, :, pl.ds(h * HD, HD)] = heads[h].astype(BF)
        lses[2] = total
        for copy in give(2, ALONG_X):
            copy.start()

    @pl.when(phase == 2)
    def _():
        for part in range(4):
            pause(part, 4 * ticks, 12 * H)
        fresh = pl.ds(pl.multiple_of(width + head * HD, HD), HD)
        segment_forward(
            len_ref[0],
            near_ref[0],
            q_ref[:, lanes],
            kc_ref[...],
            kv_ref[:, lanes],
            vc_ref[...],
            kv_ref[:, fresh],
            local_ref,
            plocal_ref,
        )

    @pl.when(tick == ticks + H - 1)
    def _():
        given(0)
        given(2)
        for k, (part, lse) in enumerate(
            ((outs[0], lses[0]), (landed[0], landed_lses[0]), (landed[2], landed_lses[2]))
        ):
            parts_ref[k] = part
            lses_ref[k] = lse
        for a in range(1, n):
            late.finish(a)
        for slot, to in ((1, ALONG_CORE), (2, ALONG_X), (3, ALONG_CORE)):
            ask(slot, to).wait_send()
        for slot, to in ((0, ALONG_CORE), (1, ALONG_CORE), (2, ALONG_X)):
            for copy in give(slot, to):
                copy.wait_send()
        for k in range(2):
            keep(k).wait()


def attend(length, near, x, table, chosen, cache, w_qkv, norms, late, orders, collective_id):
    n, n_hi = len(late) + 1, lax.axis_size("dp") // 2
    devices = n_hi * 8
    (rows, width), slots = x.shape, table.shape[1]
    own = w_qkv.shape[0]
    dma = pltpu.SemaphoreType.DMA
    shape = jax.ShapeDtypeStruct

    def gathered(a):
        return shape((devices,) + a.shape, a.dtype)

    def asked_head(p, h):
        return jnp.where(p < 2, h, H - 1)

    def segment_head(p, h):
        return jnp.where(p < 2, 0, h)

    def column(first=0):
        return pl.BlockSpec((rows, HD), lambda p, h: (0, first + segment_head(p, h)))

    return pl.pallas_call(
        functools.partial(attend_kernel, n_hi, orders),
        grid=(3, H),
        in_specs=[
            SCALARS,
            pl.BlockSpec((1, 1, 2 * NEAR), lambda p, h: (segment_head(p, h), 0, 0)),
            IN_VMEM,
            pl.BlockSpec((1, slots, 2 * HD), lambda p, h: (asked_head(p, h), 0, 0)),
            pl.BlockSpec((1, 8, 2 * rows), lambda p, h: (asked_head(p, h), 0, jnp.minimum(p, 1))),
            column(),
            column(H),
        ]
        + [ANYWHERE] * (1 + n),
        out_specs=[
            IN_VMEM,
            IN_VMEM,
            IN_VMEM,
            IN_VMEM,
            pl.BlockSpec((1, 1, 2 * rows), lambda p, h: (asked_head(p, h), 0, jnp.minimum(p, 1))),
            pl.BlockSpec(
                (1, slots, 2 * rows), lambda p, h: (jnp.minimum(p * H + h, 2 * H - 1), 0, 0)
            ),
            column(),
            pl.BlockSpec((1, 2 * W, W), lambda p, h: (segment_head(p, h), 0, 0)),
            IN_VMEM,
            IN_VMEM,
        ]
        + [ANYWHERE] * (1 + n),
        out_shape=[
            shape((rows, width), BF),
            shape((rows, width), BF),
            shape((rows, 2 * width), BF),
            shape((16, width), F32),
            shape((H, 1, 4 * rows), F32),
            shape((2 * H, slots, 2 * rows), BF),
            shape((rows, width), F32),
            shape((H, 2 * W, W), BF),
            shape((3, rows, width), BF),
            shape((3, H, rows), F32),
            shape((devices, own, width), BF),
            shape((devices, own, 2 * width), BF),
        ]
        + [gathered(a) for a in late],
        scratch_shapes=[
            pltpu.VMEM((devices, own, width), BF),
            pltpu.VMEM((devices, own, 2 * width), BF),
            pltpu.VMEM((devices,) + norms.shape, BF),
            pltpu.VMEM((4, rows, width), BF),
            pltpu.VMEM((4, rows, width), BF),
            pltpu.VMEM((3, rows, width), BF),
            pltpu.VMEM((4, H, rows), F32),
            pltpu.VMEM((3, H, rows), F32),
            dma((2,)),
            dma((4,)),
            dma((4,)),
            dma((3,)),
            dma((3,)),
            dma((3,)),
            dma((3,)),
        ]
        + gather_sems(2, n_hi)
        + gather_sems(n, n_hi),
        compiler_params=pltpu.CompilerParams(
            collective_id=collective_id, has_side_effects=True, vmem_limit_bytes=60 << 20
        ),
        cost_estimate=pl.CostEstimate(
            flops=16 * rows * slots * HD * H, bytes_accessed=128 << 20, transcendentals=0
        ),
    )(length, near, x, table, chosen, cache, cache, w_qkv, norms, *late)


def near_buckets():
    distance = np.arange(NEAR)
    exact = BUCKETS // 2
    far = exact + np.floor(
        np.log(np.maximum(distance, 1) / exact) / np.log(128.0 / exact) * exact
    )
    return np.where(distance < exact, distance, np.minimum(far, BUCKETS - 1)).astype(np.int32)


def near_hot():
    return near_buckets()[:, None] == np.arange(BUCKETS)[None, :]


def near_bias(rel_table):
    above = (rel_table - rel_table[-1:])[None]
    rows = jnp.sum(jnp.where(jnp.asarray(near_hot())[:, :, None], above, 0.0), axis=1)
    return jnp.pad(rows.T, ((0, 0), (0, NEAR)))[:, None, :]


def table_gradient(diagonals, totals):
    near = diagonals[:, 0, NEAR - 1 : 2 * NEAR - 1]
    sums = jnp.dot(near, jnp.asarray(near_hot(), F32), precision=HIGHEST)
    far = jnp.sum(totals, axis=(1, 2)) - jnp.sum(near, axis=1)
    return (sums + far[:, None] * (np.arange(BUCKETS) == BUCKETS - 1)).T


def segment_forward(length, near, q, cached_keys, keys, cached_values, values, out_ref, p_ref):
    band = pltpu.roll(
        jnp.broadcast_to(near, (NEAR, 2 * NEAR)), 0, 1, stride=1, stride_axis=0
    )
    key_ids = lax.broadcasted_iota(jnp.int32, (NEAR, NEAR), 0)
    query_ids = lax.broadcasted_iota(jnp.int32, (NEAR, NEAR), 1)
    on_diagonal = jnp.where(query_ids >= key_ids, band[:, :NEAR], NEGATIVE)
    beside = band[:, NEAR:]
    masked = jnp.full((NEAR, NEAR), NEGATIVE, F32)
    zero = jnp.zeros((NEAR, NEAR), F32)
    cache_t, values_t = cached_values.T, values.T
    step = 2 * NEAR
    for at in range(W // step):
        count = 2 * (at + 1)
        queries = q[step * at : step * (at + 1)]
        cached = dot(cached_keys, queries, NT) * SCALE
        if at == 0:
            last = cached[W - NEAR :] + jnp.concatenate([beside, zero], axis=1)
            cached = jnp.concatenate([cached[: W - NEAR], last], axis=0)
        fresh = dot(keys[: NEAR * count], queries, NT) * SCALE
        rows = [cached]
        for k in range(count):
            block = fresh[NEAR * k : NEAR * (k + 1)]
            tiles = [
                masked if q < k else on_diagonal if q == k else beside if q == k + 1 else zero
                for q in (2 * at, 2 * at + 1)
            ]
            if any(tile is not zero for tile in tiles):
                block = block + jnp.concatenate(tiles, axis=1)
            ids = lax.broadcasted_iota(jnp.int32, (NEAR, step), 0) + NEAR * k
            rows.append(jnp.where(ids < length, block, NEGATIVE))
        scores = jnp.concatenate(rows, axis=0)
        weights = jnp.exp(scores - jnp.max(scores, axis=0, keepdims=True))
        probs = (weights * (1.0 / jnp.sum(weights, axis=0, keepdims=True))).astype(BF)
        p_ref[0, pl.ds(0, W + NEAR * count), pl.ds(step * at, step)] = probs
        out = dot(cache_t, probs[:W]) + dot(values_t[:, : NEAR * count], probs[W:])
        out_ref[pl.ds(step * at, step), :] = out.T


def segment_grad(
    g_ref, q_ref, kc_ref, kn_ref, vc_ref, vn_ref, p_ref, put_q, gk_ref, gv_ref, diag_ref, tot_ref
):
    cache_t, keys_t = kc_ref[...].T, kn_ref[...].T
    on_diagonal = jnp.zeros((NEAR, NEAR), F32)
    beside = jnp.zeros((NEAR, NEAR), F32)
    step = 2 * NEAR
    total = jnp.zeros((8, step), F32)
    grad_keys, grad_values = [], []
    for at in range(W // step):
        count = 2 * (at + 1)
        grads = g_ref[pl.ds(step * at, step), :]
        queries = q_ref[pl.ds(step * at, step), :]
        grad_probs = jnp.concatenate(
            [dot(vc_ref[...], grads, NT), dot(vn_ref[pl.ds(0, NEAR * count), :], grads, NT)], axis=0
        )
        probs = p_ref[0, pl.ds(0, W + NEAR * count), pl.ds(step * at, step)]
        wide = probs.astype(F32)
        product = wide * grad_probs
        grad_scores = product - wide * jnp.sum(product, axis=0, keepdims=True)
        low = grad_scores.astype(BF)
        grad_q = dot(cache_t, low[:W]) + dot(keys_t[:, : NEAR * count], low[W:])
        put_q(step * at, (grad_q * SCALE).T)
        grad_keys.append(dot(low[W:], queries) * SCALE)
        grad_values.append(dot(probs[W:], grads))
        if at == 0:
            beside = beside + grad_scores[W - NEAR : W, :NEAR]
        for k in range(count):
            for side, q in enumerate((2 * at, 2 * at + 1)):
                tile = grad_scores[W + NEAR * k : W + NEAR * (k + 1), NEAR * side : NEAR * (side + 1)]
                if q == k:
                    on_diagonal = on_diagonal + tile
                elif q == k + 1:
                    beside = beside + tile
        total = total + jnp.sum(grad_scores.reshape(-1, 8, step), axis=0)
    for ref, (early, late) in ((gk_ref, grad_keys), (gv_ref, grad_values)):
        ref[...] = jnp.concatenate([late[:step] + early, late[step:]], axis=0).astype(BF)
    down = lax.broadcasted_iota(jnp.int32, (NEAR, NEAR), 0)
    across = lax.broadcasted_iota(jnp.int32, (NEAR, NEAR), 1)
    turned = lax.dot_general(
        (down + across == NEAR - 1).astype(F32),
        jnp.concatenate([on_diagonal, beside], axis=1),
        NN,
        precision=HIGHEST,
        preferred_element_type=F32,
    )
    diagonals = pltpu.roll(turned, 0, 1, stride=1, stride_axis=0)
    diag_ref[0] = jnp.sum(diagonals, axis=0, keepdims=True)
    tot_ref[0] = total


def recall_back(grads, table_ref, p_ref, delta, share):
    slots, step = table_ref.shape[1], 512
    keys_t = table_ref[0, :, pl.ds(0, HD)].T
    out = jnp.zeros((HD, grads.shape[0]), F32)
    for at in range(0, slots, step):
        along = dot(table_ref[0, pl.ds(at, step), pl.ds(HD, HD)], grads, NT)
        scores = (along - delta).astype(BF) * p_ref[0, pl.ds(at, step), :]
        out = out + dot(keys_t[:, at : at + step], scores)
    return (out * (share * SCALE)).T.astype(BF)


def attend_grad_kernel(n_hi, orders, *refs):
    n = len(orders)
    grec_ref, aux_ref, glocal_ref, q_ref, kc_ref, kn_ref, vc_ref, vn_ref, plocal_ref = refs[:9]
    table_ref, p_ref, lse_ref = refs[9:12]
    grads_in, rest = refs[12 : 12 + n], refs[12 + n :]
    gq_ref, gk_ref, gv_ref, diag_ref, tot_ref = rest[:5]
    sums_out, rest = rest[5 : 5 + n], rest[5 + n :]
    asked, aux, back, returned, glocal_q = rest[:5]
    ask_send, ask_recv, aux_send, aux_recv, back_send, back_recv = rest[5:11]
    buffers = [rest[11 + k * n : 11 + (k + 1) * n] for k in range(5)]
    place = Place(n_hi)
    scatter = Scatter(place, orders, grads_in, sums_out, buffers, rest[11 + 5 * n :])
    tick = pl.program_id(0)
    ticks = 3 * H
    order = near_first(n_hi)[::-1]

    def remote(src, dst, send, recv, to):
        return pltpu.make_async_remote_copy(
            src_ref=src,
            dst_ref=dst,
            send_sem=send,
            recv_sem=recv,
            device_id=place.device(to),
            device_id_type=MESH,
        )

    def ask(slot, to):
        first = slot < 3
        return [
            remote(
                grec_ref if first else asked.at[2],
                asked.at[slot],
                ask_send.at[slot],
                ask_recv.at[slot],
                to,
            ),
            remote(
                aux_ref if first else aux.at[2],
                aux.at[slot],
                aux_send.at[slot],
                aux_recv.at[slot],
                to,
            ),
        ]

    def asked_arrived(slot):
        place.arrived(asked.at[slot], ask_recv.at[slot])
        place.arrived(aux.at[slot], aux_recv.at[slot])

    def give(slot, to):
        return remote(
            back.at[(1, 3, 2)[slot]], returned.at[slot], back_send.at[slot], back_recv.at[slot], to
        )

    @pl.when(tick == 0)
    def _():
        place.greet()
        for slot, to in ((1, ALONG_CORE), (2, ALONG_X)):
            for copy in ask(slot, to):
                copy.start()
        for z in order:
            for a in range(n):
                scatter.begin(z, a)
        asked[0] = grec_ref[...]
        aux[0] = aux_ref[...]
        asked_arrived(1)

    events = []
    for k in range(n_hi + 2):
        for delay, event in enumerate((scatter.core, scatter.one, scatter.two)):
            if 0 <= k - delay < n_hi:
                events += [functools.partial(event, order[k - delay], a) for a in range(n)]
    for at in range(1, ticks):
        mine = events[len(events) * (at - 1) // (ticks - 1) : len(events) * at // (ticks - 1)]

        @pl.when(tick == at)
        def _(mine=mine):
            for event in mine:
                event()

    @pl.when(tick == H - 2)
    def _():
        asked_arrived(2)
        for copy in ask(3, ALONG_CORE):
            copy.start()

    @pl.when(tick == H)
    def _():
        asked_arrived(3)
        give(0, ALONG_CORE).start()

    @pl.when(tick < 2 * H)
    def _():
        phase = tick // H
        head = tick % H
        lanes = pl.ds(pl.multiple_of(head * HD, HD), HD)
        pair = pl.ds(phase * 2, 2)
        grads = asked[pair, :, lanes].reshape(-1, HD)
        delta = jnp.concatenate([aux[phase * 2 + k, pl.ds(head, 1), :] for k in range(2)], axis=1)
        total = jnp.concatenate(
            [aux[phase * 2 + k, pl.ds(H + head, 1), :] for k in range(2)], axis=1
        )
        share = jnp.exp(lse_ref[0] - total)
        result = recall_back(grads, table_ref, p_ref, delta, share)
        back[pair, :, lanes] = result.reshape(2, -1, HD)

    @pl.when(tick == 2 * H)
    def _():
        give(1, ALONG_CORE).start()

    @pl.when(tick == 2 * H + 1)
    def _():
        place.arrived(returned.at[1], back_recv.at[1])
        back[2] = (back[2].astype(F32) + returned[1].astype(F32)).astype(BF)
        give(2, ALONG_X).start()

    @pl.when(tick >= 2 * H)
    def _():
        lanes = pl.ds(pl.multiple_of((tick - 2 * H) * HD, HD), HD)

        def put_q(at, value):
            glocal_q[pl.ds(at, value.shape[0]), lanes] = value

        segment_grad(
            glocal_ref, q_ref, kc_ref, kn_ref, vc_ref, vn_ref, plocal_ref,
            put_q, gk_ref, gv_ref, diag_ref, tot_ref,
        )

    @pl.when(tick == ticks - 1)
    def _():
        for a in range(n):
            scatter.last(a)
        place.arrived(returned.at[0], back_recv.at[0])
        place.arrived(returned.at[2], back_recv.at[2])
        gq_ref[...] = (
            glocal_q[...]
            + back[0].astype(F32)
            + returned[0].astype(F32)
            + returned[2].astype(F32)
        ).astype(BF)
        scatter.finish()
        for slot, to in ((1, ALONG_CORE), (2, ALONG_X), (3, ALONG_CORE)):
            for copy in ask(slot, to):
                copy.wait_send()
        for slot, to in ((0, ALONG_CORE), (1, ALONG_CORE), (2, ALONG_X)):
            give(slot, to).wait_send()


def attend_grad(
    grad_recalled, aux, grad_local, queries, keys_values, cache, probs_local, table, probs, lses,
    grads, orders, collective_id,
):
    n, n_hi = len(grads), lax.axis_size("dp") // 2
    (rows, width), slots = queries.shape, table.shape[1]
    shapes = [g.shape[1:] for g in grads]
    dma = pltpu.SemaphoreType.DMA

    def column(first=0):
        return pl.BlockSpec((rows, HD), lambda t: (0, first + segment_head(t)))

    def head(*shape):
        return pl.BlockSpec((1,) + shape, lambda t: (segment_head(t),) + (0,) * len(shape))

    def segment_head(t):
        return jnp.maximum(t - 2 * H, 0)

    def asked(t):
        return jnp.minimum(t, 2 * H - 1)

    return pl.pallas_call(
        functools.partial(attend_grad_kernel, n_hi, orders),
        grid=(3 * H,),
        in_specs=[
            IN_VMEM,
            IN_VMEM,
            column(),
            column(),
            column(),
            column(),
            column(H),
            column(H),
            head(2 * W, W),
            pl.BlockSpec((1, slots, 2 * HD), lambda t: (asked(t) % H, 0, 0)),
            pl.BlockSpec((1, slots, 2 * rows), lambda t: (asked(t), 0, 0)),
            pl.BlockSpec((1, 1, 2 * rows), lambda t: (asked(t) % H, 0, asked(t) // H)),
        ]
        + [ANYWHERE] * n,
        out_specs=[IN_VMEM, column(), column(), head(1, 2 * NEAR), head(8, 2 * NEAR)]
        + [IN_VMEM] * n,
        out_shape=[
            jax.ShapeDtypeStruct((rows, width), BF),
            jax.ShapeDtypeStruct((rows, width), BF),
            jax.ShapeDtypeStruct((rows, width), BF),
            jax.ShapeDtypeStruct((H, 1, 2 * NEAR), F32),
            jax.ShapeDtypeStruct((H, 8, 2 * NEAR), F32),
        ]
        + [jax.ShapeDtypeStruct(shape, F32) for shape in shapes],
        scratch_shapes=[
            pltpu.VMEM((4, rows, width), BF),
            pltpu.VMEM((4,) + aux.shape, F32),
            pltpu.VMEM((4, rows, width), BF),
            pltpu.VMEM((3, rows, width), BF),
            pltpu.VMEM((rows, width), F32),
        ]
        + [dma((4,))] * 4
        + [dma((3,))] * 2
        + scatter_buffers(shapes, n_hi)
        + scatter_sems(n, n_hi),
        compiler_params=pltpu.CompilerParams(
            collective_id=collective_id, has_side_effects=True, vmem_limit_bytes=62 << 20
        ),
        cost_estimate=pl.CostEstimate(
            flops=16 * rows * slots * HD * H, bytes_accessed=128 << 20, transcendentals=0
        ),
    )(
        grad_recalled, aux, grad_local, queries, cache, keys_values, cache, keys_values,
        probs_local, table, probs, lses, *grads,
    )


def feed_kernel(
    parts_ref, lse_ref, local_ref, x_ref, cot_ref, gate_ref, norms_ref, wo_ref, up_ref, down_ref,
    out_ref, gatt_ref, gwo_ref, gup_ref, gdown_ref, glocal_ref, grec_ref, aux_ref, sums_ref,
    recalled, mixed_t, attended, scaled, inverse, normed, normed_t, acc, gacc,
):
    step, last = pl.program_id(0), pl.num_programs(0) - 1
    rows, width = x_ref.shape
    gate = gate_ref[...]

    @pl.when(step == 0)
    def _():
        heads, total = combined([parts_ref[k] for k in range(3)], [lse_ref[k] for k in range(3)])
        aux_ref[H:, :] = total
        for h in range(H):
            recalled[:, pl.ds(h * HD, HD)] = heads[h]
        mixed = (gate * recalled[...] + (1.0 - gate) * local_ref[...]).astype(BF)
        mixed_t[...] = mixed.T
        here = x_ref[...].astype(F32) + dot(mixed, wo_ref[...])
        attended[...] = here
        center = here - jnp.mean(here, axis=-1, keepdims=True)
        inv = lax.rsqrt(jnp.mean(center * center, axis=-1, keepdims=True) + EPSILON)
        inverse[...] = inv
        scaled[...] = center * inv
        n2 = (scaled[...] * norms_ref[1:2] + norms_ref[3:4]).astype(BF)
        normed[...] = n2
        normed_t[...] = n2.T
        acc[...] = jnp.zeros(acc.shape, F32)
        gacc[...] = jnp.zeros(gacc.shape, F32)

    up = dot(normed[...], up_ref[...])
    root = np.sqrt(2 / np.pi).astype(np.float32)
    square = up * up
    bend = jnp.tanh(root * (up + 0.044715 * (square * up)))
    hidden = (0.5 * up * (1.0 + bend)).astype(BF)
    slope = 0.5 * (1.0 + bend) + 0.5 * up * (1.0 - bend * bend) * (
        root * (1.0 + (3 * 0.044715) * square)
    )
    grad_up = (dot(cot_ref[...], down_ref[...], NT) * slope).astype(BF)
    acc[...] += dot(hidden, down_ref[...])
    gacc[...] += dot(grad_up, up_ref[...], NT)
    gdown_ref[...] = dot(hidden.T, cot_ref[...]).astype(BF)
    gup_ref[...] = dot(normed_t[...], grad_up).astype(BF)

    @pl.when(step == last)
    def _():
        out_ref[...] = (attended[...] + acc[...]).astype(BF)
        grad = gacc[...]
        sums_ref[0:1] = jnp.sum(grad * scaled[...], axis=0, keepdims=True)
        sums_ref[1:2] = jnp.sum(grad, axis=0, keepdims=True)
        grad = grad * norms_ref[1:2]
        mean_grad = jnp.mean(grad, axis=-1, keepdims=True)
        mean_cross = jnp.mean(grad * scaled[...], axis=-1, keepdims=True)
        grad = cot_ref[...].astype(F32) + inverse[...] * (
            grad - mean_grad - scaled[...] * mean_cross
        )
        gatt_ref[...] = grad
        low = grad.astype(BF)
        gwo_ref[...] = dot(mixed_t[...], low).astype(BF)
        gmixed = dot(low, wo_ref[...], NT)
        sums_ref[2:3] = jnp.sum(gmixed * (recalled[...] - local_ref[...]), axis=0, keepdims=True)
        sums_ref[3:] = jnp.zeros((5, width), F32)
        glocal_ref[...] = ((1.0 - gate) * gmixed).astype(BF)
        grec = (gate * gmixed).astype(BF)
        grec_ref[...] = grec
        product = grec.astype(F32) * recalled[...]
        delta = [
            jnp.sum(product[:, h * HD : (h + 1) * HD], axis=1, keepdims=True) for h in range(H)
        ]
        aux_ref[:H, :] = jnp.concatenate(delta, axis=1).T


def feed(parts, lses, local_out, x, cotangent, gate_row, norm_rows, w_out, w_up, w_down):
    rows, width = x.shape
    hidden = w_up.shape[1]
    block = 512
    full = jax.ShapeDtypeStruct
    return pl.pallas_call(
        feed_kernel,
        grid=(hidden // block,),
        in_specs=[IN_VMEM] * 8
        + [
            pl.BlockSpec((width, block), lambda k: (0, k)),
            pl.BlockSpec((block, width), lambda k: (k, 0)),
        ],
        out_specs=[IN_VMEM] * 3
        + [
            pl.BlockSpec((width, block), lambda k: (0, k)),
            pl.BlockSpec((block, width), lambda k: (k, 0)),
        ]
        + [IN_VMEM] * 4,
        out_shape=[
            full((rows, width), BF),
            full((rows, width), F32),
            full((width, width), BF),
            full((width, hidden), BF),
            full((hidden, width), BF),
            full((rows, width), BF),
            full((rows, width), BF),
            full((2 * H, rows), F32),
            full((8, width), F32),
        ],
        scratch_shapes=[
            pltpu.VMEM((rows, width), F32),
            pltpu.VMEM((width, rows), BF),
            pltpu.VMEM((rows, width), F32),
            pltpu.VMEM((rows, width), F32),
            pltpu.VMEM((rows, 1), F32),
            pltpu.VMEM((rows, width), BF),
            pltpu.VMEM((width, rows), BF),
            pltpu.VMEM((rows, width), F32),
            pltpu.VMEM((rows, width), F32),
        ],
        compiler_params=pltpu.CompilerParams(vmem_limit_bytes=56 << 20),
        cost_estimate=pl.CostEstimate(
            flops=12 * rows * width * hidden, bytes_accessed=36 << 20, transcendentals=0
        ),
    )(parts, lses, local_out, x, cotangent, gate_row, norm_rows, w_out, w_up, w_down)


def close_kernel(n_hi, orders, *refs):
    n = len(orders)
    normed_ref, gq_ref, gk_ref, gv_ref, x_ref, gatt_ref, norms_ref, sums_ref, rest_ref = refs[:9]
    q_hbm, kv_hbm, share_ref, tokens_ref, small_ref = refs[9:14]
    wq, wkv, small_in, small_buffer, load_sem = refs[14:19]
    grads = refs[19 : 19 + n]
    rest = refs[19 + n :]
    buffers = [rest[k * n : (k + 1) * n] for k in range(5)]
    place = Place(n_hi)
    devices, rows, columns = grads[0].shape
    outs = [share_ref.at[:, pl.ds(a * columns, columns)] for a in range(n)]
    scatter = Scatter(
        place, orders, grads, outs, buffers, rest[5 * n :], (small_in, small_ref, small_buffer)
    )
    place.greet()
    loads = [
        pltpu.make_async_copy(src, dst, load_sem.at[k])
        for k, (src, dst) in enumerate(((q_hbm, wq), (kv_hbm, wkv)))
    ]
    for load in loads:
        load.start()
    sources = (gq_ref, gk_ref, gv_ref)
    width = x_ref.shape[1]
    step = 256
    order = near_first(n_hi)[::-1]
    normed_t = normed_ref[...].T
    for a in range(n):
        for at in range(0, columns, step):
            source, first = divmod(a * columns + at, width)
            grad = dot(normed_t, sources[source][:, pl.ds(first, step)])
            grads[a][:, :, pl.ds(at, step)] = grad.reshape(devices, rows, step).astype(BF)
        for z in order:
            scatter.begin(z, a)
    tokens = x_ref.shape[0]
    piece = tokens // 4
    sums = [0.0, 0.0]

    def norm_piece(k):
        at = pl.ds(k * piece, piece)
        x = x_ref[at, :].astype(F32)
        center = x - jnp.mean(x, axis=-1, keepdims=True)
        inverse = lax.rsqrt(jnp.mean(center * center, axis=-1, keepdims=True) + EPSILON)
        scaled = center * inverse
        grad = (
            dot(gq_ref[at, :], wq[...], NT)
            + dot(gk_ref[at, :], wkv[:, pl.ds(0, width)], NT)
            + dot(gv_ref[at, :], wkv[:, pl.ds(width, width)], NT)
        )
        sums[0] = sums[0] + jnp.sum(grad * scaled, axis=0, keepdims=True)
        sums[1] = sums[1] + jnp.sum(grad, axis=0, keepdims=True)
        grad = grad * norms_ref[0:1]
        mean_grad = jnp.mean(grad, axis=-1, keepdims=True)
        mean_cross = jnp.mean(grad * scaled, axis=-1, keepdims=True)
        tokens_ref[at, :] = gatt_ref[at, :] + inverse * (grad - mean_grad - scaled * mean_cross)

    def small_go():
        lanes = width // 8
        for k, row in enumerate((sums[0], sums_ref[0:1], sums[1], sums_ref[1:2])):
            for g in range(8):
                small_in[8 * k + g : 8 * k + g + 1] = row[:, g * lanes : (g + 1) * lanes]
        small_in[32:] = rest_ref[...]
        scatter.small_begin()

    for z in order:
        for a in range(n):
            scatter.core(z, a)
    for load in loads:
        load.wait()
    for k in range(4):
        norm_piece(k)
        if k == 1:
            for a in range(n):
                scatter.one(order[0], a)
    small_go()
    rounds = len(scatter.small_steps())
    for k in range(max(n_hi + 1, rounds)):
        for a in range(n):
            if 0 < k < n_hi:
                scatter.one(order[k], a)
        for a in range(n):
            if 0 <= k - 1 < n_hi:
                scatter.two(order[k - 1], a)
        if k < rounds:
            scatter.small_next(k)
    for a in range(n):
        scatter.last(a)
    scatter.finish()


def close(
    normed, grads, x, grad_attended, norm_rows, sums, rest, full_q, full_kv, rows, orders, collective_id
):
    n, n_hi = len(orders), lax.axis_size("dp") // 2
    width = x.shape[1]
    columns = 3 * width // n
    rounds = 3 + (n_hi - 1).bit_length()
    dma = pltpu.SemaphoreType.DMA
    small = (40, width // 8)
    return pl.pallas_call(
        functools.partial(close_kernel, n_hi, orders),
        out_shape=[
            jax.ShapeDtypeStruct((rows, 3 * width), F32),
            jax.ShapeDtypeStruct(x.shape, F32),
            jax.ShapeDtypeStruct(small, F32),
        ],
        in_specs=[IN_VMEM] * 9 + [ANYWHERE] * 2,
        out_specs=[IN_VMEM] * 3,
        scratch_shapes=[
            pltpu.VMEM(full_q.shape, BF),
            pltpu.VMEM(full_kv.shape, BF),
            pltpu.VMEM(small, F32),
            pltpu.VMEM((2, rounds) + small, F32),
            dma((2,)),
        ]
        + [pltpu.VMEM((n_hi * 8, rows, columns), BF)] * n
        + scatter_buffers([(rows, columns)] * n, n_hi)
        + scatter_sems(n, n_hi)
        + [dma((rounds,)), dma((rounds,))],
        compiler_params=pltpu.CompilerParams(
            collective_id=collective_id, has_side_effects=True, vmem_limit_bytes=56 << 20
        ),
    )(normed, *grads, x, grad_attended, norm_rows, sums, rest, full_q, full_kv)


def local(
    tokens,
    norm_gains,
    norm_shifts,
    w_qkv,
    w_out,
    w_up,
    w_down,
    rel_table,
    gate_bias,
    xl_cache,
    memory,
    slot_index,
    seg_len,
    cotangent,
):
    width = tokens.shape[1]
    count = tokens.shape[0]
    slot_count = memory.shape[0]
    groups = lax.axis_size("mem")
    me = lax.axis_index("mem")

    devices = lax.axis_size("dp") * groups
    number = lax.axis_index("dp") * groups + me
    own = norm_gains.shape[1]
    per = 128 // own
    norms = jnp.tile(
        jnp.pad(jnp.concatenate([norm_gains, norm_shifts], axis=0), ((0, 12), (0, 0))), (1, per)
    )
    here = lax.broadcasted_iota(jnp.int32, norms.shape, 1) // own == number % per
    norms = jnp.where(here, norms, jnp.zeros_like(norms))
    table = memory.transpose(1, 0, 2)
    slot_rows = (slot_index - me * slot_count).reshape(groups, count, H, -1)
    picks = [
        lax.dynamic_index_in_dim(slot_rows, me ^ turn, 0, keepdims=False) for turn in range(groups)
    ]
    chosen = jnp.stack(picks).transpose(2, 3, 0, 1).reshape(H, -1, groups * count)
    (
        normed_one,
        queries,
        keys_values,
        norm_rows,
        lse_all,
        probs_all,
        local_out,
        probs_local,
        parts,
        lses,
        *full,
    ) = attend(
        seg_len,
        near_bias(rel_table),
        tokens,
        table,
        chosen,
        xl_cache,
        w_qkv,
        norms,
        (w_out, w_up, w_down),
        ("zyx", "zxy", "xyz", "xyz", "zyx", "zxy"),
        0,
    )
    full_q, full_kv, full_out, full_up, full_down = [f.reshape(-1, f.shape[2]) for f in full]
    gate_open = jax.nn.sigmoid(gate_bias)
    output, grad_attended, grad_wout, grad_up, grad_down, grad_local, grad_recalled, aux, sums = feed(
        parts,
        lses,
        local_out,
        tokens,
        cotangent,
        jnp.repeat(gate_open, HD)[None],
        norm_rows,
        full_out,
        full_up,
        full_down,
    )
    grad_gate = jnp.sum(sums[2].reshape(H, HD), axis=1) * gate_open * (1.0 - gate_open)
    grad_query, grad_keys, grad_values, diagonals, totals, share_out, share_up, share_down = attend_grad(
        grad_recalled,
        aux,
        grad_local,
        queries,
        keys_values,
        xl_cache,
        probs_local,
        table,
        probs_all,
        lse_all,
        [g.reshape(devices, -1, g.shape[1]) for g in (grad_wout, grad_up, grad_down)],
        ("xyz", "yxz", "yxz"),
        1,
    )
    grad_table = table_gradient(diagonals, totals)
    rest = jnp.pad(jnp.concatenate([grad_table.reshape(-1), grad_gate]), (0, 1024 - 264))
    share_qkv, grad_tokens, small = close(
        normed_one,
        (grad_query, grad_keys, grad_values),
        tokens,
        grad_attended,
        norm_rows,
        sums,
        rest.reshape(8, -1),
        full_q,
        full_kv,
        w_qkv.shape[0],
        ("yxz", "xyz"),
        2,
    )
    share_norms = lax.dynamic_slice_in_dim(
        small[:32].reshape(4, width), number * own, own, axis=1
    )
    rest = small[32:].reshape(-1)
    table_total, gate_total = rest[: BUCKETS * H].reshape(BUCKETS, H), rest[BUCKETS * H :][:H]
    return (
        output,
        grad_tokens,
        share_norms[:2],
        share_norms[2:],
        share_qkv,
        share_out,
        share_up,
        share_down,
        table_total,
        gate_total,
    )


def solution(mesh):
    shard = P(AXES, None)
    placed = (
        shard,
        P(None, AXES),
        P(None, AXES),
        shard,
        shard,
        shard,
        shard,
        P(),
        P(),
        shard,
        P(AXES, None, None),
        P("dp", None, "mem"),
        P(AXES),
        shard,
    )
    return jax.shard_map(
        local,
        mesh=mesh,
        in_specs=placed,
        out_specs=(
            shard,
            shard,
            P(None, AXES),
            P(None, AXES),
            shard,
            shard,
            shard,
            shard,
            P(),
            P(),
        ),
        check_vma=False,
    )
```
